32 devices in a mesh: grp: 2 (over y), bl: 4 (over z), ch: 4 (over x, core).
Axes of the slice: x: 2, y: 2, z: 4, core: 2. Of those that a mesh axis runs over, the one named last changes fastest.
Arguments:
- visibilities: bfloat16 [8, 128, 4096], P(None, 'ch', ('grp', 'bl')), parts along dimension 2, may hold values from -40 to 40
- sky_model: bfloat16 [8, 128, 4096], P(None, 'ch', ('grp', 'bl')), parts along dimension 2, may hold values from -4 to 4
- antenna_pairs: int32 [2, 4096], P(None, ('grp', 'bl')), parts along dimension 1, may hold values from 0 to 511, as said below
- tile_counts: int32 [8], P(('grp', 'bl')), parts along dimension 0, may hold values from 128 to 512, as said below
- usable_mask: int32 [128, 4096], P('ch', ('grp', 'bl')), parts along dimension 1, may hold values 0 or 1
Outputs:
- solved_gains: float32 [2, 2, 128, 1024], P(None, None, 'ch', ('grp', 'bl')), parts along dimension 3
- fitted_gains: float32 [2, 2, 128, 1024], P(None, None, 'ch', ('grp', 'bl')), parts along dimension 3
The draws below stay inside these ranges and needn't reach their ends.
There are 2 independent parts, one for each index of `grp`. The reference program is written for one: setup_inputs(seed, part) draws one part's arguments, and reference() takes and returns one part's arrays. A program takes and returns all parts, laid end to end along the dimension named above; each array names one. Nothing has to cross between parts.
Inputs may be any that keep to these rules, and one draw needn't show every extreme that they name: `antenna_pairs`: the two stations of every slot differ. Tile t's baselines are its first tile_counts[t] slots; the later slots of a tile are not used. Some tile is full in every draw.
All inputs are finite; a program needn't handle non-finite values. No bound on the sum of `usable_mask` on one device may be relied on, other than what follows from the above.
Results may differ from the reference program's by a relative error of at most 0.0003.
Values may be sent and summed in bfloat16 or wider, within the bound.
A program may use at most 64 MiB of HBM per device.

```python
import jax
import jax.numpy as jnp
from jax import lax

STATION_COUNT = 512
BL_DEV = 512
SWEEPS = 2
PASSES = 1
FREQ_CHANNELS = 128
BASELINE_SLOTS = 2048
TILES = 4


def complex_product(left_real, left_imag, right_real, right_imag):
    return (left_real * right_real - left_imag * right_imag, left_real * right_imag + left_imag * right_real)


def station_pairs(key):
    first_endpoints = jax.random.randint(jax.random.fold_in(key, 11), (BASELINE_SLOTS,), 0, STATION_COUNT)
    slot_offsets = jax.random.randint(jax.random.fold_in(key, 12), (BASELINE_SLOTS,), 1, STATION_COUNT)
    second_ends = (first_endpoints + slot_offsets) % STATION_COUNT
    return jnp.stack([first_endpoints, second_ends]).astype(jnp.int32)


def sky_parts(key):
    pair_table = station_pairs(key)
    handedness_scale = jnp.array([1.0, 0.3, 0.3, 1.0], jnp.float32)[:, None, None]
    model_real_part = 0.7 * jnp.clip(jax.random.normal(jax.random.fold_in(key, 21), (4, FREQ_CHANNELS, BASELINE_SLOTS), jnp.float32), -5.0, 5.0) * handedness_scale
    model_imaginary = 0.7 * jnp.clip(jax.random.normal(jax.random.fold_in(key, 22), (4, FREQ_CHANNELS, BASELINE_SLOTS), jnp.float32), -5.0, 5.0) * handedness_scale
    station_amp = jnp.exp(jax.random.uniform(jax.random.fold_in(key, 31), (2, 1, STATION_COUNT), jnp.float32, jnp.log(0.7), jnp.log(1.4)))
    rough = jnp.clip(jax.random.normal(jax.random.fold_in(key, 32), (2, FREQ_CHANNELS, STATION_COUNT), jnp.float32), -3.0, 3.0)
    amplitude = station_amp * (1.0 + 0.1 * rough)
    node_values = jnp.linspace(-1.0, 1.0, FREQ_CHANNELS, dtype=jnp.float32)[None, :, None]
    phase_angle = jax.random.uniform(jax.random.fold_in(key, 33), (2, 1, STATION_COUNT), jnp.float32, -jnp.pi, jnp.pi) + jax.random.uniform(jax.random.fold_in(key, 34), (2, 1, STATION_COUNT), jnp.float32, -2.0, 2.0) * node_values + 0.3 * jax.random.normal(jax.random.fold_in(key, 35), (2, FREQ_CHANNELS, STATION_COUNT), jnp.float32)
    gain_real = amplitude * jnp.cos(phase_angle)
    gain_imag = amplitude * jnp.sin(phase_angle)
    first_real = gain_real[:, :, pair_table[0]][:, None]
    first_imag = gain_imag[:, :, pair_table[0]][:, None]
    second_real = gain_real[:, :, pair_table[1]][None]
    second_imag = gain_imag[:, :, pair_table[1]][None]
    block_real_part = model_real_part.reshape(2, 2, FREQ_CHANNELS, BASELINE_SLOTS)
    block_imaginary = model_imaginary.reshape(2, 2, FREQ_CHANNELS, BASELINE_SLOTS)
    inner_real, inner_imag = complex_product(first_real, first_imag, block_real_part, block_imaginary)
    outer_real_part, outer_imaginary = complex_product(inner_real, inner_imag, second_real, -second_imag)
    noise_real_part = 0.3 * jnp.clip(jax.random.normal(jax.random.fold_in(key, 41), (4, FREQ_CHANNELS, BASELINE_SLOTS), jnp.float32), -4.0, 4.0)
    noise_imaginary = 0.3 * jnp.clip(jax.random.normal(jax.random.fold_in(key, 42), (4, FREQ_CHANNELS, BASELINE_SLOTS), jnp.float32), -4.0, 4.0)
    visibility_planes = jnp.concatenate([outer_real_part.reshape(4, FREQ_CHANNELS, BASELINE_SLOTS) + noise_real_part, outer_imaginary.reshape(4, FREQ_CHANNELS, BASELINE_SLOTS) + noise_imaginary])
    model_planes = jnp.concatenate([model_real_part, model_imaginary])
    return (visibility_planes, model_planes)


def draw_visibilities(key, part):
    return sky_parts(key)[0].astype(jnp.bfloat16)


def draw_sky_model(key, part):
    return sky_parts(key)[1].astype(jnp.bfloat16)


def draw_antenna_pairs(key, part):
    return station_pairs(key)


def draw_tile_counts(key, part):
    counts_drawn = jax.random.randint(jax.random.fold_in(key, 51), (TILES,), BL_DEV // 4, BL_DEV + 1)
    full_tile = jax.random.randint(jax.random.fold_in(key, 52), (), 0, TILES)
    return counts_drawn.at[full_tile].set(BL_DEV).astype(jnp.int32)


def set_ends(result, stream_key, low, top_value):
    longest = result.shape.index(max(result.shape))
    spots = []
    for shift in (0, 1):
        where = [jax.random.randint(jax.random.fold_in(stream_key, axis), (), 0, length) for axis, length in enumerate(result.shape)]
        where[longest] = (where[longest] + shift) % result.shape[longest]
        spots.append(tuple(where))
    return result.at[spots[0]].set(low).at[spots[1]].set(top_value)


def setup_inputs(seed: int = 0, part: int = 0) -> dict:
    splits = jax.random.split(jax.random.key(seed), 6)
    part_keys = jax.random.split(jax.random.fold_in(splits[5], part), 6)
    visibilities = draw_visibilities(jax.random.fold_in(jax.random.fold_in(splits[5], part), 71), part)
    sky_model = draw_sky_model(jax.random.fold_in(jax.random.fold_in(splits[5], part), 71), part)
    antenna_pairs = draw_antenna_pairs(jax.random.fold_in(jax.random.fold_in(splits[5], part), 71), part)
    tile_counts = draw_tile_counts(jax.random.fold_in(jax.random.fold_in(splits[5], part), 71), part)
    usable_mask = set_ends((jax.random.randint(part_keys[4], (FREQ_CHANNELS, BASELINE_SLOTS), 0, 10) < 9).astype(jnp.int32), jax.random.fold_in(part_keys[4], 1), 0, 1)
    return {"visibilities": visibilities, "sky_model": sky_model, "antenna_pairs": antenna_pairs, "tile_counts": tile_counts, "usable_mask": usable_mask}


damping = 4.0
highest = lax.Precision.HIGHEST

def split_parts(data):
    planes = data.astype(jnp.float32)
    shape_rest = planes.shape[1:]
    return (planes[:4].reshape((2, 2) + shape_rest), planes[4:].reshape((2, 2) + shape_rest))

def poly_basis(channel_total):
    node_values = (2.0 * jnp.arange(channel_total, dtype=jnp.float32) - (channel_total - 1)) / (channel_total - 1)
    basis_rows = []
    for degree in range(4):
        vector = node_values ** degree
        for earlier in basis_rows:
            vector = vector - jnp.sum(vector * earlier) * earlier
        vector = vector / jnp.sqrt(jnp.sum(vector * vector))
        basis_rows.append(vector)
    return jnp.stack(basis_rows)

def contributions(model_real_part, model_imaginary, vis_real, vis_imag, first_gain, second_gain, weights):
    second_real = second_gain[0][None]
    second_imag = second_gain[1][None]
    left_real = model_real_part * second_real + model_imaginary * second_imag
    left_imag = model_imaginary * second_real - model_real_part * second_imag
    first_num_real = lax.optimization_barrier(jnp.sum(left_real * vis_real + left_imag * vis_imag, axis=1)) * weights
    first_num_imag = lax.optimization_barrier(jnp.sum(left_real * vis_imag - left_imag * vis_real, axis=1)) * weights
    first_den = lax.optimization_barrier(jnp.sum(left_real * left_real + left_imag * left_imag, axis=1)) * weights
    first_real = first_gain[0][:, None]
    first_imag = first_gain[1][:, None]
    right_real = model_real_part * first_real - model_imaginary * first_imag
    right_imag = model_real_part * first_imag + model_imaginary * first_real
    second_num_real = lax.optimization_barrier(jnp.sum(right_real * vis_real + right_imag * vis_imag, axis=0)) * weights
    second_num_imag = lax.optimization_barrier(jnp.sum(right_imag * vis_real - right_real * vis_imag, axis=0)) * weights
    second_den = lax.optimization_barrier(jnp.sum(right_real * right_real + right_imag * right_imag, axis=0)) * weights
    return (jnp.stack([first_num_real, first_num_imag, first_den]), jnp.stack([second_num_real, second_num_imag, second_den]))

def collect(terms, station_ends):
    channel_local = terms.shape[2]
    flat_terms = terms.reshape(-1, terms.shape[3]).T
    summed = jax.ops.segment_sum(flat_terms, station_ends, num_segments=STATION_COUNT)
    return summed.T.reshape(3, 2, channel_local, STATION_COUNT)

def refresh(station_sums, previous):
    divisor = station_sums[2] + damping
    return jnp.stack([(station_sums[0] + damping * previous[0]) / divisor, (station_sums[1] + damping * previous[1]) / divisor])

def reference(visibilities, sky_model, antenna_pairs, tile_counts, usable_mask):
    first_endpoints = antenna_pairs[0]
    second_ends = antenna_pairs[1]
    station_positions = jnp.arange(BASELINE_SLOTS, dtype=jnp.int32)
    live_slots = station_positions % BL_DEV < tile_counts[station_positions // BL_DEV]
    weights = usable_mask.astype(jnp.float32) * live_slots.astype(jnp.float32)[None, :]
    block_width = 8
    block_total = FREQ_CHANNELS // block_width
    vis_blocks = visibilities.reshape(8, block_total, block_width, BASELINE_SLOTS).transpose(1, 0, 2, 3)
    model_blocks = sky_model.reshape(8, block_total, block_width, BASELINE_SLOTS).transpose(1, 0, 2, 3)
    weight_blocks = weights.reshape(block_total, block_width, BASELINE_SLOTS)

    def block_sums(items):
        vis_block, model_block, weight_block, gain_block = items
        vis_real, vis_imag = split_parts(vis_block)
        model_real_part, model_imaginary = split_parts(model_block)
        first_gain = gain_block[:, :, :, first_endpoints]
        second_gain = gain_block[:, :, :, second_ends]
        end_first, end_second = contributions(model_real_part, model_imaginary, vis_real, vis_imag, first_gain, second_gain, weight_block)
        return collect(end_first, first_endpoints) + collect(end_second, second_ends)
    gain_state = jnp.stack([jnp.ones((2, FREQ_CHANNELS, STATION_COUNT), jnp.float32), jnp.zeros((2, FREQ_CHANNELS, STATION_COUNT), jnp.float32)])
    poly_rows = poly_basis(FREQ_CHANNELS)
    solved = gain_state
    for pass_index in range(PASSES):
        for iteration in range(SWEEPS):
            gain_blocks = gain_state.reshape(2, 2, block_total, block_width, STATION_COUNT).transpose(2, 0, 1, 3, 4)
            summed_blocks = lax.map(block_sums, (vis_blocks, model_blocks, weight_blocks, gain_blocks))
            station_sums = summed_blocks.transpose(1, 2, 0, 3, 4).reshape(3, 2, FREQ_CHANNELS, STATION_COUNT)
            renewed = refresh(station_sums, gain_state)
            if iteration == 1:
                renewed = 0.5 * (renewed + gain_state)
            gain_state = renewed
        solved = gain_state
        moments = jnp.einsum('kc,rfca->krfa', poly_rows, solved, precision=highest)
        gain_state = jnp.einsum('kc,krfa->rfca', poly_rows, moments, precision=highest)
    return (solved, gain_state)
```

```python
import functools
import math

import jax
import jax.numpy as jnp
import numpy as np
from jax import lax
from jax.experimental import pallas as pl
from jax.experimental.pallas import tpu as pltpu
from jax.sharding import PartitionSpec as P

STATION_COUNT = 512
SWEEPS = 2


damping = 4.0
highest = lax.Precision.HIGHEST
MESH = pl.DeviceIdType.MESH
LANES = 128
SUBLANES = 8


def basis_coefficients(channel_total):
    x = (2.0 * np.arange(channel_total, dtype=np.float64) - (channel_total - 1)) / (channel_total - 1)
    m = np.mean(x**2)
    r = np.sum(x**4) / np.sum(x**2)
    a = [1.0 / np.sqrt(np.sum(v * v)) for v in (np.ones_like(x), x, x**2 - m, x**3 - r * x)]
    return [float(v) for v in a], float(m), float(r)


def split_hi_lo(values):
    hi = values.astype(jnp.bfloat16)
    lo = (values - hi.astype(jnp.float32)).astype(jnp.bfloat16)
    return jnp.concatenate([hi, lo], axis=0)


def exchange_partner(me, k):
    partner, bit = 0, 1
    while bit <= k:
        digit = (me // bit) % 2
        partner = partner + (1 - digit if k & bit else digit) * bit
        bit *= 2
    return partner + (me // bit) * bit


def calibrate(
    n_bl, n_ch, vis_ref, model_ref, pairs_ref, counts_ref, mask_ref, sol_out, fit_out,
    outgoing, incoming, pairs_all, onehot, products, state, sol, moments, moments_in,
    data_send, data_recv, pair_send, pair_recv, sol_send, sol_recv, mom_send, mom_recv,
):
    me_bl = lax.axis_index("bl")
    me_ch = lax.axis_index("ch")
    channels, slots = mask_ref.shape
    own = channels // n_bl
    stations = state.shape[2]
    owned = stations // n_bl
    f32 = jnp.float32

    barrier = pltpu.get_barrier_semaphore()
    for k in range(1, n_bl):
        pl.semaphore_signal(barrier, inc=1, device_id={"bl": exchange_partner(me_bl, k)}, device_id_type=MESH)
    for k in range(1, n_ch):
        pl.semaphore_signal(barrier, inc=1, device_id={"ch": lax.rem(me_ch + k, n_ch)}, device_id_type=MESH)

    live = lax.broadcasted_iota(jnp.int32, (channels, slots), 1) < counts_ref[0]
    weights = jnp.where(live, mask_ref[...], 0).astype(f32)
    for plane in range(0, 16, 2):
        pair = []
        for j in (plane, plane + 1):
            if j < 8:
                pair.append(vis_ref[j].astype(f32))
            else:
                pair.append(model_ref[j - 8].astype(f32) * weights)
        for z in range(n_bl):
            rows = slice(z * own, (z + 1) * own)
            both = jnp.concatenate([pair[0][rows], pair[1][rows]], axis=0)
            outgoing[z, plane * own : (plane + 2) * own, :] = both.astype(jnp.bfloat16)

    pl.semaphore_wait(barrier, n_bl + n_ch - 2)

    pair_copies, data_copies = {}, {}
    for k in range(1, n_bl):
        pair_copies[k] = pltpu.make_async_remote_copy(
            src_ref=pairs_ref, dst_ref=pairs_all.at[k], send_sem=pair_send.at[k], recv_sem=pair_recv.at[k],
            device_id={"bl": exchange_partner(me_bl, k)}, device_id_type=MESH,
        )
        pair_copies[k].start()
    for k in range(n_bl - 1, 0, -1):
        partner = exchange_partner(me_bl, k)
        data_copies[k] = pltpu.make_async_remote_copy(
            src_ref=outgoing.at[partner], dst_ref=incoming.at[k], send_sem=data_send.at[k],
            recv_sem=data_recv.at[k], device_id={"bl": partner}, device_id_type=MESH,
        )
        data_copies[k].start()

    def build_onehot(k):
        ends = pairs_ref[...] if k == 0 else pairs_all[k]
        step = 64

        def rows(i, carry):
            base = pl.multiple_of(i * step, step)
            station = lax.broadcasted_iota(jnp.int32, (step, slots), 0) + base
            for e in range(2):
                hit = jnp.where(station == ends[e : e + 1, :], 1.0, 0.0).astype(jnp.bfloat16)
                onehot[k, pl.ds(base, step), e * slots : (e + 1) * slots] = hit
            return carry

        lax.fori_loop(0, stations // step, rows, 0)

    def scatter(k, first, second):
        terms = jnp.concatenate(
            [jnp.concatenate(first, axis=0), jnp.concatenate(second, axis=0)], axis=1
        )
        summed = lax.dot_general(
            split_hi_lo(terms), onehot[k], (((1,), (1,)), ((), ())), preferred_element_type=f32
        )
        half = terms.shape[0]
        return summed[:half] + summed[half:]

    def make_products(k, block):
        planes = block.astype(f32).reshape(16, own, slots)
        a_re, a_im, b = [], [], []
        for j in range(4):
            vr, vi, mr, mi = planes[j], planes[4 + j], planes[8 + j], planes[12 + j]
            a_re.append(mr * vr + mi * vi)
            a_im.append(mr * vi - mi * vr)
            b.append(mr * mr + mi * mi)
        for j in range(4):
            products[k, j] = a_re[j]
            products[k, 4 + j] = a_im[j]
            products[k, 8 + j] = b[j]
        first = [a_re[0] + a_re[1], a_re[2] + a_re[3], a_im[0] + a_im[1], a_im[2] + a_im[3], b[0] + b[1], b[2] + b[3]]
        second = [
            a_re[0] + a_re[2], a_re[1] + a_re[3], -(a_im[0] + a_im[2]), -(a_im[1] + a_im[3]), b[0] + b[2], b[1] + b[3],
        ]
        return scatter(k, first, second)

    build_onehot(0)
    total = make_products(0, outgoing[me_bl])
    for k in range(1, n_bl):
        pair_copies[k].wait()
        build_onehot(k)
    for k in range(1, n_bl):
        data_copies[k].wait_recv()
        total = total + make_products(k, incoming[k])

    feeds = 2 * own
    divisor = total[2 * feeds :] + damping
    gain_re = (total[:feeds] + damping) / divisor
    gain_im = total[feeds : 2 * feeds] / divisor
    gains = jnp.concatenate([gain_re, gain_im], axis=0)

    split_gains = split_hi_lo(gains)
    total = None
    for k in range(n_bl):
        both = jnp.dot(split_gains, onehot[k], preferred_element_type=f32)
        both = both[: 2 * feeds] + both[2 * feeds :]
        at = [[both[i * own : (i + 1) * own, e * slots : (e + 1) * slots] for i in range(4)] for e in range(2)]
        ga, ge = at
        ga_sq = [ga[p] * ga[p] + ga[2 + p] * ga[2 + p] for p in range(2)]
        ge_sq = [ge[p] * ge[p] + ge[2 + p] * ge[2 + p] for p in range(2)]
        a_re = [products[k, j] for j in range(4)]
        a_im = [products[k, 4 + j] for j in range(4)]
        b = [products[k, 8 + j] for j in range(4)]
        first, second = [[], [], []], [[], [], []]
        for p in range(2):
            j0, j1 = 2 * p, 2 * p + 1
            first[0].append(a_re[j0] * ge[0] - a_im[j0] * ge[2] + a_re[j1] * ge[1] - a_im[j1] * ge[3])
            first[1].append(a_re[j0] * ge[2] + a_im[j0] * ge[0] + a_re[j1] * ge[3] + a_im[j1] * ge[1])
            first[2].append(b[j0] * ge_sq[0] + b[j1] * ge_sq[1])
        for q in range(2):
            j0, j1 = q, 2 + q
            second[0].append(a_re[j0] * ga[0] + a_im[j0] * ga[2] + a_re[j1] * ga[1] + a_im[j1] * ga[3])
            second[1].append(a_re[j0] * ga[2] - a_im[j0] * ga[0] + a_re[j1] * ga[3] - a_im[j1] * ga[1])
            second[2].append(b[j0] * ga_sq[0] + b[j1] * ga_sq[1])
        part = scatter(k, sum(first, []), sum(second, []))
        total = part if total is None else total + part

    divisor = total[2 * feeds :] + damping
    for i in range(2):
        previous = gains[i * feeds : (i + 1) * feeds]
        renewed = (total[i * feeds : (i + 1) * feeds] + damping * previous) / divisor
        state[2 * i : 2 * i + 2] = (0.5 * (renewed + previous)).reshape(2, own, stations)

    my_rows = pl.ds(pl.multiple_of(me_bl * own, SUBLANES), own)
    sol_copies = []
    for k in range(n_bl - 1, 0, -1):
        partner = exchange_partner(me_bl, k)
        sol_copies.append(
            pltpu.make_async_remote_copy(
                src_ref=state.at[:, :, pl.ds(pl.multiple_of(partner * owned, LANES), owned)],
                dst_ref=sol.at[:, my_rows, :], send_sem=sol_send.at[k], recv_sem=sol_recv.at[k],
                device_id={"bl": partner}, device_id_type=MESH,
            )
        )
        sol_copies[-1].start()
    sol[:, my_rows, :] = state[:, :, pl.ds(pl.multiple_of(me_bl * owned, LANES), owned)]

    channel_total = channels * n_ch
    scale, mean_square, ratio = basis_coefficients(channel_total)
    index = lax.broadcasted_iota(jnp.int32, (channels, owned), 0) + me_ch * channels
    x = (2.0 * index.astype(f32) - (channel_total - 1.0)) * (1.0 / (channel_total - 1.0))
    basis = [
        jnp.full((channels, owned), scale[0], f32),
        scale[1] * x,
        scale[2] * (x * x - mean_square),
        scale[3] * (x * (x * x - ratio)),
    ]
    for copy in sol_copies:
        copy.wait_recv()
    solved = [sol[i] for i in range(4)]
    for i in range(4):
        for d in range(4):
            moments[4 * i + d : 4 * i + d + 1, :] = jnp.sum(basis[d] * solved[i], axis=0, keepdims=True)
    mom_copies = []
    for k in range(1, n_ch):
        mom_copies.append(
            pltpu.make_async_remote_copy(
                src_ref=moments, dst_ref=moments_in.at[k], send_sem=mom_send.at[k], recv_sem=mom_recv.at[k],
                device_id={"ch": lax.rem(me_ch + k, n_ch)}, device_id_type=MESH,
            )
        )
        mom_copies[-1].start()
    for i in range(4):
        sol_out[i] = solved[i]
    whole = moments[...]
    for k, copy in enumerate(mom_copies, 1):
        copy.wait_recv()
        whole = whole + moments_in[k]
    for i in range(4):
        row = basis[0] * whole[4 * i : 4 * i + 1, :]
        for d in range(1, 4):
            row = row + basis[d] * whole[4 * i + d : 4 * i + d + 1, :]
        fit_out[i] = row
    for copy in list(pair_copies.values())[:0] + list(data_copies.values()) + sol_copies + mom_copies:
        copy.wait_send()


def fused(n_bl, n_ch, visibilities, sky_model, antenna_pairs, tile_counts, usable_mask):
    channels, slots = usable_mask.shape
    own = channels // n_bl
    owned = STATION_COUNT // n_bl
    out = jax.ShapeDtypeStruct((4, channels, owned), jnp.float32)
    vmem = pl.BlockSpec(memory_space=pltpu.VMEM)
    dma = pltpu.SemaphoreType.DMA
    solved, fitted = pl.pallas_call(
        functools.partial(calibrate, n_bl, n_ch),
        out_shape=(out, out),
        in_specs=[vmem, vmem, vmem, pl.BlockSpec(memory_space=pltpu.SMEM), vmem],
        out_specs=(vmem, vmem),
        scratch_shapes=[
            pltpu.VMEM((n_bl, 16 * own, slots), jnp.bfloat16),
            pltpu.VMEM((n_bl, 16 * own, slots), jnp.bfloat16),
            pltpu.VMEM((n_bl, 2, slots), jnp.int32),
            pltpu.VMEM((n_bl, STATION_COUNT, 2 * slots), jnp.bfloat16),
            pltpu.VMEM((n_bl, 12, own, slots), jnp.float32),
            pltpu.VMEM((4, own, STATION_COUNT), jnp.float32),
            pltpu.VMEM((4, channels, owned), jnp.float32),
            pltpu.VMEM((16, owned), jnp.float32),
            pltpu.VMEM((n_ch, 16, owned), jnp.float32),
            dma((n_bl,)), dma((n_bl,)), dma((n_bl,)), dma((n_bl,)),
            dma((n_bl,)), dma((n_bl,)), dma((n_ch,)), dma((n_ch,)),
        ],
        compiler_params=pltpu.CompilerParams(
            collective_id=0, has_side_effects=True, vmem_limit_bytes=40 * 1024 * 1024
        ),
    )(visibilities, sky_model, antenna_pairs, tile_counts, usable_mask)
    shape = (2, 2, channels, owned)
    return solved.reshape(shape), fitted.reshape(shape)


def split_parts(data):
    planes = data.astype(jnp.float32)
    shape_rest = planes.shape[1:]
    return (planes[:4].reshape((2, 2) + shape_rest), planes[4:].reshape((2, 2) + shape_rest))


def poly_basis(channel_total):
    node_values = (2.0 * jnp.arange(channel_total, dtype=jnp.float32) - (channel_total - 1)) / (
        channel_total - 1
    )
    basis_rows = []
    for degree in range(4):
        vector = node_values**degree
        for earlier in basis_rows:
            vector = vector - jnp.sum(vector * earlier) * earlier
        vector = vector / jnp.sqrt(jnp.sum(vector * vector))
        basis_rows.append(vector)
    return jnp.stack(basis_rows)


def contributions(
    model_real_part, model_imaginary, vis_real, vis_imag, first_gain, second_gain, weights
):
    second_real = second_gain[0][None]
    second_imag = second_gain[1][None]
    left_real = model_real_part * second_real + model_imaginary * second_imag
    left_imag = model_imaginary * second_real - model_real_part * second_imag
    first_num_real = jnp.sum(left_real * vis_real + left_imag * vis_imag, axis=1) * weights
    first_num_imag = jnp.sum(left_real * vis_imag - left_imag * vis_real, axis=1) * weights
    first_den = jnp.sum(left_real * left_real + left_imag * left_imag, axis=1) * weights
    first_real = first_gain[0][:, None]
    first_imag = first_gain[1][:, None]
    right_real = model_real_part * first_real - model_imaginary * first_imag
    right_imag = model_real_part * first_imag + model_imaginary * first_real
    second_num_real = jnp.sum(right_real * vis_real + right_imag * vis_imag, axis=0) * weights
    second_num_imag = jnp.sum(right_imag * vis_real - right_real * vis_imag, axis=0) * weights
    second_den = jnp.sum(right_real * right_real + right_imag * right_imag, axis=0) * weights
    return (
        jnp.stack([first_num_real, first_num_imag, first_den]),
        jnp.stack([second_num_real, second_num_imag, second_den]),
    )


def refresh(station_sums, previous):
    divisor = station_sums[2] + damping
    return jnp.stack(
        [
            (station_sums[0] + damping * previous[0]) / divisor,
            (station_sums[1] + damping * previous[1]) / divisor,
        ]
    )


def station_totals(end_first, end_second, first_endpoints, second_ends):
    total_slots = end_first.shape[3]
    flat_first = end_first.reshape(-1, total_slots)
    flat_second = end_second.reshape(-1, total_slots)
    block_rows = math.gcd(total_slots, 1024)
    block_count = total_slots // block_rows
    station_index = jnp.arange(STATION_COUNT, dtype=jnp.int32)

    def add_block(block, total):
        table_first = (first_endpoints[:, None] == station_index[None, :]).astype(jnp.float32)
        table_second = (second_ends[:, None] == station_index[None, :]).astype(jnp.float32)
        return (
            total
            + jnp.dot(
                flat_first, table_first, precision=highest, preferred_element_type=jnp.float32
            )
            + jnp.dot(
                flat_second, table_second, precision=highest, preferred_element_type=jnp.float32
            )
        )

    empty = jnp.zeros((flat_first.shape[0], STATION_COUNT), jnp.float32)
    summed = lax.fori_loop(0, block_count, add_block, empty)
    return summed.reshape(end_first.shape[:3] + (STATION_COUNT,))


def spread(owned_gains):
    return lax.all_gather(owned_gains, "bl", axis=3, tiled=True)


def local(visibilities, sky_model, antenna_pairs, tile_counts, usable_mask):
    vis_real, vis_imag = split_parts(visibilities)
    model_real_part, model_imaginary = split_parts(sky_model)
    channel_local = visibilities.shape[1]
    tile_rows = visibilities.shape[2]
    owner_count = lax.axis_size("bl")
    owned_count = STATION_COUNT // owner_count
    owner_start = lax.axis_index("bl") * owned_count
    live_slots = jnp.arange(tile_rows, dtype=jnp.int32) < tile_counts[0]
    weights = usable_mask.astype(jnp.float32) * live_slots.astype(jnp.float32)[None, :]
    channel_total = channel_local * lax.axis_size("ch")
    poly_rows = lax.dynamic_slice_in_dim(
        poly_basis(channel_total), lax.axis_index("ch") * channel_local, channel_local, 1
    )
    gain_state = jnp.stack(
        [
            jnp.ones((2, channel_local, STATION_COUNT), jnp.float32),
            jnp.zeros((2, channel_local, STATION_COUNT), jnp.float32),
        ]
    )
    solved = gain_state
    for iteration in range(SWEEPS):
        first_gain = jnp.take(gain_state, antenna_pairs[0], axis=3)
        second_gain = jnp.take(gain_state, antenna_pairs[1], axis=3)
        end_first, end_second = contributions(
            model_real_part, model_imaginary, vis_real, vis_imag, first_gain, second_gain, weights
        )
        partial_sums = station_totals(end_first, end_second, antenna_pairs[0], antenna_pairs[1])
        station_sums = lax.psum_scatter(partial_sums, "bl", scatter_dimension=3, tiled=True)
        previous = lax.dynamic_slice_in_dim(gain_state, owner_start, owned_count, 3)
        renewed = refresh(station_sums, previous)
        if iteration == 1:
            renewed = 0.5 * (renewed + previous)
        solved = renewed
        if iteration < SWEEPS - 1:
            gain_state = spread(renewed)
    local_moments = jnp.einsum("kc,rfca->krfa", poly_rows, solved, precision=highest)
    moments = lax.psum(local_moments, "ch")
    fitted = jnp.einsum("kc,krfa->rfca", poly_rows, moments, precision=highest)
    return (solved, fitted)


def solution(mesh):
    n_bl, n_ch = mesh.shape["bl"], mesh.shape["ch"]

    def run(visibilities, sky_model, antenna_pairs, tile_counts, usable_mask):
        channels, slots = usable_mask.shape
        whole_tiles = (
            channels % (n_bl * SUBLANES) == 0
            and slots % LANES == 0
            and STATION_COUNT % (n_bl * LANES) == 0
            and n_bl & (n_bl - 1) == 0
        )
        plan = functools.partial(fused, n_bl, n_ch) if whole_tiles else local
        return plan(visibilities, sky_model, antenna_pairs, tile_counts, usable_mask)

    return jax.shard_map(
        run,
        mesh=mesh,
        in_specs=(
            P(None, "ch", ("grp", "bl")),
            P(None, "ch", ("grp", "bl")),
            P(None, ("grp", "bl")),
            P(("grp", "bl")),
            P("ch", ("grp", "bl")),
        ),
        out_specs=(P(None, None, "ch", ("grp", "bl")), P(None, None, "ch", ("grp", "bl"))),
        check_vma=False,
    )
```

```python
import functools
import math

import jax
import jax.numpy as jnp
import numpy as np
from jax import lax
from jax.experimental import pallas as pl
from jax.experimental.pallas import tpu as pltpu
from jax.sharding import PartitionSpec as P

STATION_COUNT = 512
SWEEPS = 2


damping = 4.0
highest = lax.Precision.HIGHEST
MESH = pl.DeviceIdType.MESH
LANES = 128
SUBLANES = 8


def basis_coefficients(channel_total):
    x = (2.0 * np.arange(channel_total, dtype=np.float64) - (channel_total - 1)) / (channel_total - 1)
    m = np.mean(x**2)
    r = np.sum(x**4) / np.sum(x**2)
    a = [1.0 / np.sqrt(np.sum(v * v)) for v in (np.ones_like(x), x, x**2 - m, x**3 - r * x)]
    return [float(v) for v in a], float(m), float(r)


def split_hi_lo(values):
    hi = values.astype(jnp.bfloat16)
    lo = (values - hi.astype(jnp.float32)).astype(jnp.bfloat16)
    return jnp.concatenate([hi, lo], axis=0)


def exchange_partner(me, k):
    partner, bit = 0, 1
    while bit <= k:
        digit = (me // bit) % 2
        partner = partner + (1 - digit if k & bit else digit) * bit
        bit *= 2
    return partner + (me // bit) * bit


def calibrate(
    n_bl, n_ch, vis_hbm, model_hbm, pairs_hbm, counts_ref, mask_hbm, sol_out, fit_out,
    vis_ref, model_ref, mask_ref, outgoing, incoming, pairs_all, onehot, products, state, sol, fit, moments, moments_in,
    load_sem, store_sem, data_send, data_recv, pair_send, pair_recv, sol_send, sol_recv, mom_send, mom_recv,
):
    me_bl = lax.axis_index("bl")
    me_ch = lax.axis_index("ch")
    channels, slots = mask_ref.shape
    own = channels // n_bl
    stations = state.shape[2]
    owned = stations // n_bl
    half = stations // 2
    f32 = jnp.float32

    loads = [
        pltpu.make_async_copy(pairs_hbm, pairs_all.at[0], load_sem.at[0]),
        pltpu.make_async_copy(vis_hbm, vis_ref, load_sem.at[1]),
        pltpu.make_async_copy(mask_hbm, mask_ref, load_sem.at[2]),
        pltpu.make_async_copy(model_hbm, model_ref, load_sem.at[3]),
    ]
    for load in loads:
        load.start()
    barrier = pltpu.get_barrier_semaphore()
    for k in range(1, n_bl):
        pl.semaphore_signal(barrier, inc=1, device_id={"bl": exchange_partner(me_bl, k)}, device_id_type=MESH)
    for k in range(1, n_ch):
        pl.semaphore_signal(barrier, inc=1, device_id={"ch": lax.rem(me_ch + k, n_ch)}, device_id_type=MESH)

    def prepare(part, ref, weights):
        for plane in range(0, 8, 2):
            pair = [ref[j].astype(f32) for j in (plane, plane + 1)]
            if weights is not None:
                pair = [v * weights for v in pair]
            for z in range(n_bl):
                rows = slice(z * own, (z + 1) * own)
                both = jnp.concatenate([pair[0][rows], pair[1][rows]], axis=0)
                outgoing[part, z, plane * own : (plane + 2) * own, :] = both.astype(jnp.bfloat16)

    data_copies = {}

    def send(part):
        for k in range(n_bl - 1, 0, -1):
            partner = exchange_partner(me_bl, k)
            data_copies[part, k] = pltpu.make_async_remote_copy(
                src_ref=outgoing.at[part, partner], dst_ref=incoming.at[part, k], send_sem=data_send.at[part, k],
                recv_sem=data_recv.at[part, k], device_id={"bl": partner}, device_id_type=MESH,
            )
            data_copies[part, k].start()

    loads[0].wait()
    loads[1].wait()
    prepare(0, vis_ref, None)
    pl.semaphore_wait(barrier, n_bl + n_ch - 2)
    pair_copies = {}
    for k in range(1, n_bl):
        pair_copies[k] = pltpu.make_async_remote_copy(
            src_ref=pairs_all.at[0], dst_ref=pairs_all.at[k], send_sem=pair_send.at[k], recv_sem=pair_recv.at[k],
            device_id={"bl": exchange_partner(me_bl, k)}, device_id_type=MESH,
        )
        pair_copies[k].start()
    send(0)
    loads[2].wait()
    loads[3].wait()
    live = lax.broadcasted_iota(jnp.int32, (channels, slots), 1) < counts_ref[0]
    prepare(1, model_ref, jnp.where(live, mask_ref[...], 0).astype(f32))
    send(1)

    def end_row(k):
        return jnp.concatenate([pairs_all[k, 0:1, :], pairs_all[k, 1:2, :]], axis=1)

    def is_upper(k):
        return end_row(k) >= half

    def build_onehot(k):
        ends = end_row(k)
        within = jnp.where(ends >= half, ends - half, ends)
        step = 32

        def rows(i, carry):
            base = pl.multiple_of(i * step, step)
            station = lax.broadcasted_iota(jnp.int32, (step, 2 * slots), 0) + base
            onehot[k, pl.ds(base, step), :] = jnp.where(station == within, 1.0, 0.0).astype(jnp.bfloat16)
            return carry

        lax.fori_loop(0, half // step, rows, 0)

    def scatter(k, first, second):
        terms = jnp.concatenate(
            [jnp.concatenate(first, axis=0), jnp.concatenate(second, axis=0)], axis=1
        )
        upper = jnp.where(is_upper(k), terms, 0.0)
        both = jnp.concatenate([split_hi_lo(terms - upper), split_hi_lo(upper)], axis=0)
        summed = lax.dot_general(both, onehot[k], (((1,), (1,)), ((), ())), preferred_element_type=f32)
        n = terms.shape[0]
        return summed[:n] + summed[n : 2 * n], summed[2 * n : 3 * n] + summed[3 * n :]

    def add(left, right):
        return right if left is None else (left[0] + right[0], left[1] + right[1])

    def make_products(k, vis_block, model_block):
        vis = vis_block.astype(f32).reshape(8, own, slots)
        model = model_block.astype(f32).reshape(8, own, slots)
        a_re, a_im, b = [], [], []
        for j in range(4):
            vr, vi, mr, mi = vis[j], vis[4 + j], model[j], model[4 + j]
            a_re.append(mr * vr + mi * vi)
            a_im.append(mr * vi - mi * vr)
            b.append(mr * mr + mi * mi)
        for j in range(4):
            products[k, j] = a_re[j]
            products[k, 4 + j] = a_im[j]
            products[k, 8 + j] = b[j]
        first = [a_re[0] + a_re[1], a_re[2] + a_re[3], a_im[0] + a_im[1], a_im[2] + a_im[3], b[0] + b[1], b[2] + b[3]]
        second = [
            a_re[0] + a_re[2], a_re[1] + a_re[3], -(a_im[0] + a_im[2]), -(a_im[1] + a_im[3]), b[0] + b[2], b[1] + b[3],
        ]
        return scatter(k, first, second)

    build_onehot(0)
    total = make_products(0, outgoing[0, me_bl], outgoing[1, me_bl])
    for k in range(1, n_bl):
        pair_copies[k].wait()
        build_onehot(k)
    for k in range(1, n_bl):
        data_copies[0, k].wait_recv()
        data_copies[1, k].wait_recv()
        total = add(total, make_products(k, incoming[0, k], incoming[1, k]))

    feeds = 2 * own
    total = jnp.concatenate(total, axis=1)
    divisor = total[2 * feeds :] + damping
    gain_re = (total[:feeds] + damping) / divisor
    gain_im = total[feeds : 2 * feeds] / divisor
    gains = jnp.concatenate([gain_re, gain_im], axis=0)

    split_gains = split_hi_lo(gains)
    split_gains = jnp.concatenate([split_gains[:, :half], split_gains[:, half:]], axis=0)
    total = None
    for k in range(n_bl):
        both = jnp.dot(split_gains, onehot[k], preferred_element_type=f32)
        n = 2 * feeds
        both = jnp.where(is_upper(k), both[2 * n : 3 * n] + both[3 * n :], both[:n] + both[n : 2 * n])
        at = [[both[i * own : (i + 1) * own, e * slots : (e + 1) * slots] for i in range(4)] for e in range(2)]
        ga, ge = at
        ga_sq = [ga[p] * ga[p] + ga[2 + p] * ga[2 + p] for p in range(2)]
        ge_sq = [ge[p] * ge[p] + ge[2 + p] * ge[2 + p] for p in range(2)]
        a_re = [products[k, j] for j in range(4)]
        a_im = [products[k, 4 + j] for j in range(4)]
        b = [products[k, 8 + j] for j in range(4)]
        first, second = [[], [], []], [[], [], []]
        for p in range(2):
            j0, j1 = 2 * p, 2 * p + 1
            first[0].append(a_re[j0] * ge[0] - a_im[j0] * ge[2] + a_re[j1] * ge[1] - a_im[j1] * ge[3])
            first[1].append(a_re[j0] * ge[2] + a_im[j0] * ge[0] + a_re[j1] * ge[3] + a_im[j1] * ge[1])
            first[2].append(b[j0] * ge_sq[0] + b[j1] * ge_sq[1])
        for q in range(2):
            j0, j1 = q, 2 + q
            second[0].append(a_re[j0] * ga[0] + a_im[j0] * ga[2] + a_re[j1] * ga[1] + a_im[j1] * ga[3])
            second[1].append(a_re[j0] * ga[2] - a_im[j0] * ga[0] + a_re[j1] * ga[3] - a_im[j1] * ga[1])
            second[2].append(b[j0] * ga_sq[0] + b[j1] * ga_sq[1])
        total = add(total, scatter(k, sum(first, []), sum(second, [])))

    total = jnp.concatenate(total, axis=1)
    divisor = total[2 * feeds :] + damping
    for i in range(2):
        previous = gains[i * feeds : (i + 1) * feeds]
        renewed = (total[i * feeds : (i + 1) * feeds] + damping * previous) / divisor
        state[2 * i : 2 * i + 2] = (0.5 * (renewed + previous)).reshape(2, own, stations)

    my_rows = pl.ds(pl.multiple_of(me_bl * own, SUBLANES), own)
    sol_copies = []
    for k in range(n_bl - 1, 0, -1):
        partner = exchange_partner(me_bl, k)
        sol_copies.append(
            pltpu.make_async_remote_copy(
                src_ref=state.at[:, :, pl.ds(pl.multiple_of(partner * owned, LANES), owned)],
                dst_ref=sol.at[:, my_rows, :], send_sem=sol_send.at[k], recv_sem=sol_recv.at[k],
                device_id={"bl": partner}, device_id_type=MESH,
            )
        )
        sol_copies[-1].start()
    sol[:, my_rows, :] = state[:, :, pl.ds(pl.multiple_of(me_bl * owned, LANES), owned)]

    channel_total = channels * n_ch
    scale, mean_square, ratio = basis_coefficients(channel_total)
    index = lax.broadcasted_iota(jnp.int32, (channels, owned), 0) + me_ch * channels
    x = (2.0 * index.astype(f32) - (channel_total - 1.0)) * (1.0 / (channel_total - 1.0))
    basis = [
        jnp.full((channels, owned), scale[0], f32),
        scale[1] * x,
        scale[2] * (x * x - mean_square),
        scale[3] * (x * (x * x - ratio)),
    ]
    for copy in sol_copies:
        copy.wait_recv()
    stores = [
        pltpu.make_async_copy(sol, sol_out, store_sem.at[0]),
        pltpu.make_async_copy(fit, fit_out, store_sem.at[1]),
    ]
    stores[0].start()
    for i in range(4):
        solved = sol[i]
        for d in range(4):
            moments[4 * i + d : 4 * i + d + 1, :] = jnp.sum(basis[d] * solved, axis=0, keepdims=True)
    mom_copies = []
    for k in range(1, n_ch):
        mom_copies.append(
            pltpu.make_async_remote_copy(
                src_ref=moments, dst_ref=moments_in.at[k], send_sem=mom_send.at[k], recv_sem=mom_recv.at[k],
                device_id={"ch": lax.rem(me_ch + k, n_ch)}, device_id_type=MESH,
            )
        )
        mom_copies[-1].start()
    whole = moments[...]
    for k, copy in enumerate(mom_copies, 1):
        copy.wait_recv()
        whole = whole + moments_in[k]
    for i in range(4):
        row = basis[0] * whole[4 * i : 4 * i + 1, :]
        for d in range(1, 4):
            row = row + basis[d] * whole[4 * i + d : 4 * i + d + 1, :]
        fit[i] = row
    stores[1].start()
    for copy in list(data_copies.values()) + sol_copies + mom_copies:
        copy.wait_send()
    for store in stores:
        store.wait()


def write_out(solved_ref, fitted_ref, solved_out, fitted_out, sems):
    copies = [
        pltpu.make_async_copy(solved_ref, solved_out, sems.at[0]),
        pltpu.make_async_copy(fitted_ref, fitted_out, sems.at[1]),
    ]
    for copy in copies:
        copy.start()
    for copy in copies:
        copy.wait()


def fused(n_bl, n_ch, visibilities, sky_model, antenna_pairs, tile_counts, usable_mask):
    channels, slots = usable_mask.shape
    own = channels // n_bl
    owned = STATION_COUNT // n_bl
    out = jax.ShapeDtypeStruct((4, channels, owned), jnp.float32)
    hbm = pl.BlockSpec(memory_space=pltpu.HBM)
    dma = pltpu.SemaphoreType.DMA
    solved, fitted = pl.pallas_call(
        functools.partial(calibrate, n_bl, n_ch),
        out_shape=(out, out),
        in_specs=[hbm, hbm, hbm, pl.BlockSpec(memory_space=pltpu.SMEM), hbm],
        out_specs=(hbm, hbm),
        scratch_shapes=[
            pltpu.VMEM(visibilities.shape, visibilities.dtype),
            pltpu.VMEM(sky_model.shape, sky_model.dtype),
            pltpu.VMEM(usable_mask.shape, usable_mask.dtype),
            pltpu.VMEM((2, n_bl, 8 * own, slots), jnp.bfloat16),
            pltpu.VMEM((2, n_bl, 8 * own, slots), jnp.bfloat16),
            pltpu.VMEM((n_bl, 2, slots), jnp.int32),
            pltpu.VMEM((n_bl, STATION_COUNT // 2, 2 * slots), jnp.bfloat16),
            pltpu.VMEM((n_bl, 12, own, slots), jnp.float32),
            pltpu.VMEM((4, own, STATION_COUNT), jnp.float32),
            pltpu.VMEM((4, channels, owned), jnp.float32),
            pltpu.VMEM((4, channels, owned), jnp.float32),
            pltpu.VMEM((16, owned), jnp.float32),
            pltpu.VMEM((n_ch, 16, owned), jnp.float32),
            dma((4,)), dma((2,)), dma((2, n_bl)), dma((2, n_bl)), dma((n_bl,)), dma((n_bl,)),
            dma((n_bl,)), dma((n_bl,)), dma((n_ch,)), dma((n_ch,)),
        ],
        compiler_params=pltpu.CompilerParams(
            collective_id=0, has_side_effects=True, vmem_limit_bytes=64 * 1024 * 1024
        ),
    )(visibilities, sky_model, antenna_pairs, tile_counts, usable_mask)
    solved, fitted = pl.pallas_call(
        write_out,
        out_shape=(out, out),
        in_specs=[hbm, hbm],
        out_specs=(hbm, hbm),
        scratch_shapes=[dma((2,))],
        compiler_params=pltpu.CompilerParams(vmem_limit_bytes=64 * 1024 * 1024),
    )(solved, fitted)
    shape = (2, 2, channels, owned)
    return solved.reshape(shape), fitted.reshape(shape)


def split_parts(data):
    planes = data.astype(jnp.float32)
    shape_rest = planes.shape[1:]
    return (planes[:4].reshape((2, 2) + shape_rest), planes[4:].reshape((2, 2) + shape_rest))


def poly_basis(channel_total):
    node_values = (2.0 * jnp.arange(channel_total, dtype=jnp.float32) - (channel_total - 1)) / (
        channel_total - 1
    )
    basis_rows = []
    for degree in range(4):
        vector = node_values**degree
        for earlier in basis_rows:
            vector = vector - jnp.sum(vector * earlier) * earlier
        vector = vector / jnp.sqrt(jnp.sum(vector * vector))
        basis_rows.append(vector)
    return jnp.stack(basis_rows)


def contributions(
    model_real_part, model_imaginary, vis_real, vis_imag, first_gain, second_gain, weights
):
    second_real = second_gain[0][None]
    second_imag = second_gain[1][None]
    left_real = model_real_part * second_real + model_imaginary * second_imag
    left_imag = model_imaginary * second_real - model_real_part * second_imag
    first_num_real = jnp.sum(left_real * vis_real + left_imag * vis_imag, axis=1) * weights
    first_num_imag = jnp.sum(left_real * vis_imag - left_imag * vis_real, axis=1) * weights
    first_den = jnp.sum(left_real * left_real + left_imag * left_imag, axis=1) * weights
    first_real = first_gain[0][:, None]
    first_imag = first_gain[1][:, None]
    right_real = model_real_part * first_real - model_imaginary * first_imag
    right_imag = model_real_part * first_imag + model_imaginary * first_real
    second_num_real = jnp.sum(right_real * vis_real + right_imag * vis_imag, axis=0) * weights
    second_num_imag = jnp.sum(right_imag * vis_real - right_real * vis_imag, axis=0) * weights
    second_den = jnp.sum(right_real * right_real + right_imag * right_imag, axis=0) * weights
    return (
        jnp.stack([first_num_real, first_num_imag, first_den]),
        jnp.stack([second_num_real, second_num_imag, second_den]),
    )


def refresh(station_sums, previous):
    divisor = station_sums[2] + damping
    return jnp.stack(
        [
            (station_sums[0] + damping * previous[0]) / divisor,
            (station_sums[1] + damping * previous[1]) / divisor,
        ]
    )


def station_totals(end_first, end_second, first_endpoints, second_ends):
    total_slots = end_first.shape[3]
    flat_first = end_first.reshape(-1, total_slots)
    flat_second = end_second.reshape(-1, total_slots)
    block_rows = math.gcd(total_slots, 1024)
    block_count = total_slots // block_rows
    station_index = jnp.arange(STATION_COUNT, dtype=jnp.int32)

    def add_block(block, total):
        table_first = (first_endpoints[:, None] == station_index[None, :]).astype(jnp.float32)
        table_second = (second_ends[:, None] == station_index[None, :]).astype(jnp.float32)
        return (
            total
            + jnp.dot(
                flat_first, table_first, precision=highest, preferred_element_type=jnp.float32
            )
            + jnp.dot(
                flat_second, table_second, precision=highest, preferred_element_type=jnp.float32
            )
        )

    empty = jnp.zeros((flat_first.shape[0], STATION_COUNT), jnp.float32)
    summed = lax.fori_loop(0, block_count, add_block, empty)
    return summed.reshape(end_first.shape[:3] + (STATION_COUNT,))


def spread(owned_gains):
    return lax.all_gather(owned_gains, "bl", axis=3, tiled=True)


def local(visibilities, sky_model, antenna_pairs, tile_counts, usable_mask):
    vis_real, vis_imag = split_parts(visibilities)
    model_real_part, model_imaginary = split_parts(sky_model)
    channel_local = visibilities.shape[1]
    tile_rows = visibilities.shape[2]
    owner_count = lax.axis_size("bl")
    owned_count = STATION_COUNT // owner_count
    owner_start = lax.axis_index("bl") * owned_count
    live_slots = jnp.arange(tile_rows, dtype=jnp.int32) < tile_counts[0]
    weights = usable_mask.astype(jnp.float32) * live_slots.astype(jnp.float32)[None, :]
    channel_total = channel_local * lax.axis_size("ch")
    poly_rows = lax.dynamic_slice_in_dim(
        poly_basis(channel_total), lax.axis_index("ch") * channel_local, channel_local, 1
    )
    gain_state = jnp.stack(
        [
            jnp.ones((2, channel_local, STATION_COUNT), jnp.float32),
            jnp.zeros((2, channel_local, STATION_COUNT), jnp.float32),
        ]
    )
    solved = gain_state
    for iteration in range(SWEEPS):
        first_gain = jnp.take(gain_state, antenna_pairs[0], axis=3)
        second_gain = jnp.take(gain_state, antenna_pairs[1], axis=3)
        end_first, end_second = contributions(
            model_real_part, model_imaginary, vis_real, vis_imag, first_gain, second_gain, weights
        )
        partial_sums = station_totals(end_first, end_second, antenna_pairs[0], antenna_pairs[1])
        station_sums = lax.psum_scatter(partial_sums, "bl", scatter_dimension=3, tiled=True)
        previous = lax.dynamic_slice_in_dim(gain_state, owner_start, owned_count, 3)
        renewed = refresh(station_sums, previous)
        if iteration == 1:
            renewed = 0.5 * (renewed + previous)
        solved = renewed
        if iteration < SWEEPS - 1:
            gain_state = spread(renewed)
    local_moments = jnp.einsum("kc,rfca->krfa", poly_rows, solved, precision=highest)
    moments = lax.psum(local_moments, "ch")
    fitted = jnp.einsum("kc,krfa->rfca", poly_rows, moments, precision=highest)
    return (solved, fitted)


def solution(mesh):
    n_bl, n_ch = mesh.shape["bl"], mesh.shape["ch"]

    def run(visibilities, sky_model, antenna_pairs, tile_counts, usable_mask):
        channels, slots = usable_mask.shape
        whole_tiles = (
            channels % (n_bl * SUBLANES) == 0
            and slots % LANES == 0
            and STATION_COUNT % (n_bl * LANES) == 0
            and n_bl & (n_bl - 1) == 0
        )
        plan = functools.partial(fused, n_bl, n_ch) if whole_tiles else local
        return plan(visibilities, sky_model, antenna_pairs, tile_counts, usable_mask)

    return jax.shard_map(
        run,
        mesh=mesh,
        in_specs=(
            P(None, "ch", ("grp", "bl")),
            P(None, "ch", ("grp", "bl")),
            P(None, ("grp", "bl")),
            P(("grp", "bl")),
            P("ch", ("grp", "bl")),
        ),
        out_specs=(P(None, None, "ch", ("grp", "bl")), P(None, None, "ch", ("grp", "bl"))),
        check_vma=False,
    )
```

```python
import functools
import math

import jax
import jax.numpy as jnp
import numpy as np
from jax import lax
from jax.experimental import pallas as pl
from jax.experimental.pallas import tpu as pltpu
from jax.sharding import PartitionSpec as P

STATION_COUNT = 512
SWEEPS = 2


damping = 4.0
highest = lax.Precision.HIGHEST
MESH = pl.DeviceIdType.MESH
LANES = 128
SUBLANES = 8


def basis_coefficients(channel_total):
    x = (2.0 * np.arange(channel_total, dtype=np.float64) - (channel_total - 1)) / (channel_total - 1)
    m = np.mean(x**2)
    r = np.sum(x**4) / np.sum(x**2)
    a = [1.0 / np.sqrt(np.sum(v * v)) for v in (np.ones_like(x), x, x**2 - m, x**3 - r * x)]
    return [float(v) for v in a], float(m), float(r)


def split_hi_lo(values):
    hi = values.astype(jnp.bfloat16)
    lo = (values - hi.astype(jnp.float32)).astype(jnp.bfloat16)
    return jnp.concatenate([hi, lo], axis=0)


def exchange_partner(me, k):
    partner, bit = 0, 1
    while bit <= k:
        digit = (me // bit) % 2
        partner = partner + (1 - digit if k & bit else digit) * bit
        bit *= 2
    return partner + (me // bit) * bit


def calibrate(
    n_bl, n_ch, vis_hbm, model_hbm, pairs_hbm, counts_ref, mask_hbm, sol, fit,
    vis_ref, model_ref, mask_ref, outgoing, incoming, pairs_all, onehot, onehot_t, products, state, moments, moments_in,
    load_sem, data_send, data_recv, pair_send, pair_recv, sol_send, sol_recv, mom_send, mom_recv,
):
    me_bl = lax.axis_index("bl")
    me_ch = lax.axis_index("ch")
    channels, slots = mask_ref.shape
    own = channels // n_bl
    stations = state.shape[2]
    owned = stations // n_bl
    half = stations // 2
    f32 = jnp.float32

    loads = [
        pltpu.make_async_copy(pairs_hbm, pairs_all.at[0], load_sem.at[0]),
        pltpu.make_async_copy(vis_hbm, vis_ref, load_sem.at[1]),
        pltpu.make_async_copy(mask_hbm, mask_ref, load_sem.at[2]),
        pltpu.make_async_copy(model_hbm, model_ref, load_sem.at[3]),
    ]
    for load in loads:
        load.start()
    barrier = pltpu.get_barrier_semaphore()
    for k in range(1, n_bl):
        pl.semaphore_signal(barrier, inc=1, device_id={"bl": exchange_partner(me_bl, k)}, device_id_type=MESH)
    for k in range(1, n_ch):
        pl.semaphore_signal(barrier, inc=1, device_id={"ch": lax.rem(me_ch + k, n_ch)}, device_id_type=MESH)

    def prepare(part, ref, weights):
        for plane in range(0, 8, 2):
            pair = [ref[j].astype(f32) for j in (plane, plane + 1)]
            if weights is not None:
                pair = [v * weights for v in pair]
            for z in range(n_bl):
                rows = slice(z * own, (z + 1) * own)
                both = jnp.concatenate([pair[0][rows], pair[1][rows]], axis=0)
                outgoing[part, z, plane * own : (plane + 2) * own, :] = both.astype(jnp.bfloat16)

    data_copies = {}

    def send(part):
        for k in range(n_bl - 1, 0, -1):
            partner = exchange_partner(me_bl, k)
            data_copies[part, k] = pltpu.make_async_remote_copy(
                src_ref=outgoing.at[part, partner], dst_ref=incoming.at[part, k], send_sem=data_send.at[part, k],
                recv_sem=data_recv.at[part, k], device_id={"bl": partner}, device_id_type=MESH,
            )
            data_copies[part, k].start()

    loads[0].wait()
    loads[1].wait()
    prepare(0, vis_ref, None)
    pl.semaphore_wait(barrier, n_bl + n_ch - 2)
    pair_copies = {}
    for k in range(1, n_bl):
        pair_copies[k] = pltpu.make_async_remote_copy(
            src_ref=pairs_all.at[0], dst_ref=pairs_all.at[k], send_sem=pair_send.at[k], recv_sem=pair_recv.at[k],
            device_id={"bl": exchange_partner(me_bl, k)}, device_id_type=MESH,
        )
        pair_copies[k].start()
    send(0)
    loads[2].wait()
    loads[3].wait()
    live = lax.broadcasted_iota(jnp.int32, (channels, slots), 1) < counts_ref[0]
    prepare(1, model_ref, jnp.where(live, mask_ref[...], 0).astype(f32))
    send(1)

    def end_row(k):
        return jnp.concatenate([pairs_all[k, 0:1, :], pairs_all[k, 1:2, :]], axis=1)

    def is_upper(k):
        return end_row(k) >= half

    def build_onehot(k):
        ends = end_row(k)
        within = jnp.where(ends >= half, ends - half, ends)
        step = 32

        def rows(i, carry):
            base = pl.multiple_of(i * step, step)
            station = lax.broadcasted_iota(jnp.int32, (step, 2 * slots), 0) + base
            onehot[k, pl.ds(base, step), :] = jnp.where(station == within, 1.0, 0.0).astype(jnp.bfloat16)
            return carry

        lax.fori_loop(0, half // step, rows, 0)
        onehot_t[k] = onehot[k].T

    def scatter(k, first, second):
        terms = jnp.concatenate(
            [jnp.concatenate(first, axis=0), jnp.concatenate(second, axis=0)], axis=1
        )
        split = split_hi_lo(terms)
        upper = split * jnp.where(is_upper(k), 1.0, 0.0).astype(jnp.bfloat16)
        both = jnp.concatenate([split - upper, upper], axis=0)
        summed = jnp.dot(both, onehot_t[k], preferred_element_type=f32)
        n = terms.shape[0]
        return summed[:n] + summed[n : 2 * n], summed[2 * n : 3 * n] + summed[3 * n :]

    def add(left, right):
        return right if left is None else (left[0] + right[0], left[1] + right[1])

    def make_products(k, vis_block, model_block):
        vis = vis_block.astype(f32).reshape(8, own, slots)
        model = model_block.astype(f32).reshape(8, own, slots)
        a_re, a_im, b = [], [], []
        for j in range(4):
            vr, vi, mr, mi = vis[j], vis[4 + j], model[j], model[4 + j]
            a_re.append(mr * vr + mi * vi)
            a_im.append(mr * vi - mi * vr)
            b.append(mr * mr + mi * mi)
        for j in range(4):
            products[k, j] = a_re[j]
            products[k, 4 + j] = a_im[j]
            products[k, 8 + j] = b[j]
        first = [a_re[0] + a_re[1], a_re[2] + a_re[3], a_im[0] + a_im[1], a_im[2] + a_im[3], b[0] + b[1], b[2] + b[3]]
        second = [
            a_re[0] + a_re[2], a_re[1] + a_re[3], -(a_im[0] + a_im[2]), -(a_im[1] + a_im[3]), b[0] + b[2], b[1] + b[3],
        ]
        return scatter(k, first, second)

    build_onehot(0)
    total = make_products(0, outgoing[0, me_bl], outgoing[1, me_bl])
    for k in range(1, n_bl):
        pair_copies[k].wait()
        build_onehot(k)
    for k in range(1, n_bl):
        data_copies[0, k].wait_recv()
        data_copies[1, k].wait_recv()
        total = add(total, make_products(k, incoming[0, k], incoming[1, k]))

    feeds = 2 * own
    total = jnp.concatenate(total, axis=1)
    divisor = total[2 * feeds :] + damping
    gain_re = (total[:feeds] + damping) / divisor
    gain_im = total[feeds : 2 * feeds] / divisor
    gains = jnp.concatenate([gain_re, gain_im], axis=0)

    split_gains = split_hi_lo(gains)
    split_gains = jnp.concatenate([split_gains[:, :half], split_gains[:, half:]], axis=0)
    total = None
    for k in range(n_bl):
        both = jnp.dot(split_gains, onehot[k], preferred_element_type=f32)
        n = 2 * feeds
        both = jnp.where(is_upper(k), both[2 * n : 3 * n] + both[3 * n :], both[:n] + both[n : 2 * n])
        at = [[both[i * own : (i + 1) * own, e * slots : (e + 1) * slots] for i in range(4)] for e in range(2)]
        ga, ge = at
        ga_sq = [ga[p] * ga[p] + ga[2 + p] * ga[2 + p] for p in range(2)]
        ge_sq = [ge[p] * ge[p] + ge[2 + p] * ge[2 + p] for p in range(2)]
        a_re = [products[k, j] for j in range(4)]
        a_im = [products[k, 4 + j] for j in range(4)]
        b = [products[k, 8 + j] for j in range(4)]
        first, second = [[], [], []], [[], [], []]
        for p in range(2):
            j0, j1 = 2 * p, 2 * p + 1
            first[0].append(a_re[j0] * ge[0] - a_im[j0] * ge[2] + a_re[j1] * ge[1] - a_im[j1] * ge[3])
            first[1].append(a_re[j0] * ge[2] + a_im[j0] * ge[0] + a_re[j1] * ge[3] + a_im[j1] * ge[1])
            first[2].append(b[j0] * ge_sq[0] + b[j1] * ge_sq[1])
        for q in range(2):
            j0, j1 = q, 2 + q
            second[0].append(a_re[j0] * ga[0] + a_im[j0] * ga[2] + a_re[j1] * ga[1] + a_im[j1] * ga[3])
            second[1].append(a_re[j0] * ga[2] - a_im[j0] * ga[0] + a_re[j1] * ga[3] - a_im[j1] * ga[1])
            second[2].append(b[j0] * ga_sq[0] + b[j1] * ga_sq[1])
        total = add(total, scatter(k, sum(first, []), sum(second, [])))

    total = jnp.concatenate(total, axis=1)
    divisor = total[2 * feeds :] + damping
    for i in range(2):
        previous = gains[i * feeds : (i + 1) * feeds]
        renewed = (total[i * feeds : (i + 1) * feeds] + damping * previous) / divisor
        state[2 * i : 2 * i + 2] = (0.5 * (renewed + previous)).reshape(2, own, stations)

    my_rows = pl.ds(pl.multiple_of(me_bl * own, SUBLANES), own)
    sol_copies = []
    for k in range(n_bl - 1, 0, -1):
        partner = exchange_partner(me_bl, k)
        sol_copies.append(
            pltpu.make_async_remote_copy(
                src_ref=state.at[:, :, pl.ds(pl.multiple_of(partner * owned, LANES), owned)],
                dst_ref=sol.at[:, my_rows, :], send_sem=sol_send.at[k], recv_sem=sol_recv.at[k],
                device_id={"bl": partner}, device_id_type=MESH,
            )
        )
        sol_copies[-1].start()
    sol[:, my_rows, :] = state[:, :, pl.ds(pl.multiple_of(me_bl * owned, LANES), owned)]

    channel_total = channels * n_ch
    scale, mean_square, ratio = basis_coefficients(channel_total)
    index = lax.broadcasted_iota(jnp.int32, (channels, owned), 0) + me_ch * channels
    x = (2.0 * index.astype(f32) - (channel_total - 1.0)) * (1.0 / (channel_total - 1.0))
    basis = [
        jnp.full((channels, owned), scale[0], f32),
        scale[1] * x,
        scale[2] * (x * x - mean_square),
        scale[3] * (x * (x * x - ratio)),
    ]
    for copy in sol_copies:
        copy.wait_recv()
    for i in range(4):
        solved = sol[i]
        for d in range(4):
            moments[4 * i + d : 4 * i + d + 1, :] = jnp.sum(basis[d] * solved, axis=0, keepdims=True)
    mom_copies = []
    for k in range(1, n_ch):
        mom_copies.append(
            pltpu.make_async_remote_copy(
                src_ref=moments, dst_ref=moments_in.at[k], send_sem=mom_send.at[k], recv_sem=mom_recv.at[k],
                device_id={"ch": lax.rem(me_ch + k, n_ch)}, device_id_type=MESH,
            )
        )
        mom_copies[-1].start()
    whole = moments[...]
    for k, copy in enumerate(mom_copies, 1):
        copy.wait_recv()
        whole = whole + moments_in[k]
    for i in range(4):
        row = basis[0] * whole[4 * i : 4 * i + 1, :]
        for d in range(1, 4):
            row = row + basis[d] * whole[4 * i + d : 4 * i + d + 1, :]
        fit[i] = row
    for copy in list(data_copies.values()) + sol_copies + mom_copies:
        copy.wait_send()


def write_out(solved_ref, fitted_ref, solved_out, fitted_out, sems):
    copies = [
        pltpu.make_async_copy(solved_ref, solved_out, sems.at[0]),
        pltpu.make_async_copy(fitted_ref, fitted_out, sems.at[1]),
    ]
    for copy in copies:
        copy.start()
    for copy in copies:
        copy.wait()


def fused(n_bl, n_ch, visibilities, sky_model, antenna_pairs, tile_counts, usable_mask):
    channels, slots = usable_mask.shape
    own = channels // n_bl
    owned = STATION_COUNT // n_bl
    out = jax.ShapeDtypeStruct((4, channels, owned), jnp.float32)
    vmem = pl.BlockSpec(memory_space=pltpu.VMEM)
    hbm = pl.BlockSpec(memory_space=pltpu.HBM)
    dma = pltpu.SemaphoreType.DMA
    solved, fitted = pl.pallas_call(
        functools.partial(calibrate, n_bl, n_ch),
        out_shape=(out, out),
        in_specs=[hbm, hbm, hbm, pl.BlockSpec(memory_space=pltpu.SMEM), hbm],
        out_specs=(vmem, vmem),
        scratch_shapes=[
            pltpu.VMEM(visibilities.shape, visibilities.dtype),
            pltpu.VMEM(sky_model.shape, sky_model.dtype),
            pltpu.VMEM(usable_mask.shape, usable_mask.dtype),
            pltpu.VMEM((2, n_bl, 8 * own, slots), jnp.bfloat16),
            pltpu.VMEM((2, n_bl, 8 * own, slots), jnp.bfloat16),
            pltpu.VMEM((n_bl, 2, slots), jnp.int32),
            pltpu.VMEM((n_bl, STATION_COUNT // 2, 2 * slots), jnp.bfloat16),
            pltpu.VMEM((n_bl, 2 * slots, STATION_COUNT // 2), jnp.bfloat16),
            pltpu.VMEM((n_bl, 12, own, slots), jnp.float32),
            pltpu.VMEM((4, own, STATION_COUNT), jnp.float32),
            pltpu.VMEM((16, owned), jnp.float32),
            pltpu.VMEM((n_ch, 16, owned), jnp.float32),
            dma((4,)), dma((2, n_bl)), dma((2, n_bl)), dma((n_bl,)), dma((n_bl,)),
            dma((n_bl,)), dma((n_bl,)), dma((n_ch,)), dma((n_ch,)),
        ],
        compiler_params=pltpu.CompilerParams(
            collective_id=0, has_side_effects=True, vmem_limit_bytes=40 * 1024 * 1024
        ),
    )(
        pltpu.with_memory_space_constraint(visibilities, pltpu.HBM),
        pltpu.with_memory_space_constraint(sky_model, pltpu.HBM),
        pltpu.with_memory_space_constraint(antenna_pairs, pltpu.HBM),
        tile_counts,
        pltpu.with_memory_space_constraint(usable_mask, pltpu.HBM),
    )
    solved, fitted = pl.pallas_call(
        write_out,
        out_shape=(out, out),
        in_specs=[vmem, vmem],
        out_specs=(hbm, hbm),
        scratch_shapes=[dma((2,))],
    )(solved, fitted)
    shape = (2, 2, channels, owned)
    return solved.reshape(shape), fitted.reshape(shape)


def split_parts(data):
    planes = data.astype(jnp.float32)
    shape_rest = planes.shape[1:]
    return (planes[:4].reshape((2, 2) + shape_rest), planes[4:].reshape((2, 2) + shape_rest))


def poly_basis(channel_total):
    node_values = (2.0 * jnp.arange(channel_total, dtype=jnp.float32) - (channel_total - 1)) / (
        channel_total - 1
    )
    basis_rows = []
    for degree in range(4):
        vector = node_values**degree
        for earlier in basis_rows:
            vector = vector - jnp.sum(vector * earlier) * earlier
        vector = vector / jnp.sqrt(jnp.sum(vector * vector))
        basis_rows.append(vector)
    return jnp.stack(basis_rows)


def contributions(
    model_real_part, model_imaginary, vis_real, vis_imag, first_gain, second_gain, weights
):
    second_real = second_gain[0][None]
    second_imag = second_gain[1][None]
    left_real = model_real_part * second_real + model_imaginary * second_imag
    left_imag = model_imaginary * second_real - model_real_part * second_imag
    first_num_real = jnp.sum(left_real * vis_real + left_imag * vis_imag, axis=1) * weights
    first_num_imag = jnp.sum(left_real * vis_imag - left_imag * vis_real, axis=1) * weights
    first_den = jnp.sum(left_real * left_real + left_imag * left_imag, axis=1) * weights
    first_real = first_gain[0][:, None]
    first_imag = first_gain[1][:, None]
    right_real = model_real_part * first_real - model_imaginary * first_imag
    right_imag = model_real_part * first_imag + model_imaginary * first_real
    second_num_real = jnp.sum(right_real * vis_real + right_imag * vis_imag, axis=0) * weights
    second_num_imag = jnp.sum(right_imag * vis_real - right_real * vis_imag, axis=0) * weights
    second_den = jnp.sum(right_real * right_real + right_imag * right_imag, axis=0) * weights
    return (
        jnp.stack([first_num_real, first_num_imag, first_den]),
        jnp.stack([second_num_real, second_num_imag, second_den]),
    )


def refresh(station_sums, previous):
    divisor = station_sums[2] + damping
    return jnp.stack(
        [
            (station_sums[0] + damping * previous[0]) / divisor,
            (station_sums[1] + damping * previous[1]) / divisor,
        ]
    )


def station_totals(end_first, end_second, first_endpoints, second_ends):
    total_slots = end_first.shape[3]
    flat_first = end_first.reshape(-1, total_slots)
    flat_second = end_second.reshape(-1, total_slots)
    block_rows = math.gcd(total_slots, 1024)
    block_count = total_slots // block_rows
    station_index = jnp.arange(STATION_COUNT, dtype=jnp.int32)

    def add_block(block, total):
        table_first = (first_endpoints[:, None] == station_index[None, :]).astype(jnp.float32)
        table_second = (second_ends[:, None] == station_index[None, :]).astype(jnp.float32)
        return (
            total
            + jnp.dot(
                flat_first, table_first, precision=highest, preferred_element_type=jnp.float32
            )
            + jnp.dot(
                flat_second, table_second, precision=highest, preferred_element_type=jnp.float32
            )
        )

    empty = jnp.zeros((flat_first.shape[0], STATION_COUNT), jnp.float32)
    summed = lax.fori_loop(0, block_count, add_block, empty)
    return summed.reshape(end_first.shape[:3] + (STATION_COUNT,))


def spread(owned_gains):
    return lax.all_gather(owned_gains, "bl", axis=3, tiled=True)


def local(visibilities, sky_model, antenna_pairs, tile_counts, usable_mask):
    vis_real, vis_imag = split_parts(visibilities)
    model_real_part, model_imaginary = split_parts(sky_model)
    channel_local = visibilities.shape[1]
    tile_rows = visibilities.shape[2]
    owner_count = lax.axis_size("bl")
    owned_count = STATION_COUNT // owner_count
    owner_start = lax.axis_index("bl") * owned_count
    live_slots = jnp.arange(tile_rows, dtype=jnp.int32) < tile_counts[0]
    weights = usable_mask.astype(jnp.float32) * live_slots.astype(jnp.float32)[None, :]
    channel_total = channel_local * lax.axis_size("ch")
    poly_rows = lax.dynamic_slice_in_dim(
        poly_basis(channel_total), lax.axis_index("ch") * channel_local, channel_local, 1
    )
    gain_state = jnp.stack(
        [
            jnp.ones((2, channel_local, STATION_COUNT), jnp.float32),
            jnp.zeros((2, channel_local, STATION_COUNT), jnp.float32),
        ]
    )
    solved = gain_state
    for iteration in range(SWEEPS):
        first_gain = jnp.take(gain_state, antenna_pairs[0], axis=3)
        second_gain = jnp.take(gain_state, antenna_pairs[1], axis=3)
        end_first, end_second = contributions(
            model_real_part, model_imaginary, vis_real, vis_imag, first_gain, second_gain, weights
        )
        partial_sums = station_totals(end_first, end_second, antenna_pairs[0], antenna_pairs[1])
        station_sums = lax.psum_scatter(partial_sums, "bl", scatter_dimension=3, tiled=True)
        previous = lax.dynamic_slice_in_dim(gain_state, owner_start, owned_count, 3)
        renewed = refresh(station_sums, previous)
        if iteration == 1:
            renewed = 0.5 * (renewed + previous)
        solved = renewed
        if iteration < SWEEPS - 1:
            gain_state = spread(renewed)
    local_moments = jnp.einsum("kc,rfca->krfa", poly_rows, solved, precision=highest)
    moments = lax.psum(local_moments, "ch")
    fitted = jnp.einsum("kc,krfa->rfca", poly_rows, moments, precision=highest)
    return (solved, fitted)


def solution(mesh):
    n_bl, n_ch = mesh.shape["bl"], mesh.shape["ch"]

    def run(visibilities, sky_model, antenna_pairs, tile_counts, usable_mask):
        channels, slots = usable_mask.shape
        whole_tiles = (
            channels % (n_bl * SUBLANES) == 0
            and slots % LANES == 0
            and STATION_COUNT % (n_bl * LANES) == 0
            and n_bl & (n_bl - 1) == 0
        )
        plan = functools.partial(fused, n_bl, n_ch) if whole_tiles else local
        return plan(visibilities, sky_model, antenna_pairs, tile_counts, usable_mask)

    return jax.shard_map(
        run,
        mesh=mesh,
        in_specs=(
            P(None, "ch", ("grp", "bl")),
            P(None, "ch", ("grp", "bl")),
            P(None, ("grp", "bl")),
            P(("grp", "bl")),
            P("ch", ("grp", "bl")),
        ),
        out_specs=(P(None, None, "ch", ("grp", "bl")), P(None, None, "ch", ("grp", "bl"))),
        check_vma=False,
    )
```

```python
import functools
import math

import jax
import jax.numpy as jnp
import numpy as np
from jax import lax
from jax.experimental import pallas as pl
from jax.experimental.pallas import tpu as pltpu
from jax.sharding import PartitionSpec as P

STATION_COUNT = 512
SWEEPS = 2


damping = 4.0
highest = lax.Precision.HIGHEST
MESH = pl.DeviceIdType.MESH
LANES = 128
SUBLANES = 8


def basis_coefficients(channel_total):
    x = (2.0 * np.arange(channel_total, dtype=np.float64) - (channel_total - 1)) / (channel_total - 1)
    m = np.mean(x**2)
    r = np.sum(x**4) / np.sum(x**2)
    a = [1.0 / np.sqrt(np.sum(v * v)) for v in (np.ones_like(x), x, x**2 - m, x**3 - r * x)]
    return [float(v) for v in a], float(m), float(r)


def split_hi_lo(values):
    hi = values.astype(jnp.bfloat16)
    lo = (values - hi.astype(jnp.float32)).astype(jnp.bfloat16)
    return jnp.concatenate([hi, lo], axis=0)


def exchange_partner(me, k, n):
    partner, bit = 0, 1
    while bit < n:
        mine, other = (me // bit) % 2, (k // bit) % 2
        partner = partner + (mine + other - 2 * mine * other) * bit
        bit *= 2
    return partner


def calibrate(
    n_bl, n_ch, vis_hbm, model_hbm, pairs_hbm, counts_ref, mask_hbm, sol, fit,
    vis_ref, model_ref, mask_ref, outgoing, incoming, pairs_all, onehot, onehot_t, products, state, moments, moments_in,
    load_sem, data_send, data_recv, pair_send, pair_recv, sol_send, sol_recv, mom_send, mom_recv,
):
    me_bl = lax.axis_index("bl")
    me_ch = lax.axis_index("ch")
    channels, slots = mask_ref.shape
    own = channels // n_bl
    stations = state.shape[2]
    owned = stations // n_bl
    half = stations // 2
    f32 = jnp.float32

    loads = [
        pltpu.make_async_copy(pairs_hbm, pairs_all.at[0], load_sem.at[0]),
        pltpu.make_async_copy(vis_hbm, vis_ref, load_sem.at[1]),
        pltpu.make_async_copy(mask_hbm, mask_ref, load_sem.at[2]),
        pltpu.make_async_copy(model_hbm, model_ref, load_sem.at[3]),
    ]
    for load in loads:
        load.start()
    barrier = pltpu.get_barrier_semaphore()
    for k in range(1, n_bl):
        pl.semaphore_signal(barrier, inc=1, device_id={"bl": exchange_partner(me_bl, k, n_bl)}, device_id_type=MESH)
    for k in range(1, n_ch):
        pl.semaphore_signal(barrier, inc=1, device_id={"ch": lax.rem(me_ch + k, n_ch)}, device_id_type=MESH)

    def prepare(part, ref, weights):
        for plane in range(0, 8, 2):
            pair = [ref[j].astype(f32) for j in (plane, plane + 1)]
            if weights is not None:
                pair = [v * weights for v in pair]
            for z in range(n_bl):
                rows = slice(z * own, (z + 1) * own)
                both = jnp.concatenate([pair[0][rows], pair[1][rows]], axis=0)
                outgoing[part, z, plane * own : (plane + 2) * own, :] = both.astype(jnp.bfloat16)

    def data_copy(part, k):
        partner = exchange_partner(me_bl, k, n_bl)
        return pltpu.make_async_remote_copy(
            src_ref=outgoing.at[part, partner], dst_ref=incoming.at[part, k], send_sem=data_send.at[part, k],
            recv_sem=data_recv.at[part, k], device_id={"bl": partner}, device_id_type=MESH,
        )

    odd = lax.rem(me_ch, 2)

    def send(part):
        for i in range(1, n_bl):
            data_copy(part, i + odd * (n_bl - 2 * i)).start()

    loads[0].wait()
    loads[1].wait()
    prepare(0, vis_ref, None)
    pl.semaphore_wait(barrier, n_bl + n_ch - 2)
    pair_copies = {}
    for k in range(1, n_bl):
        pair_copies[k] = pltpu.make_async_remote_copy(
            src_ref=pairs_all.at[0], dst_ref=pairs_all.at[k], send_sem=pair_send.at[k], recv_sem=pair_recv.at[k],
            device_id={"bl": exchange_partner(me_bl, k, n_bl)}, device_id_type=MESH,
        )
        pair_copies[k].start()
    send(0)
    loads[2].wait()
    loads[3].wait()
    live = lax.broadcasted_iota(jnp.int32, (channels, slots), 1) < counts_ref[0]
    prepare(1, model_ref, jnp.where(live, mask_ref[...], 0).astype(f32))
    send(1)

    def end_row(k):
        return jnp.concatenate([pairs_all[k, 0:1, :], pairs_all[k, 1:2, :]], axis=1)

    def is_upper(k):
        return end_row(k) >= half

    def build_onehot(k):
        ends = end_row(k)
        within = jnp.where(ends >= half, ends - half, ends)
        step = 32

        def rows(i, carry):
            base = pl.multiple_of(i * step, step)
            station = lax.broadcasted_iota(jnp.int32, (step, 2 * slots), 0) + base
            onehot[k, pl.ds(base, step), :] = jnp.where(station == within, 1.0, 0.0).astype(jnp.bfloat16)
            return carry

        lax.fori_loop(0, half // step, rows, 0)
        onehot_t[k] = onehot[k].T

    def scatter(k, first, second):
        terms = jnp.concatenate(
            [jnp.concatenate(first, axis=0), jnp.concatenate(second, axis=0)], axis=1
        )
        split = split_hi_lo(terms)
        upper = split * jnp.where(is_upper(k), 1.0, 0.0).astype(jnp.bfloat16)
        both = jnp.concatenate([split - upper, upper], axis=0)
        summed = jnp.dot(both, onehot_t[k], preferred_element_type=f32)
        n = terms.shape[0]
        return summed[:n] + summed[n : 2 * n], summed[2 * n : 3 * n] + summed[3 * n :]

    def add(left, right):
        return right if left is None else (left[0] + right[0], left[1] + right[1])

    def make_products(k, vis_block, model_block):
        vis = vis_block.astype(f32).reshape(8, own, slots)
        model = model_block.astype(f32).reshape(8, own, slots)
        a_re, a_im, b = [], [], []
        for j in range(4):
            vr, vi, mr, mi = vis[j], vis[4 + j], model[j], model[4 + j]
            a_re.append(mr * vr + mi * vi)
            a_im.append(mr * vi - mi * vr)
            b.append(mr * mr + mi * mi)
        for j in range(4):
            products[k, j] = a_re[j]
            products[k, 4 + j] = a_im[j]
            products[k, 8 + j] = b[j]
        first = [a_re[0] + a_re[1], a_re[2] + a_re[3], a_im[0] + a_im[1], a_im[2] + a_im[3], b[0] + b[1], b[2] + b[3]]
        second = [
            a_re[0] + a_re[2], a_re[1] + a_re[3], -(a_im[0] + a_im[2]), -(a_im[1] + a_im[3]), b[0] + b[2], b[1] + b[3],
        ]
        return scatter(k, first, second)

    build_onehot(0)
    total = make_products(0, outgoing[0, me_bl], outgoing[1, me_bl])
    for k in range(1, n_bl):
        pair_copies[k].wait()
        build_onehot(k)
    for k in range(1, n_bl):
        data_copy(0, k).wait_recv()
        data_copy(1, k).wait_recv()
        total = add(total, make_products(k, incoming[0, k], incoming[1, k]))

    feeds = 2 * own
    total = jnp.concatenate(total, axis=1)
    divisor = total[2 * feeds :] + damping
    gain_re = (total[:feeds] + damping) / divisor
    gain_im = total[feeds : 2 * feeds] / divisor
    gains = jnp.concatenate([gain_re, gain_im], axis=0)

    split_gains = split_hi_lo(gains)
    split_gains = jnp.concatenate([split_gains[:, :half], split_gains[:, half:]], axis=0)
    total = None
    for k in range(n_bl):
        both = jnp.dot(split_gains, onehot[k], preferred_element_type=f32)
        n = 2 * feeds
        both = jnp.where(is_upper(k), both[2 * n : 3 * n] + both[3 * n :], both[:n] + both[n : 2 * n])
        at = [[both[i * own : (i + 1) * own, e * slots : (e + 1) * slots] for i in range(4)] for e in range(2)]
        ga, ge = at
        ga_sq = [ga[p] * ga[p] + ga[2 + p] * ga[2 + p] for p in range(2)]
        ge_sq = [ge[p] * ge[p] + ge[2 + p] * ge[2 + p] for p in range(2)]
        a_re = [products[k, j] for j in range(4)]
        a_im = [products[k, 4 + j] for j in range(4)]
        b = [products[k, 8 + j] for j in range(4)]
        first, second = [[], [], []], [[], [], []]
        for p in range(2):
            j0, j1 = 2 * p, 2 * p + 1
            first[0].append(a_re[j0] * ge[0] - a_im[j0] * ge[2] + a_re[j1] * ge[1] - a_im[j1] * ge[3])
            first[1].append(a_re[j0] * ge[2] + a_im[j0] * ge[0] + a_re[j1] * ge[3] + a_im[j1] * ge[1])
            first[2].append(b[j0] * ge_sq[0] + b[j1] * ge_sq[1])
        for q in range(2):
            j0, j1 = q, 2 + q
            second[0].append(a_re[j0] * ga[0] + a_im[j0] * ga[2] + a_re[j1] * ga[1] + a_im[j1] * ga[3])
            second[1].append(a_re[j0] * ga[2] - a_im[j0] * ga[0] + a_re[j1] * ga[3] - a_im[j1] * ga[1])
            second[2].append(b[j0] * ga_sq[0] + b[j1] * ga_sq[1])
        total = add(total, scatter(k, sum(first, []), sum(second, [])))

    total = jnp.concatenate(total, axis=1)
    divisor = total[2 * feeds :] + damping
    for i in range(2):
        previous = gains[i * feeds : (i + 1) * feeds]
        renewed = (total[i * feeds : (i + 1) * feeds] + damping * previous) / divisor
        state[2 * i : 2 * i + 2] = (0.5 * (renewed + previous)).reshape(2, own, stations)

    my_rows = pl.ds(pl.multiple_of(me_bl * own, SUBLANES), own)
    sol_copies = []
    for k in range(n_bl - 1, 0, -1):
        partner = exchange_partner(me_bl, k, n_bl)
        sol_copies.append(
            pltpu.make_async_remote_copy(
                src_ref=state.at[:, :, pl.ds(pl.multiple_of(partner * owned, LANES), owned)],
                dst_ref=sol.at[:, my_rows, :], send_sem=sol_send.at[k], recv_sem=sol_recv.at[k],
                device_id={"bl": partner}, device_id_type=MESH,
            )
        )
        sol_copies[-1].start()
    sol[:, my_rows, :] = state[:, :, pl.ds(pl.multiple_of(me_bl * owned, LANES), owned)]

    channel_total = channels * n_ch
    scale, mean_square, ratio = basis_coefficients(channel_total)
    index = lax.broadcasted_iota(jnp.int32, (channels, owned), 0) + me_ch * channels
    x = (2.0 * index.astype(f32) - (channel_total - 1.0)) * (1.0 / (channel_total - 1.0))
    basis = [
        jnp.full((channels, owned), scale[0], f32),
        scale[1] * x,
        scale[2] * (x * x - mean_square),
        scale[3] * (x * (x * x - ratio)),
    ]
    for copy in sol_copies:
        copy.wait_recv()
    for i in range(4):
        solved = sol[i]
        for d in range(4):
            moments[4 * i + d : 4 * i + d + 1, :] = jnp.sum(basis[d] * solved, axis=0, keepdims=True)
    mom_copies = []
    for k in range(1, n_ch):
        mom_copies.append(
            pltpu.make_async_remote_copy(
                src_ref=moments, dst_ref=moments_in.at[k], send_sem=mom_send.at[k], recv_sem=mom_recv.at[k],
                device_id={"ch": lax.rem(me_ch + k, n_ch)}, device_id_type=MESH,
            )
        )
        mom_copies[-1].start()
    whole = moments[...]
    for k, copy in enumerate(mom_copies, 1):
        copy.wait_recv()
        whole = whole + moments_in[k]
    for i in range(4):
        row = basis[0] * whole[4 * i : 4 * i + 1, :]
        for d in range(1, 4):
            row = row + basis[d] * whole[4 * i + d : 4 * i + d + 1, :]
        fit[i] = row
    sent = [data_copy(part, k) for part in range(2) for k in range(1, n_bl)]
    for copy in sent + sol_copies + mom_copies:
        copy.wait_send()


def write_out(solved_ref, fitted_ref, solved_out, fitted_out, sems):
    copies = [
        pltpu.make_async_copy(solved_ref, solved_out, sems.at[0]),
        pltpu.make_async_copy(fitted_ref, fitted_out, sems.at[1]),
    ]
    for copy in copies:
        copy.start()
    for copy in copies:
        copy.wait()


def fused(n_bl, n_ch, visibilities, sky_model, antenna_pairs, tile_counts, usable_mask):
    channels, slots = usable_mask.shape
    own = channels // n_bl
    owned = STATION_COUNT // n_bl
    out = jax.ShapeDtypeStruct((4, channels, owned), jnp.float32)
    vmem = pl.BlockSpec(memory_space=pltpu.VMEM)
    hbm = pl.BlockSpec(memory_space=pltpu.HBM)
    dma = pltpu.SemaphoreType.DMA
    solved, fitted = pl.pallas_call(
        functools.partial(calibrate, n_bl, n_ch),
        out_shape=(out, out),
        in_specs=[hbm, hbm, hbm, pl.BlockSpec(memory_space=pltpu.SMEM), hbm],
        out_specs=(vmem, vmem),
        scratch_shapes=[
            pltpu.VMEM(visibilities.shape, visibilities.dtype),
            pltpu.VMEM(sky_model.shape, sky_model.dtype),
            pltpu.VMEM(usable_mask.shape, usable_mask.dtype),
            pltpu.VMEM((2, n_bl, 8 * own, slots), jnp.bfloat16),
            pltpu.VMEM((2, n_bl, 8 * own, slots), jnp.bfloat16),
            pltpu.VMEM((n_bl, 2, slots), jnp.int32),
            pltpu.VMEM((n_bl, STATION_COUNT // 2, 2 * slots), jnp.bfloat16),
            pltpu.VMEM((n_bl, 2 * slots, STATION_COUNT // 2), jnp.bfloat16),
            pltpu.VMEM((n_bl, 12, own, slots), jnp.float32),
            pltpu.VMEM((4, own, STATION_COUNT), jnp.float32),
            pltpu.VMEM((16, owned), jnp.float32),
            pltpu.VMEM((n_ch, 16, owned), jnp.float32),
            dma((4,)), dma((2, n_bl)), dma((2, n_bl)), dma((n_bl,)), dma((n_bl,)),
            dma((n_bl,)), dma((n_bl,)), dma((n_ch,)), dma((n_ch,)),
        ],
        compiler_params=pltpu.CompilerParams(
            collective_id=0, has_side_effects=True, vmem_limit_bytes=40 * 1024 * 1024
        ),
    )(
        pltpu.with_memory_space_constraint(visibilities, pltpu.HBM),
        pltpu.with_memory_space_constraint(sky_model, pltpu.HBM),
        pltpu.with_memory_space_constraint(antenna_pairs, pltpu.HBM),
        tile_counts,
        pltpu.with_memory_space_constraint(usable_mask, pltpu.HBM),
    )
    solved, fitted = pl.pallas_call(
        write_out,
        out_shape=(out, out),
        in_specs=[vmem, vmem],
        out_specs=(hbm, hbm),
        scratch_shapes=[dma((2,))],
        compiler_params=pltpu.CompilerParams(vmem_limit_bytes=4 * 1024 * 1024),
    )(solved, fitted)
    shape = (2, 2, channels, owned)
    return solved.reshape(shape), fitted.reshape(shape)


def split_parts(data):
    planes = data.astype(jnp.float32)
    shape_rest = planes.shape[1:]
    return (planes[:4].reshape((2, 2) + shape_rest), planes[4:].reshape((2, 2) + shape_rest))


def poly_basis(channel_total):
    node_values = (2.0 * jnp.arange(channel_total, dtype=jnp.float32) - (channel_total - 1)) / (
        channel_total - 1
    )
    basis_rows = []
    for degree in range(4):
        vector = node_values**degree
        for earlier in basis_rows:
            vector = vector - jnp.sum(vector * earlier) * earlier
        vector = vector / jnp.sqrt(jnp.sum(vector * vector))
        basis_rows.append(vector)
    return jnp.stack(basis_rows)


def contributions(
    model_real_part, model_imaginary, vis_real, vis_imag, first_gain, second_gain, weights
):
    second_real = second_gain[0][None]
    second_imag = second_gain[1][None]
    left_real = model_real_part * second_real + model_imaginary * second_imag
    left_imag = model_imaginary * second_real - model_real_part * second_imag
    first_num_real = jnp.sum(left_real * vis_real + left_imag * vis_imag, axis=1) * weights
    first_num_imag = jnp.sum(left_real * vis_imag - left_imag * vis_real, axis=1) * weights
    first_den = jnp.sum(left_real * left_real + left_imag * left_imag, axis=1) * weights
    first_real = first_gain[0][:, None]
    first_imag = first_gain[1][:, None]
    right_real = model_real_part * first_real - model_imaginary * first_imag
    right_imag = model_real_part * first_imag + model_imaginary * first_real
    second_num_real = jnp.sum(right_real * vis_real + right_imag * vis_imag, axis=0) * weights
    second_num_imag = jnp.sum(right_imag * vis_real - right_real * vis_imag, axis=0) * weights
    second_den = jnp.sum(right_real * right_real + right_imag * right_imag, axis=0) * weights
    return (
        jnp.stack([first_num_real, first_num_imag, first_den]),
        jnp.stack([second_num_real, second_num_imag, second_den]),
    )


def refresh(station_sums, previous):
    divisor = station_sums[2] + damping
    return jnp.stack(
        [
            (station_sums[0] + damping * previous[0]) / divisor,
            (station_sums[1] + damping * previous[1]) / divisor,
        ]
    )


def station_totals(end_first, end_second, first_endpoints, second_ends):
    total_slots = end_first.shape[3]
    flat_first = end_first.reshape(-1, total_slots)
    flat_second = end_second.reshape(-1, total_slots)
    block_rows = math.gcd(total_slots, 1024)
    block_count = total_slots // block_rows
    station_index = jnp.arange(STATION_COUNT, dtype=jnp.int32)

    def add_block(block, total):
        table_first = (first_endpoints[:, None] == station_index[None, :]).astype(jnp.float32)
        table_second = (second_ends[:, None] == station_index[None, :]).astype(jnp.float32)
        return (
            total
            + jnp.dot(
                flat_first, table_first, precision=highest, preferred_element_type=jnp.float32
            )
            + jnp.dot(
                flat_second, table_second, precision=highest, preferred_element_type=jnp.float32
            )
        )

    empty = jnp.zeros((flat_first.shape[0], STATION_COUNT), jnp.float32)
    summed = lax.fori_loop(0, block_count, add_block, empty)
    return summed.reshape(end_first.shape[:3] + (STATION_COUNT,))


def spread(owned_gains):
    return lax.all_gather(owned_gains, "bl", axis=3, tiled=True)


def local(visibilities, sky_model, antenna_pairs, tile_counts, usable_mask):
    vis_real, vis_imag = split_parts(visibilities)
    model_real_part, model_imaginary = split_parts(sky_model)
    channel_local = visibilities.shape[1]
    tile_rows = visibilities.shape[2]
    owner_count = lax.axis_size("bl")
    owned_count = STATION_COUNT // owner_count
    owner_start = lax.axis_index("bl") * owned_count
    live_slots = jnp.arange(tile_rows, dtype=jnp.int32) < tile_counts[0]
    weights = usable_mask.astype(jnp.float32) * live_slots.astype(jnp.float32)[None, :]
    channel_total = channel_local * lax.axis_size("ch")
    poly_rows = lax.dynamic_slice_in_dim(
        poly_basis(channel_total), lax.axis_index("ch") * channel_local, channel_local, 1
    )
    gain_state = jnp.stack(
        [
            jnp.ones((2, channel_local, STATION_COUNT), jnp.float32),
            jnp.zeros((2, channel_local, STATION_COUNT), jnp.float32),
        ]
    )
    solved = gain_state
    for iteration in range(SWEEPS):
        first_gain = jnp.take(gain_state, antenna_pairs[0], axis=3)
        second_gain = jnp.take(gain_state, antenna_pairs[1], axis=3)
        end_first, end_second = contributions(
            model_real_part, model_imaginary, vis_real, vis_imag, first_gain, second_gain, weights
        )
        partial_sums = station_totals(end_first, end_second, antenna_pairs[0], antenna_pairs[1])
        station_sums = lax.psum_scatter(partial_sums, "bl", scatter_dimension=3, tiled=True)
        previous = lax.dynamic_slice_in_dim(gain_state, owner_start, owned_count, 3)
        renewed = refresh(station_sums, previous)
        if iteration == 1:
            renewed = 0.5 * (renewed + previous)
        solved = renewed
        if iteration < SWEEPS - 1:
            gain_state = spread(renewed)
    local_moments = jnp.einsum("kc,rfca->krfa", poly_rows, solved, precision=highest)
    moments = lax.psum(local_moments, "ch")
    fitted = jnp.einsum("kc,krfa->rfca", poly_rows, moments, precision=highest)
    return (solved, fitted)


def solution(mesh):
    n_bl, n_ch = mesh.shape["bl"], mesh.shape["ch"]

    def run(visibilities, sky_model, antenna_pairs, tile_counts, usable_mask):
        channels, slots = usable_mask.shape
        whole_tiles = (
            channels % (n_bl * SUBLANES) == 0
            and slots % LANES == 0
            and STATION_COUNT % (n_bl * LANES) == 0
            and n_bl & (n_bl - 1) == 0
        )
        plan = functools.partial(fused, n_bl, n_ch) if whole_tiles else local
        return plan(visibilities, sky_model, antenna_pairs, tile_counts, usable_mask)

    return jax.shard_map(
        run,
        mesh=mesh,
        in_specs=(
            P(None, "ch", ("grp", "bl")),
            P(None, "ch", ("grp", "bl")),
            P(None, ("grp", "bl")),
            P(("grp", "bl")),
            P("ch", ("grp", "bl")),
        ),
        out_specs=(P(None, None, "ch", ("grp", "bl")), P(None, None, "ch", ("grp", "bl"))),
        check_vma=False,
    )
```

```python
import functools
import math

import jax
import jax.numpy as jnp
import numpy as np
from jax import lax
from jax.experimental import pallas as pl
from jax.experimental.pallas import tpu as pltpu
from jax.sharding import PartitionSpec as P

STATION_COUNT = 512
SWEEPS = 2


damping = 4.0
highest = lax.Precision.HIGHEST
MESH = pl.DeviceIdType.MESH
LANES = 128
SUBLANES = 8


def basis_coefficients(channel_total):
    x = (2.0 * np.arange(channel_total, dtype=np.float64) - (channel_total - 1)) / (channel_total - 1)
    m = np.mean(x**2)
    r = np.sum(x**4) / np.sum(x**2)
    a = [1.0 / np.sqrt(np.sum(v * v)) for v in (np.ones_like(x), x, x**2 - m, x**3 - r * x)]
    return [float(v) for v in a], float(m), float(r)


def split_hi_lo(values):
    hi = values.astype(jnp.bfloat16).astype(jnp.float32)
    return jnp.concatenate([hi, values - hi], axis=0).astype(jnp.bfloat16)


def exchange_partner(me, k, n):
    partner, bit = 0, 1
    while bit < n:
        mine, other = (me // bit) % 2, (k // bit) % 2
        partner = partner + (mine + other - 2 * mine * other) * bit
        bit *= 2
    return partner


def calibrate(
    n_bl, n_ch, vis_hbm, model_hbm, pairs_hbm, counts_ref, mask_hbm, sol, fit,
    vis_ref, model_ref, mask_ref, outgoing, incoming, pairs_all, onehot, onehot_t, products, state, moments, moments_in,
    load_sem, data_send, data_recv, pair_send, pair_recv, sol_send, sol_recv, mom_send, mom_recv,
):
    me_bl = lax.axis_index("bl")
    me_ch = lax.axis_index("ch")
    channels, slots = mask_ref.shape
    own = channels // n_bl
    stations = state.shape[2]
    owned = stations // n_bl
    half = stations // 2
    f32 = jnp.float32

    loads = [
        pltpu.make_async_copy(pairs_hbm, pairs_all.at[0], load_sem.at[0]),
        pltpu.make_async_copy(vis_hbm, vis_ref, load_sem.at[1]),
        pltpu.make_async_copy(mask_hbm, mask_ref, load_sem.at[2]),
        pltpu.make_async_copy(model_hbm, model_ref, load_sem.at[3]),
    ]
    for load in loads:
        load.start()
    barrier = pltpu.get_barrier_semaphore()
    for k in range(1, n_bl):
        pl.semaphore_signal(barrier, inc=1, device_id={"bl": exchange_partner(me_bl, k, n_bl)}, device_id_type=MESH)
    for k in range(1, n_ch):
        pl.semaphore_signal(barrier, inc=1, device_id={"ch": lax.rem(me_ch + k, n_ch)}, device_id_type=MESH)

    group = own // 2

    def prepare(h, weights):
        for part, ref in enumerate((vis_ref, model_ref)):
            for plane in range(0, 8, 4):
                four = [ref[j].astype(f32) for j in range(plane, plane + 4)]
                if part == 1:
                    four = [v * weights for v in four]
                base = (4 * part + plane // 2) * own
                for z in range(n_bl):
                    rows = slice(z * own + h * group, z * own + (h + 1) * group)
                    block = jnp.concatenate([v[rows] for v in four], axis=0)
                    outgoing[h, z, base : base + 2 * own, :] = block.astype(jnp.bfloat16)

    def data_copy(part, k):
        partner = exchange_partner(me_bl, k, n_bl)
        return pltpu.make_async_remote_copy(
            src_ref=outgoing.at[part, partner], dst_ref=incoming.at[part, k], send_sem=data_send.at[part, k],
            recv_sem=data_recv.at[part, k], device_id={"bl": partner}, device_id_type=MESH,
        )

    odd = lax.rem(me_ch, 2)

    def send(part):
        for i in range(1, n_bl):
            data_copy(part, i + odd * (n_bl - 2 * i)).start()

    for load in loads:
        load.wait()
    live = lax.broadcasted_iota(jnp.int32, (channels, slots), 1) < counts_ref[0]
    weights = jnp.where(live, mask_ref[...], 0).astype(f32)
    prepare(0, weights)
    pl.semaphore_wait(barrier, n_bl + n_ch - 2)
    pair_copies = {}
    for k in range(1, n_bl):
        pair_copies[k] = pltpu.make_async_remote_copy(
            src_ref=pairs_all.at[0], dst_ref=pairs_all.at[k], send_sem=pair_send.at[k], recv_sem=pair_recv.at[k],
            device_id={"bl": exchange_partner(me_bl, k, n_bl)}, device_id_type=MESH,
        )
        pair_copies[k].start()
    send(0)
    prepare(1, weights)
    send(1)

    def end_row(k):
        return jnp.concatenate([pairs_all[k, 0:1, :], pairs_all[k, 1:2, :]], axis=1)

    def is_upper(k, e):
        return pairs_all[k, e : e + 1, :] >= half

    def build_onehot(k):
        ends = end_row(k)
        within = jnp.where(ends >= half, ends - half, ends)
        step = 32

        def rows(i, carry):
            base = pl.multiple_of(i * step, step)
            station = lax.broadcasted_iota(jnp.int32, (step, 2 * slots), 0) + base
            onehot[k, pl.ds(base, step), :] = jnp.where(station == within, 1.0, 0.0).astype(jnp.bfloat16)
            return carry

        lax.fori_loop(0, half // step, rows, 0)
        onehot_t[k] = onehot[k].T

    def scatter(k, e, blocks):
        split = split_hi_lo(jnp.concatenate(blocks, axis=0))
        upper = split * jnp.where(is_upper(k, e), 1.0, 0.0).astype(jnp.bfloat16)
        both = jnp.concatenate([split - upper, upper], axis=0)
        summed = jnp.dot(both, onehot_t[k, e * slots : (e + 1) * slots, :], preferred_element_type=f32)
        n = len(blocks) * own
        return jnp.concatenate([summed[:n] + summed[n : 2 * n], summed[2 * n : 3 * n] + summed[3 * n :]], axis=1)

    def gather(k, e, split_gains):
        both = jnp.dot(split_gains, onehot[k, :, e * slots : (e + 1) * slots], preferred_element_type=f32)
        n = split_gains.shape[0] // 4
        both = jnp.where(is_upper(k, e), both[2 * n : 3 * n] + both[3 * n :], both[:n] + both[n : 2 * n])
        return both.reshape(n // own, own, slots)

    def split_halves(blocks):
        split = split_hi_lo(jnp.concatenate(blocks, axis=0))
        return jnp.concatenate([split[:, :half], split[:, half:]], axis=0)

    def make_products(h, k, block):
        block = block.astype(f32).reshape(8, own, slots)
        a_re, a_im, b = [], [], []
        for p in range(2):
            vr, vi, mr, mi = block[p], block[2 + p], block[4 + p], block[6 + p]
            a_re.append(mr * vr + mi * vi)
            a_im.append(mr * vi - mi * vr)
            b.append(mr * mr + mi * mi)
            products[h, k, p] = a_re[p]
            products[h, k, 2 + p] = a_im[p]
            products[h, k, 4 + p] = b[p]
        first = scatter(k, 0, a_re + a_im + b)
        second = scatter(k, 1, [a_re[0] + a_re[1], -(a_im[0] + a_im[1]), b[0] + b[1]])
        return first, second

    def add(left, right):
        return right if left is None else (left[0] + right[0], left[1] + right[1])

    def station_sums(total):
        first = total[0].reshape(6, own, stations)
        second = total[1].reshape(3, own, stations)
        sums = []
        for i in range(3):
            feeds = [first[2 * i + p][:group] + first[2 * i + p][group:] for p in range(2)]
            sums.append(jnp.concatenate(feeds, axis=0) + second[i])
        return sums

    def solve(h, total):
        num_re, num_im, den = station_sums(total)
        gain_re = (num_re + damping) / (den + damping)
        gain_im = num_im / (den + damping)
        for_second = split_halves([gain_re, gain_im])
        twice = [jnp.concatenate([g[f * group : (f + 1) * group]] * 2, axis=0) for g in (gain_re, gain_im) for f in range(2)]
        for_first = split_halves(twice)
        total = None
        for k in range(n_bl):
            ga = gather(k, 0, for_first)
            ge_re, ge_im = gather(k, 1, for_second)
            ge_sq = ge_re * ge_re + ge_im * ge_im
            first, second = [[], [], []], [[], [], []]
            for p in range(2):
                a_re, a_im, b = products[h, k, p], products[h, k, 2 + p], products[h, k, 4 + p]
                ga_re, ga_im = ga[p], ga[2 + p]
                first[0].append(a_re * ge_re - a_im * ge_im)
                first[1].append(a_re * ge_im + a_im * ge_re)
                first[2].append(b * ge_sq)
                second[0].append(a_re * ga_re + a_im * ga_im)
                second[1].append(a_re * ga_im - a_im * ga_re)
                second[2].append(b * (ga_re * ga_re + ga_im * ga_im))
            part = scatter(k, 0, sum(first, [])), scatter(k, 1, [v[0] + v[1] for v in second])
            total = add(total, part)
        num_re, num_im, den = station_sums(total)
        for i, (num, previous) in enumerate(((num_re, gain_re), (num_im, gain_im))):
            solved = 0.5 * ((num + damping * previous) / (den + damping) + previous)
            for f in range(2):
                state[2 * i + f, h * group : (h + 1) * group, :] = solved[f * group : (f + 1) * group]

    build_onehot(0)
    totals = [make_products(h, 0, outgoing[h, me_bl]) for h in range(2)]
    for k in range(1, n_bl):
        pair_copies[k].wait()
        build_onehot(k)
    for h in range(2):
        total = totals[h]
        for k in range(1, n_bl):
            data_copy(h, k).wait_recv()
            total = add(total, make_products(h, k, incoming[h, k]))
        solve(h, total)

    my_rows = pl.ds(pl.multiple_of(me_bl * own, SUBLANES), own)
    sol_copies = []
    for k in range(n_bl - 1, 0, -1):
        partner = exchange_partner(me_bl, k, n_bl)
        sol_copies.append(
            pltpu.make_async_remote_copy(
                src_ref=state.at[:, :, pl.ds(pl.multiple_of(partner * owned, LANES), owned)],
                dst_ref=sol.at[:, my_rows, :], send_sem=sol_send.at[k], recv_sem=sol_recv.at[k],
                device_id={"bl": partner}, device_id_type=MESH,
            )
        )
        sol_copies[-1].start()
    sol[:, my_rows, :] = state[:, :, pl.ds(pl.multiple_of(me_bl * owned, LANES), owned)]

    channel_total = channels * n_ch
    scale, mean_square, ratio = basis_coefficients(channel_total)
    index = lax.broadcasted_iota(jnp.int32, (channels, owned), 0) + me_ch * channels
    x = (2.0 * index.astype(f32) - (channel_total - 1.0)) * (1.0 / (channel_total - 1.0))
    basis = [
        jnp.full((channels, owned), scale[0], f32),
        scale[1] * x,
        scale[2] * (x * x - mean_square),
        scale[3] * (x * (x * x - ratio)),
    ]
    for copy in sol_copies:
        copy.wait_recv()
    for i in range(4):
        solved = sol[i]
        for d in range(4):
            moments[4 * i + d : 4 * i + d + 1, :] = jnp.sum(basis[d] * solved, axis=0, keepdims=True)
    mom_copies = []
    for k in range(1, n_ch):
        mom_copies.append(
            pltpu.make_async_remote_copy(
                src_ref=moments, dst_ref=moments_in.at[k], send_sem=mom_send.at[k], recv_sem=mom_recv.at[k],
                device_id={"ch": lax.rem(me_ch + k, n_ch)}, device_id_type=MESH,
            )
        )
        mom_copies[-1].start()
    whole = moments[...]
    for k, copy in enumerate(mom_copies, 1):
        copy.wait_recv()
        whole = whole + moments_in[k]
    for i in range(4):
        row = basis[0] * whole[4 * i : 4 * i + 1, :]
        for d in range(1, 4):
            row = row + basis[d] * whole[4 * i + d : 4 * i + d + 1, :]
        fit[i] = row
    sent = [data_copy(part, k) for part in range(2) for k in range(1, n_bl)]
    for copy in sent + sol_copies + mom_copies:
        copy.wait_send()


def write_out(solved_ref, fitted_ref, solved_out, fitted_out, sems):
    copies = [
        pltpu.make_async_copy(solved_ref, solved_out, sems.at[0]),
        pltpu.make_async_copy(fitted_ref, fitted_out, sems.at[1]),
    ]
    for copy in copies:
        copy.start()
    for copy in copies:
        copy.wait()


def fused(n_bl, n_ch, visibilities, sky_model, antenna_pairs, tile_counts, usable_mask):
    channels, slots = usable_mask.shape
    own = channels // n_bl
    owned = STATION_COUNT // n_bl
    out = jax.ShapeDtypeStruct((4, channels, owned), jnp.float32)
    vmem = pl.BlockSpec(memory_space=pltpu.VMEM)
    hbm = pl.BlockSpec(memory_space=pltpu.HBM)
    dma = pltpu.SemaphoreType.DMA
    solved, fitted = pl.pallas_call(
        functools.partial(calibrate, n_bl, n_ch),
        out_shape=(out, out),
        in_specs=[hbm, hbm, hbm, pl.BlockSpec(memory_space=pltpu.SMEM), hbm],
        out_specs=(vmem, vmem),
        scratch_shapes=[
            pltpu.VMEM(visibilities.shape, visibilities.dtype),
            pltpu.VMEM(sky_model.shape, sky_model.dtype),
            pltpu.VMEM(usable_mask.shape, usable_mask.dtype),
            pltpu.VMEM((2, n_bl, 8 * own, slots), jnp.bfloat16),
            pltpu.VMEM((2, n_bl, 8 * own, slots), jnp.bfloat16),
            pltpu.VMEM((n_bl, 2, slots), jnp.int32),
            pltpu.VMEM((n_bl, STATION_COUNT // 2, 2 * slots), jnp.bfloat16),
            pltpu.VMEM((n_bl, 2 * slots, STATION_COUNT // 2), jnp.bfloat16),
            pltpu.VMEM((2, n_bl, 6, own, slots), jnp.float32),
            pltpu.VMEM((4, own, STATION_COUNT), jnp.float32),
            pltpu.VMEM((16, owned), jnp.float32),
            pltpu.VMEM((n_ch, 16, owned), jnp.float32),
            dma((4,)), dma((2, n_bl)), dma((2, n_bl)), dma((n_bl,)), dma((n_bl,)),
            dma((n_bl,)), dma((n_bl,)), dma((n_ch,)), dma((n_ch,)),
        ],
        compiler_params=pltpu.CompilerParams(
            collective_id=0, has_side_effects=True, vmem_limit_bytes=40 * 1024 * 1024
        ),
    )(
        pltpu.with_memory_space_constraint(visibilities, pltpu.HBM),
        pltpu.with_memory_space_constraint(sky_model, pltpu.HBM),
        pltpu.with_memory_space_constraint(antenna_pairs, pltpu.HBM),
        tile_counts,
        pltpu.with_memory_space_constraint(usable_mask, pltpu.HBM),
    )
    solved, fitted = pl.pallas_call(
        write_out,
        out_shape=(out, out),
        in_specs=[vmem, vmem],
        out_specs=(hbm, hbm),
        scratch_shapes=[dma((2,))],
        compiler_params=pltpu.CompilerParams(vmem_limit_bytes=4 * 1024 * 1024),
    )(solved, fitted)
    shape = (2, 2, channels, owned)
    return solved.reshape(shape), fitted.reshape(shape)


def split_parts(data):
    planes = data.astype(jnp.float32)
    shape_rest = planes.shape[1:]
    return (planes[:4].reshape((2, 2) + shape_rest), planes[4:].reshape((2, 2) + shape_rest))


def poly_basis(channel_total):
    node_values = (2.0 * jnp.arange(channel_total, dtype=jnp.float32) - (channel_total - 1)) / (
        channel_total - 1
    )
    basis_rows = []
    for degree in range(4):
        vector = node_values**degree
        for earlier in basis_rows:
            vector = vector - jnp.sum(vector * earlier) * earlier
        vector = vector / jnp.sqrt(jnp.sum(vector * vector))
        basis_rows.append(vector)
    return jnp.stack(basis_rows)


def contributions(
    model_real_part, model_imaginary, vis_real, vis_imag, first_gain, second_gain, weights
):
    second_real = second_gain[0][None]
    second_imag = second_gain[1][None]
    left_real = model_real_part * second_real + model_imaginary * second_imag
    left_imag = model_imaginary * second_real - model_real_part * second_imag
    first_num_real = jnp.sum(left_real * vis_real + left_imag * vis_imag, axis=1) * weights
    first_num_imag = jnp.sum(left_real * vis_imag - left_imag * vis_real, axis=1) * weights
    first_den = jnp.sum(left_real * left_real + left_imag * left_imag, axis=1) * weights
    first_real = first_gain[0][:, None]
    first_imag = first_gain[1][:, None]
    right_real = model_real_part * first_real - model_imaginary * first_imag
    right_imag = model_real_part * first_imag + model_imaginary * first_real
    second_num_real = jnp.sum(right_real * vis_real + right_imag * vis_imag, axis=0) * weights
    second_num_imag = jnp.sum(right_imag * vis_real - right_real * vis_imag, axis=0) * weights
    second_den = jnp.sum(right_real * right_real + right_imag * right_imag, axis=0) * weights
    return (
        jnp.stack([first_num_real, first_num_imag, first_den]),
        jnp.stack([second_num_real, second_num_imag, second_den]),
    )


def refresh(station_sums, previous):
    divisor = station_sums[2] + damping
    return jnp.stack(
        [
            (station_sums[0] + damping * previous[0]) / divisor,
            (station_sums[1] + damping * previous[1]) / divisor,
        ]
    )


def station_totals(end_first, end_second, first_endpoints, second_ends):
    total_slots = end_first.shape[3]
    flat_first = end_first.reshape(-1, total_slots)
    flat_second = end_second.reshape(-1, total_slots)
    block_rows = math.gcd(total_slots, 1024)
    block_count = total_slots // block_rows
    station_index = jnp.arange(STATION_COUNT, dtype=jnp.int32)

    def add_block(block, total):
        table_first = (first_endpoints[:, None] == station_index[None, :]).astype(jnp.float32)
        table_second = (second_ends[:, None] == station_index[None, :]).astype(jnp.float32)
        return (
            total
            + jnp.dot(
                flat_first, table_first, precision=highest, preferred_element_type=jnp.float32
            )
            + jnp.dot(
                flat_second, table_second, precision=highest, preferred_element_type=jnp.float32
            )
        )

    empty = jnp.zeros((flat_first.shape[0], STATION_COUNT), jnp.float32)
    summed = lax.fori_loop(0, block_count, add_block, empty)
    return summed.reshape(end_first.shape[:3] + (STATION_COUNT,))


def spread(owned_gains):
    return lax.all_gather(owned_gains, "bl", axis=3, tiled=True)


def local(visibilities, sky_model, antenna_pairs, tile_counts, usable_mask):
    vis_real, vis_imag = split_parts(visibilities)
    model_real_part, model_imaginary = split_parts(sky_model)
    channel_local = visibilities.shape[1]
    tile_rows = visibilities.shape[2]
    owner_count = lax.axis_size("bl")
    owned_count = STATION_COUNT // owner_count
    owner_start = lax.axis_index("bl") * owned_count
    live_slots = jnp.arange(tile_rows, dtype=jnp.int32) < tile_counts[0]
    weights = usable_mask.astype(jnp.float32) * live_slots.astype(jnp.float32)[None, :]
    channel_total = channel_local * lax.axis_size("ch")
    poly_rows = lax.dynamic_slice_in_dim(
        poly_basis(channel_total), lax.axis_index("ch") * channel_local, channel_local, 1
    )
    gain_state = jnp.stack(
        [
            jnp.ones((2, channel_local, STATION_COUNT), jnp.float32),
            jnp.zeros((2, channel_local, STATION_COUNT), jnp.float32),
        ]
    )
    solved = gain_state
    for iteration in range(SWEEPS):
        first_gain = jnp.take(gain_state, antenna_pairs[0], axis=3)
        second_gain = jnp.take(gain_state, antenna_pairs[1], axis=3)
        end_first, end_second = contributions(
            model_real_part, model_imaginary, vis_real, vis_imag, first_gain, second_gain, weights
        )
        partial_sums = station_totals(end_first, end_second, antenna_pairs[0], antenna_pairs[1])
        station_sums = lax.psum_scatter(partial_sums, "bl", scatter_dimension=3, tiled=True)
        previous = lax.dynamic_slice_in_dim(gain_state, owner_start, owned_count, 3)
        renewed = refresh(station_sums, previous)
        if iteration == 1:
            renewed = 0.5 * (renewed + previous)
        solved = renewed
        if iteration < SWEEPS - 1:
            gain_state = spread(renewed)
    local_moments = jnp.einsum("kc,rfca->krfa", poly_rows, solved, precision=highest)
    moments = lax.psum(local_moments, "ch")
    fitted = jnp.einsum("kc,krfa->rfca", poly_rows, moments, precision=highest)
    return (solved, fitted)


def solution(mesh):
    n_bl, n_ch = mesh.shape["bl"], mesh.shape["ch"]

    def run(visibilities, sky_model, antenna_pairs, tile_counts, usable_mask):
        channels, slots = usable_mask.shape
        whole_tiles = (
            channels % (n_bl * SUBLANES) == 0
            and slots % LANES == 0
            and STATION_COUNT % (n_bl * LANES) == 0
            and n_bl & (n_bl - 1) == 0
        )
        plan = functools.partial(fused, n_bl, n_ch) if whole_tiles else local
        return plan(visibilities, sky_model, antenna_pairs, tile_counts, usable_mask)

    return jax.shard_map(
        run,
        mesh=mesh,
        in_specs=(
            P(None, "ch", ("grp", "bl")),
            P(None, "ch", ("grp", "bl")),
            P(None, ("grp", "bl")),
            P(("grp", "bl")),
            P("ch", ("grp", "bl")),
        ),
        out_specs=(P(None, None, "ch", ("grp", "bl")), P(None, None, "ch", ("grp", "bl"))),
        check_vma=False,
    )
```

```python
import functools
import math

import jax
import jax.numpy as jnp
import numpy as np
from jax import lax
from jax.experimental import pallas as pl
from jax.experimental.pallas import tpu as pltpu
from jax.sharding import PartitionSpec as P

STATION_COUNT = 512
SWEEPS = 2


damping = 4.0
highest = lax.Precision.HIGHEST
MESH = pl.DeviceIdType.MESH
LANES = 128
SUBLANES = 8


def basis_coefficients(channel_total):
    x = (2.0 * np.arange(channel_total, dtype=np.float64) - (channel_total - 1)) / (channel_total - 1)
    m = np.mean(x**2)
    r = np.sum(x**4) / np.sum(x**2)
    a = [1.0 / np.sqrt(np.sum(v * v)) for v in (np.ones_like(x), x, x**2 - m, x**3 - r * x)]
    return [float(v) for v in a], float(m), float(r)


def split_hi_lo(values):
    hi = values.astype(jnp.bfloat16).astype(jnp.float32)
    return jnp.concatenate([hi, values - hi], axis=0).astype(jnp.bfloat16)


def exchange_partner(me, k, n):
    partner, bit = 0, 1
    while bit < n:
        mine, other = (me // bit) % 2, (k // bit) % 2
        partner = partner + (mine + other - 2 * mine * other) * bit
        bit *= 2
    return partner


def calibrate(
    n_bl, n_ch, vis_hbm, model_hbm, pairs_hbm, counts_ref, mask_hbm, sol, fit,
    vis_ref, model_ref, mask_ref, outgoing, incoming, pairs_all, onehot, onehot_t, products, state, moments, moments_in,
    load_sem, data_send, data_recv, pair_send, pair_recv, sol_send, sol_recv, mom_send, mom_recv,
):
    me_bl = lax.axis_index("bl")
    me_ch = lax.axis_index("ch")
    channels, slots = mask_ref.shape
    own = channels // n_bl
    stations = state.shape[2]
    owned = stations // n_bl
    half = stations // 2
    f32 = jnp.float32

    loads = [
        pltpu.make_async_copy(pairs_hbm, pairs_all.at[0], load_sem.at[0]),
        pltpu.make_async_copy(vis_hbm, vis_ref, load_sem.at[1]),
        pltpu.make_async_copy(mask_hbm, mask_ref, load_sem.at[2]),
        pltpu.make_async_copy(model_hbm, model_ref, load_sem.at[3]),
    ]
    for load in loads:
        load.start()
    barrier = pltpu.get_barrier_semaphore()
    for k in range(1, n_bl):
        pl.semaphore_signal(barrier, inc=1, device_id={"bl": exchange_partner(me_bl, k, n_bl)}, device_id_type=MESH)
    for k in range(1, n_ch):
        pl.semaphore_signal(barrier, inc=1, device_id={"ch": lax.rem(me_ch + k, n_ch)}, device_id_type=MESH)

    group = own // 2

    def prepare(h, weights):
        for part, ref in enumerate((vis_ref, model_ref)):
            for plane in range(0, 8, 4):
                four = [ref[j].astype(f32) for j in range(plane, plane + 4)]
                if part == 1:
                    four = [v * weights for v in four]
                base = (4 * part + plane // 2) * own
                for z in range(n_bl):
                    rows = slice(z * own + h * group, z * own + (h + 1) * group)
                    block = jnp.concatenate([v[rows] for v in four], axis=0)
                    outgoing[h, z, base : base + 2 * own, :] = block.astype(jnp.bfloat16)

    def data_copy(part, k):
        partner = exchange_partner(me_bl, k, n_bl)
        return pltpu.make_async_remote_copy(
            src_ref=outgoing.at[part, partner], dst_ref=incoming.at[part, k], send_sem=data_send.at[part, k],
            recv_sem=data_recv.at[part, k], device_id={"bl": partner}, device_id_type=MESH,
        )

    odd = lax.rem(me_ch, 2)

    def send(h):
        for i in range(1, n_bl):
            k = i + odd * (n_bl - 2 * i)
            if h:
                data_copy(h - 1, k).wait_send()
            data_copy(h, k).start()

    for load in loads:
        load.wait()
    live = lax.broadcasted_iota(jnp.int32, (channels, slots), 1) < counts_ref[0]
    weights = jnp.where(live, mask_ref[...], 0).astype(f32)
    prepare(0, weights)
    pl.semaphore_wait(barrier, n_bl + n_ch - 2)
    pair_copies = {}
    for k in range(1, n_bl):
        pair_copies[k] = pltpu.make_async_remote_copy(
            src_ref=pairs_all.at[0], dst_ref=pairs_all.at[k], send_sem=pair_send.at[k], recv_sem=pair_recv.at[k],
            device_id={"bl": exchange_partner(me_bl, k, n_bl)}, device_id_type=MESH,
        )
        pair_copies[k].start()
    send(0)
    prepare(1, weights)

    def end_row(k):
        return jnp.concatenate([pairs_all[k, 0:1, :], pairs_all[k, 1:2, :]], axis=1)

    def is_upper(k, e):
        return pairs_all[k, e : e + 1, :] >= half

    def build_onehot(k):
        ends = end_row(k)
        within = jnp.where(ends >= half, ends - half, ends)
        step = 32

        def rows(i, carry):
            base = pl.multiple_of(i * step, step)
            station = lax.broadcasted_iota(jnp.int32, (step, 2 * slots), 0) + base
            onehot[k, pl.ds(base, step), :] = jnp.where(station == within, 1.0, 0.0).astype(jnp.bfloat16)
            return carry

        lax.fori_loop(0, half // step, rows, 0)
        onehot_t[k] = onehot[k].T

    def scatter(k, e, blocks):
        split = split_hi_lo(jnp.concatenate(blocks, axis=0))
        upper = split * jnp.where(is_upper(k, e), 1.0, 0.0).astype(jnp.bfloat16)
        both = jnp.concatenate([split - upper, upper], axis=0)
        summed = jnp.dot(both, onehot_t[k, e * slots : (e + 1) * slots, :], preferred_element_type=f32)
        n = len(blocks) * own
        return jnp.concatenate([summed[:n] + summed[n : 2 * n], summed[2 * n : 3 * n] + summed[3 * n :]], axis=1)

    def gather(k, e, split_gains):
        both = jnp.dot(split_gains, onehot[k, :, e * slots : (e + 1) * slots], preferred_element_type=f32)
        n = split_gains.shape[0] // 4
        both = jnp.where(is_upper(k, e), both[2 * n : 3 * n] + both[3 * n :], both[:n] + both[n : 2 * n])
        return both.reshape(n // own, own, slots)

    def split_halves(blocks):
        split = split_hi_lo(jnp.concatenate(blocks, axis=0))
        return jnp.concatenate([split[:, :half], split[:, half:]], axis=0)

    def make_products(h, k, block):
        block = block.astype(f32).reshape(8, own, slots)
        a_re, a_im, b = [], [], []
        for p in range(2):
            vr, vi, mr, mi = block[p], block[2 + p], block[4 + p], block[6 + p]
            a_re.append(mr * vr + mi * vi)
            a_im.append(mr * vi - mi * vr)
            b.append(mr * mr + mi * mi)
            products[h, k, p] = a_re[p]
            products[h, k, 2 + p] = a_im[p]
            products[h, k, 4 + p] = b[p]
        first = scatter(k, 0, a_re + a_im + b)
        second = scatter(k, 1, [a_re[0] + a_re[1], -(a_im[0] + a_im[1]), b[0] + b[1]])
        return first, second

    def add(left, right):
        return right if left is None else (left[0] + right[0], left[1] + right[1])

    def station_sums(total):
        first = total[0].reshape(6, own, stations)
        second = total[1].reshape(3, own, stations)
        sums = []
        for i in range(3):
            feeds = [first[2 * i + p][:group] + first[2 * i + p][group:] for p in range(2)]
            sums.append(jnp.concatenate(feeds, axis=0) + second[i])
        return sums

    def solve(h, total):
        num_re, num_im, den = station_sums(total)
        gain_re = (num_re + damping) / (den + damping)
        gain_im = num_im / (den + damping)
        for_second = split_halves([gain_re, gain_im])
        twice = [jnp.concatenate([g[f * group : (f + 1) * group]] * 2, axis=0) for g in (gain_re, gain_im) for f in range(2)]
        for_first = split_halves(twice)
        total = None
        for k in range(n_bl):
            ga = gather(k, 0, for_first)
            ge_re, ge_im = gather(k, 1, for_second)
            ge_sq = ge_re * ge_re + ge_im * ge_im
            first, second = [[], [], []], [[], [], []]
            for p in range(2):
                a_re, a_im, b = products[h, k, p], products[h, k, 2 + p], products[h, k, 4 + p]
                ga_re, ga_im = ga[p], ga[2 + p]
                first[0].append(a_re * ge_re - a_im * ge_im)
                first[1].append(a_re * ge_im + a_im * ge_re)
                first[2].append(b * ge_sq)
                second[0].append(a_re * ga_re + a_im * ga_im)
                second[1].append(a_re * ga_im - a_im * ga_re)
                second[2].append(b * (ga_re * ga_re + ga_im * ga_im))
            part = scatter(k, 0, sum(first, [])), scatter(k, 1, [v[0] + v[1] for v in second])
            total = add(total, part)
        num_re, num_im, den = station_sums(total)
        for i, (num, previous) in enumerate(((num_re, gain_re), (num_im, gain_im))):
            solved = 0.5 * ((num + damping * previous) / (den + damping) + previous)
            for f in range(2):
                state[2 * i + f, h * group : (h + 1) * group, :] = solved[f * group : (f + 1) * group]

    build_onehot(0)
    totals = [make_products(h, 0, outgoing[h, me_bl]) for h in range(2)]
    for k in range(1, n_bl):
        pair_copies[k].wait()
        build_onehot(k)
    send(1)
    for h in range(2):
        total = totals[h]
        for k in range(1, n_bl):
            data_copy(h, k).wait_recv()
            total = add(total, make_products(h, k, incoming[h, k]))
        solve(h, total)

    my_rows = pl.ds(pl.multiple_of(me_bl * own, SUBLANES), own)
    sol_copies = []
    for k in range(n_bl - 1, 0, -1):
        partner = exchange_partner(me_bl, k, n_bl)
        sol_copies.append(
            pltpu.make_async_remote_copy(
                src_ref=state.at[:, :, pl.ds(pl.multiple_of(partner * owned, LANES), owned)],
                dst_ref=sol.at[:, my_rows, :], send_sem=sol_send.at[k], recv_sem=sol_recv.at[k],
                device_id={"bl": partner}, device_id_type=MESH,
            )
        )
        sol_copies[-1].start()
    sol[:, my_rows, :] = state[:, :, pl.ds(pl.multiple_of(me_bl * owned, LANES), owned)]

    channel_total = channels * n_ch
    scale, mean_square, ratio = basis_coefficients(channel_total)
    index = lax.broadcasted_iota(jnp.int32, (channels, owned), 0) + me_ch * channels
    x = (2.0 * index.astype(f32) - (channel_total - 1.0)) * (1.0 / (channel_total - 1.0))
    basis = [
        jnp.full((channels, owned), scale[0], f32),
        scale[1] * x,
        scale[2] * (x * x - mean_square),
        scale[3] * (x * (x * x - ratio)),
    ]
    for copy in sol_copies:
        copy.wait_recv()
    for i in range(4):
        solved = sol[i]
        for d in range(4):
            moments[4 * i + d : 4 * i + d + 1, :] = jnp.sum(basis[d] * solved, axis=0, keepdims=True)
    mom_copies = []
    for k in range(1, n_ch):
        mom_copies.append(
            pltpu.make_async_remote_copy(
                src_ref=moments, dst_ref=moments_in.at[k], send_sem=mom_send.at[k], recv_sem=mom_recv.at[k],
                device_id={"ch": lax.rem(me_ch + k, n_ch)}, device_id_type=MESH,
            )
        )
        mom_copies[-1].start()
    whole = moments[...]
    for k, copy in enumerate(mom_copies, 1):
        copy.wait_recv()
        whole = whole + moments_in[k]
    for i in range(4):
        row = basis[0] * whole[4 * i : 4 * i + 1, :]
        for d in range(1, 4):
            row = row + basis[d] * whole[4 * i + d : 4 * i + d + 1, :]
        fit[i] = row
    sent = [data_copy(1, k) for k in range(1, n_bl)]
    for copy in sent + sol_copies + mom_copies:
        copy.wait_send()


def write_out(solved_ref, fitted_ref, solved_out, fitted_out, sems):
    copies = [
        pltpu.make_async_copy(solved_ref, solved_out, sems.at[0]),
        pltpu.make_async_copy(fitted_ref, fitted_out, sems.at[1]),
    ]
    for copy in copies:
        copy.start()
    for copy in copies:
        copy.wait()


def fused(n_bl, n_ch, visibilities, sky_model, antenna_pairs, tile_counts, usable_mask):
    channels, slots = usable_mask.shape
    own = channels // n_bl
    owned = STATION_COUNT // n_bl
    out = jax.ShapeDtypeStruct((4, channels, owned), jnp.float32)
    vmem = pl.BlockSpec(memory_space=pltpu.VMEM)
    hbm = pl.BlockSpec(memory_space=pltpu.HBM)
    dma = pltpu.SemaphoreType.DMA
    solved, fitted = pl.pallas_call(
        functools.partial(calibrate, n_bl, n_ch),
        out_shape=(out, out),
        in_specs=[hbm, hbm, hbm, pl.BlockSpec(memory_space=pltpu.SMEM), hbm],
        out_specs=(vmem, vmem),
        scratch_shapes=[
            pltpu.VMEM(visibilities.shape, visibilities.dtype),
            pltpu.VMEM(sky_model.shape, sky_model.dtype),
            pltpu.VMEM(usable_mask.shape, usable_mask.dtype),
            pltpu.VMEM((2, n_bl, 8 * own, slots), jnp.bfloat16),
            pltpu.VMEM((2, n_bl, 8 * own, slots), jnp.bfloat16),
            pltpu.VMEM((n_bl, 2, slots), jnp.int32),
            pltpu.VMEM((n_bl, STATION_COUNT // 2, 2 * slots), jnp.bfloat16),
            pltpu.VMEM((n_bl, 2 * slots, STATION_COUNT // 2), jnp.bfloat16),
            pltpu.VMEM((2, n_bl, 6, own, slots), jnp.float32),
            pltpu.VMEM((4, own, STATION_COUNT), jnp.float32),
            pltpu.VMEM((16, owned), jnp.float32),
            pltpu.VMEM((n_ch, 16, owned), jnp.float32),
            dma((4,)), dma((2, n_bl)), dma((2, n_bl)), dma((n_bl,)), dma((n_bl,)),
            dma((n_bl,)), dma((n_bl,)), dma((n_ch,)), dma((n_ch,)),
        ],
        compiler_params=pltpu.CompilerParams(
            collective_id=0, has_side_effects=True, vmem_limit_bytes=40 * 1024 * 1024
        ),
    )(
        pltpu.with_memory_space_constraint(visibilities, pltpu.HBM),
        pltpu.with_memory_space_constraint(sky_model, pltpu.HBM),
        pltpu.with_memory_space_constraint(antenna_pairs, pltpu.HBM),
        tile_counts,
        pltpu.with_memory_space_constraint(usable_mask, pltpu.HBM),
    )
    solved, fitted = pl.pallas_call(
        write_out,
        out_shape=(out, out),
        in_specs=[vmem, vmem],
        out_specs=(hbm, hbm),
        scratch_shapes=[dma((2,))],
        compiler_params=pltpu.CompilerParams(vmem_limit_bytes=4 * 1024 * 1024),
    )(solved, fitted)
    shape = (2, 2, channels, owned)
    return solved.reshape(shape), fitted.reshape(shape)


def split_parts(data):
    planes = data.astype(jnp.float32)
    shape_rest = planes.shape[1:]
    return (planes[:4].reshape((2, 2) + shape_rest), planes[4:].reshape((2, 2) + shape_rest))


def poly_basis(channel_total):
    node_values = (2.0 * jnp.arange(channel_total, dtype=jnp.float32) - (channel_total - 1)) / (
        channel_total - 1
    )
    basis_rows = []
    for degree in range(4):
        vector = node_values**degree
        for earlier in basis_rows:
            vector = vector - jnp.sum(vector * earlier) * earlier
        vector = vector / jnp.sqrt(jnp.sum(vector * vector))
        basis_rows.append(vector)
    return jnp.stack(basis_rows)


def contributions(
    model_real_part, model_imaginary, vis_real, vis_imag, first_gain, second_gain, weights
):
    second_real = second_gain[0][None]
    second_imag = second_gain[1][None]
    left_real = model_real_part * second_real + model_imaginary * second_imag
    left_imag = model_imaginary * second_real - model_real_part * second_imag
    first_num_real = jnp.sum(left_real * vis_real + left_imag * vis_imag, axis=1) * weights
    first_num_imag = jnp.sum(left_real * vis_imag - left_imag * vis_real, axis=1) * weights
    first_den = jnp.sum(left_real * left_real + left_imag * left_imag, axis=1) * weights
    first_real = first_gain[0][:, None]
    first_imag = first_gain[1][:, None]
    right_real = model_real_part * first_real - model_imaginary * first_imag
    right_imag = model_real_part * first_imag + model_imaginary * first_real
    second_num_real = jnp.sum(right_real * vis_real + right_imag * vis_imag, axis=0) * weights
    second_num_imag = jnp.sum(right_imag * vis_real - right_real * vis_imag, axis=0) * weights
    second_den = jnp.sum(right_real * right_real + right_imag * right_imag, axis=0) * weights
    return (
        jnp.stack([first_num_real, first_num_imag, first_den]),
        jnp.stack([second_num_real, second_num_imag, second_den]),
    )


def refresh(station_sums, previous):
    divisor = station_sums[2] + damping
    return jnp.stack(
        [
            (station_sums[0] + damping * previous[0]) / divisor,
            (station_sums[1] + damping * previous[1]) / divisor,
        ]
    )


def station_totals(end_first, end_second, first_endpoints, second_ends):
    total_slots = end_first.shape[3]
    flat_first = end_first.reshape(-1, total_slots)
    flat_second = end_second.reshape(-1, total_slots)
    block_rows = math.gcd(total_slots, 1024)
    block_count = total_slots // block_rows
    station_index = jnp.arange(STATION_COUNT, dtype=jnp.int32)

    def add_block(block, total):
        table_first = (first_endpoints[:, None] == station_index[None, :]).astype(jnp.float32)
        table_second = (second_ends[:, None] == station_index[None, :]).astype(jnp.float32)
        return (
            total
            + jnp.dot(
                flat_first, table_first, precision=highest, preferred_element_type=jnp.float32
            )
            + jnp.dot(
                flat_second, table_second, precision=highest, preferred_element_type=jnp.float32
            )
        )

    empty = jnp.zeros((flat_first.shape[0], STATION_COUNT), jnp.float32)
    summed = lax.fori_loop(0, block_count, add_block, empty)
    return summed.reshape(end_first.shape[:3] + (STATION_COUNT,))


def spread(owned_gains):
    return lax.all_gather(owned_gains, "bl", axis=3, tiled=True)


def local(visibilities, sky_model, antenna_pairs, tile_counts, usable_mask):
    vis_real, vis_imag = split_parts(visibilities)
    model_real_part, model_imaginary = split_parts(sky_model)
    channel_local = visibilities.shape[1]
    tile_rows = visibilities.shape[2]
    owner_count = lax.axis_size("bl")
    owned_count = STATION_COUNT // owner_count
    owner_start = lax.axis_index("bl") * owned_count
    live_slots = jnp.arange(tile_rows, dtype=jnp.int32) < tile_counts[0]
    weights = usable_mask.astype(jnp.float32) * live_slots.astype(jnp.float32)[None, :]
    channel_total = channel_local * lax.axis_size("ch")
    poly_rows = lax.dynamic_slice_in_dim(
        poly_basis(channel_total), lax.axis_index("ch") * channel_local, channel_local, 1
    )
    gain_state = jnp.stack(
        [
            jnp.ones((2, channel_local, STATION_COUNT), jnp.float32),
            jnp.zeros((2, channel_local, STATION_COUNT), jnp.float32),
        ]
    )
    solved = gain_state
    for iteration in range(SWEEPS):
        first_gain = jnp.take(gain_state, antenna_pairs[0], axis=3)
        second_gain = jnp.take(gain_state, antenna_pairs[1], axis=3)
        end_first, end_second = contributions(
            model_real_part, model_imaginary, vis_real, vis_imag, first_gain, second_gain, weights
        )
        partial_sums = station_totals(end_first, end_second, antenna_pairs[0], antenna_pairs[1])
        station_sums = lax.psum_scatter(partial_sums, "bl", scatter_dimension=3, tiled=True)
        previous = lax.dynamic_slice_in_dim(gain_state, owner_start, owned_count, 3)
        renewed = refresh(station_sums, previous)
        if iteration == 1:
            renewed = 0.5 * (renewed + previous)
        solved = renewed
        if iteration < SWEEPS - 1:
            gain_state = spread(renewed)
    local_moments = jnp.einsum("kc,rfca->krfa", poly_rows, solved, precision=highest)
    moments = lax.psum(local_moments, "ch")
    fitted = jnp.einsum("kc,krfa->rfca", poly_rows, moments, precision=highest)
    return (solved, fitted)


def solution(mesh):
    n_bl, n_ch = mesh.shape["bl"], mesh.shape["ch"]

    def run(visibilities, sky_model, antenna_pairs, tile_counts, usable_mask):
        channels, slots = usable_mask.shape
        whole_tiles = (
            channels % (n_bl * SUBLANES) == 0
            and slots % LANES == 0
            and STATION_COUNT % (n_bl * LANES) == 0
            and n_bl & (n_bl - 1) == 0
        )
        plan = functools.partial(fused, n_bl, n_ch) if whole_tiles else local
        return plan(visibilities, sky_model, antenna_pairs, tile_counts, usable_mask)

    return jax.shard_map(
        run,
        mesh=mesh,
        in_specs=(
            P(None, "ch", ("grp", "bl")),
            P(None, "ch", ("grp", "bl")),
            P(None, ("grp", "bl")),
            P(("grp", "bl")),
            P("ch", ("grp", "bl")),
        ),
        out_specs=(P(None, None, "ch", ("grp", "bl")), P(None, None, "ch", ("grp", "bl"))),
        check_vma=False,
    )
```

```python
import functools
import math

import jax
import jax.numpy as jnp
import numpy as np
from jax import lax
from jax.experimental import pallas as pl
from jax.experimental.pallas import tpu as pltpu
from jax.sharding import PartitionSpec as P

STATION_COUNT = 512
SWEEPS = 2


damping = 4.0
highest = lax.Precision.HIGHEST
MESH = pl.DeviceIdType.MESH
LANES = 128
SUBLANES = 8


def basis_coefficients(channel_total):
    x = (2.0 * np.arange(channel_total, dtype=np.float64) - (channel_total - 1)) / (channel_total - 1)
    m = np.mean(x**2)
    r = np.sum(x**4) / np.sum(x**2)
    a = [1.0 / np.sqrt(np.sum(v * v)) for v in (np.ones_like(x), x, x**2 - m, x**3 - r * x)]
    return [float(v) for v in a], float(m), float(r)


def split_hi_lo(values):
    hi = values.astype(jnp.bfloat16).astype(jnp.float32)
    return jnp.concatenate([hi, values - hi], axis=0).astype(jnp.bfloat16)


def exchange_partner(me, k, n):
    partner, bit = 0, 1
    while bit < n:
        mine, other = (me // bit) % 2, (k // bit) % 2
        partner = partner + (mine + other - 2 * mine * other) * bit
        bit *= 2
    return partner


def calibrate(
    n_bl, n_ch, vis_hbm, model_hbm, pairs_hbm, counts_ref, mask_hbm, sol, fit,
    vis_ref, model_ref, mask_ref, outgoing, incoming, pairs_all, onehot, onehot_t, products, state, landed, moments, moments_in,
    load_sem, data_send, data_recv, pair_send, pair_recv, sol_send, sol_recv, mom_send, mom_recv,
):
    me_bl = lax.axis_index("bl")
    me_ch = lax.axis_index("ch")
    channels, slots = mask_ref.shape
    own = channels // n_bl
    stations = state.shape[3]
    owned = stations // n_bl
    half = stations // 2
    f32 = jnp.float32

    loads = [
        pltpu.make_async_copy(pairs_hbm, pairs_all.at[0], load_sem.at[0]),
        pltpu.make_async_copy(vis_hbm, vis_ref, load_sem.at[1]),
        pltpu.make_async_copy(mask_hbm, mask_ref, load_sem.at[2]),
        pltpu.make_async_copy(model_hbm, model_ref, load_sem.at[3]),
    ]
    for load in loads:
        load.start()
    barrier = pltpu.get_barrier_semaphore()
    for k in range(1, n_bl):
        pl.semaphore_signal(barrier, inc=1, device_id={"bl": exchange_partner(me_bl, k, n_bl)}, device_id_type=MESH)
    for k in range(1, n_ch):
        pl.semaphore_signal(barrier, inc=1, device_id={"ch": lax.rem(me_ch + k, n_ch)}, device_id_type=MESH)

    group = own // 2

    def prepare(h, weights):
        for part, ref in enumerate((vis_ref, model_ref)):
            for plane in range(0, 8, 4):
                four = [ref[j].astype(f32) for j in range(plane, plane + 4)]
                if part == 1:
                    four = [v * weights for v in four]
                base = (4 * part + plane // 2) * own
                for z in range(n_bl):
                    rows = slice(z * own + h * group, z * own + (h + 1) * group)
                    block = jnp.concatenate([v[rows] for v in four], axis=0)
                    outgoing[h, z, base : base + 2 * own, :] = block.astype(jnp.bfloat16)

    def data_copy(part, k):
        partner = exchange_partner(me_bl, k, n_bl)
        return pltpu.make_async_remote_copy(
            src_ref=outgoing.at[part, partner], dst_ref=incoming.at[part, k], send_sem=data_send.at[part, k],
            recv_sem=data_recv.at[part, k], device_id={"bl": partner}, device_id_type=MESH,
        )

    odd = lax.rem(me_ch, 2)

    def send(h):
        for i in range(1, n_bl):
            k = i + odd * (n_bl - 2 * i)
            if h:
                data_copy(h - 1, k).wait_send()
            data_copy(h, k).start()

    for load in loads:
        load.wait()
    live = lax.broadcasted_iota(jnp.int32, (channels, slots), 1) < counts_ref[0]
    weights = jnp.where(live, mask_ref[...], 0).astype(f32)
    prepare(0, weights)
    pl.semaphore_wait(barrier, n_bl + n_ch - 2)
    pair_copies = {}
    for k in range(1, n_bl):
        pair_copies[k] = pltpu.make_async_remote_copy(
            src_ref=pairs_all.at[0], dst_ref=pairs_all.at[k], send_sem=pair_send.at[k], recv_sem=pair_recv.at[k],
            device_id={"bl": exchange_partner(me_bl, k, n_bl)}, device_id_type=MESH,
        )
        pair_copies[k].start()
    send(0)
    prepare(1, weights)

    def end_row(k):
        return jnp.concatenate([pairs_all[k, 0:1, :], pairs_all[k, 1:2, :]], axis=1)

    def is_upper(k, e):
        return pairs_all[k, e : e + 1, :] >= half

    def build_onehot(k):
        ends = end_row(k)
        within = jnp.where(ends >= half, ends - half, ends)
        step = 32

        def rows(i, carry):
            base = pl.multiple_of(i * step, step)
            station = lax.broadcasted_iota(jnp.int32, (step, 2 * slots), 0) + base
            onehot[k, pl.ds(base, step), :] = jnp.where(station == within, 1.0, 0.0).astype(jnp.bfloat16)
            return carry

        lax.fori_loop(0, half // step, rows, 0)
        onehot_t[k] = onehot[k].T

    def scatter(k, e, blocks):
        split = split_hi_lo(jnp.concatenate(blocks, axis=0))
        upper = split * jnp.where(is_upper(k, e), 1.0, 0.0).astype(jnp.bfloat16)
        both = jnp.concatenate([split - upper, upper], axis=0)
        summed = jnp.dot(both, onehot_t[k, e * slots : (e + 1) * slots, :], preferred_element_type=f32)
        n = len(blocks) * own
        return jnp.concatenate([summed[:n] + summed[n : 2 * n], summed[2 * n : 3 * n] + summed[3 * n :]], axis=1)

    def gather(k, e, split_gains):
        both = jnp.dot(split_gains, onehot[k, :, e * slots : (e + 1) * slots], preferred_element_type=f32)
        n = split_gains.shape[0] // 4
        both = jnp.where(is_upper(k, e), both[2 * n : 3 * n] + both[3 * n :], both[:n] + both[n : 2 * n])
        return both.reshape(n // own, own, slots)

    def split_halves(blocks):
        split = split_hi_lo(jnp.concatenate(blocks, axis=0))
        return jnp.concatenate([split[:, :half], split[:, half:]], axis=0)

    def make_products(h, k, block):
        block = block.astype(f32).reshape(8, own, slots)
        a_re, a_im, b = [], [], []
        for p in range(2):
            vr, vi, mr, mi = block[p], block[2 + p], block[4 + p], block[6 + p]
            a_re.append(mr * vr + mi * vi)
            a_im.append(mr * vi - mi * vr)
            b.append(mr * mr + mi * mi)
            products[h, k, p] = a_re[p]
            products[h, k, 2 + p] = a_im[p]
            products[h, k, 4 + p] = b[p]
        first = scatter(k, 0, a_re + a_im + b)
        second = scatter(k, 1, [a_re[0] + a_re[1], -(a_im[0] + a_im[1]), b[0] + b[1]])
        return first, second

    def add(left, right):
        return right if left is None else (left[0] + right[0], left[1] + right[1])

    def station_sums(total):
        first = total[0].reshape(6, own, stations)
        second = total[1].reshape(3, own, stations)
        sums = []
        for i in range(3):
            feeds = [first[2 * i + p][:group] + first[2 * i + p][group:] for p in range(2)]
            sums.append(jnp.concatenate(feeds, axis=0) + second[i])
        return sums

    def solve(h, total):
        num_re, num_im, den = station_sums(total)
        gain_re = (num_re + damping) / (den + damping)
        gain_im = num_im / (den + damping)
        for_second = split_halves([gain_re, gain_im])
        twice = [jnp.concatenate([g[f * group : (f + 1) * group]] * 2, axis=0) for g in (gain_re, gain_im) for f in range(2)]
        for_first = split_halves(twice)
        total = None
        for k in range(n_bl):
            ga = gather(k, 0, for_first)
            ge_re, ge_im = gather(k, 1, for_second)
            ge_sq = ge_re * ge_re + ge_im * ge_im
            first, second = [[], [], []], [[], [], []]
            for p in range(2):
                a_re, a_im, b = products[h, k, p], products[h, k, 2 + p], products[h, k, 4 + p]
                ga_re, ga_im = ga[p], ga[2 + p]
                first[0].append(a_re * ge_re - a_im * ge_im)
                first[1].append(a_re * ge_im + a_im * ge_re)
                first[2].append(b * ge_sq)
                second[0].append(a_re * ga_re + a_im * ga_im)
                second[1].append(a_re * ga_im - a_im * ga_re)
                second[2].append(b * (ga_re * ga_re + ga_im * ga_im))
            part = scatter(k, 0, sum(first, [])), scatter(k, 1, [v[0] + v[1] for v in second])
            total = add(total, part)
        num_re, num_im, den = station_sums(total)
        for i, (num, previous) in enumerate(((num_re, gain_re), (num_im, gain_im))):
            state[h, i] = 0.5 * ((num + damping * previous) / (den + damping) + previous)

    def sol_copy(h, k):
        partner = exchange_partner(me_bl, k, n_bl)
        return pltpu.make_async_remote_copy(
            src_ref=state.at[h, :, :, pl.ds(pl.multiple_of(partner * owned, LANES), owned)],
            dst_ref=landed.at[h, me_bl], send_sem=sol_send.at[h, k], recv_sem=sol_recv.at[h, k],
            device_id={"bl": partner}, device_id_type=MESH,
        )

    build_onehot(0)
    totals = [make_products(h, 0, outgoing[h, me_bl]) for h in range(2)]
    for k in range(1, n_bl):
        pair_copies[k].wait()
        build_onehot(k)
    send(1)
    for h in range(2):
        total = totals[h]
        for k in range(1, n_bl):
            data_copy(h, k).wait_recv()
            total = add(total, make_products(h, k, incoming[h, k]))
        solve(h, total)
        for k in range(n_bl - 1, 0, -1):
            sol_copy(h, k).start()
        landed[h, me_bl] = state[h, :, :, pl.ds(pl.multiple_of(me_bl * owned, LANES), owned)]

    channel_total = channels * n_ch
    scale, mean_square, ratio = basis_coefficients(channel_total)
    index = lax.broadcasted_iota(jnp.int32, (channels, owned), 0) + me_ch * channels
    x = (2.0 * index.astype(f32) - (channel_total - 1.0)) * (1.0 / (channel_total - 1.0))
    basis = [
        jnp.full((channels, owned), scale[0], f32),
        scale[1] * x,
        scale[2] * (x * x - mean_square),
        scale[3] * (x * (x * x - ratio)),
    ]
    for h in range(2):
        for k in range(1, n_bl):
            sol_copy(h, k).wait_recv()
        for z in range(n_bl):
            rows = slice(z * own + h * group, z * own + (h + 1) * group)
            for i in range(2):
                block = landed[h, z, i]
                for f in range(2):
                    sol[2 * i + f, rows, :] = block[f * group : (f + 1) * group]
    for i in range(4):
        solved = sol[i]
        for d in range(4):
            moments[4 * i + d : 4 * i + d + 1, :] = jnp.sum(basis[d] * solved, axis=0, keepdims=True)
    mom_copies = []
    for k in range(1, n_ch):
        mom_copies.append(
            pltpu.make_async_remote_copy(
                src_ref=moments, dst_ref=moments_in.at[k], send_sem=mom_send.at[k], recv_sem=mom_recv.at[k],
                device_id={"ch": lax.rem(me_ch + k, n_ch)}, device_id_type=MESH,
            )
        )
        mom_copies[-1].start()
    whole = moments[...]
    for k, copy in enumerate(mom_copies, 1):
        copy.wait_recv()
        whole = whole + moments_in[k]
    for i in range(4):
        row = basis[0] * whole[4 * i : 4 * i + 1, :]
        for d in range(1, 4):
            row = row + basis[d] * whole[4 * i + d : 4 * i + d + 1, :]
        fit[i] = row
    sent = [data_copy(1, k) for k in range(1, n_bl)]
    sent += [sol_copy(h, k) for h in range(2) for k in range(1, n_bl)]
    for copy in sent + mom_copies:
        copy.wait_send()


def write_out(solved_ref, fitted_ref, solved_out, fitted_out, sems):
    copies = [
        pltpu.make_async_copy(solved_ref, solved_out, sems.at[0]),
        pltpu.make_async_copy(fitted_ref, fitted_out, sems.at[1]),
    ]
    for copy in copies:
        copy.start()
    for copy in copies:
        copy.wait()


def fused(n_bl, n_ch, visibilities, sky_model, antenna_pairs, tile_counts, usable_mask):
    channels, slots = usable_mask.shape
    own = channels // n_bl
    owned = STATION_COUNT // n_bl
    out = jax.ShapeDtypeStruct((4, channels, owned), jnp.float32)
    vmem = pl.BlockSpec(memory_space=pltpu.VMEM)
    hbm = pl.BlockSpec(memory_space=pltpu.HBM)
    dma = pltpu.SemaphoreType.DMA
    solved, fitted = pl.pallas_call(
        functools.partial(calibrate, n_bl, n_ch),
        out_shape=(out, out),
        in_specs=[hbm, hbm, hbm, pl.BlockSpec(memory_space=pltpu.SMEM), hbm],
        out_specs=(vmem, vmem),
        scratch_shapes=[
            pltpu.VMEM(visibilities.shape, visibilities.dtype),
            pltpu.VMEM(sky_model.shape, sky_model.dtype),
            pltpu.VMEM(usable_mask.shape, usable_mask.dtype),
            pltpu.VMEM((2, n_bl, 8 * own, slots), jnp.bfloat16),
            pltpu.VMEM((2, n_bl, 8 * own, slots), jnp.bfloat16),
            pltpu.VMEM((n_bl, 2, slots), jnp.int32),
            pltpu.VMEM((n_bl, STATION_COUNT // 2, 2 * slots), jnp.bfloat16),
            pltpu.VMEM((n_bl, 2 * slots, STATION_COUNT // 2), jnp.bfloat16),
            pltpu.VMEM((2, n_bl, 6, own, slots), jnp.float32),
            pltpu.VMEM((2, 2, own, STATION_COUNT), jnp.float32),
            pltpu.VMEM((2, n_bl, 2, own, owned), jnp.float32),
            pltpu.VMEM((16, owned), jnp.float32),
            pltpu.VMEM((n_ch, 16, owned), jnp.float32),
            dma((4,)), dma((2, n_bl)), dma((2, n_bl)), dma((n_bl,)), dma((n_bl,)),
            dma((2, n_bl)), dma((2, n_bl)), dma((n_ch,)), dma((n_ch,)),
        ],
        compiler_params=pltpu.CompilerParams(
            collective_id=0, has_side_effects=True, vmem_limit_bytes=40 * 1024 * 1024
        ),
    )(
        pltpu.with_memory_space_constraint(visibilities, pltpu.HBM),
        pltpu.with_memory_space_constraint(sky_model, pltpu.HBM),
        pltpu.with_memory_space_constraint(antenna_pairs, pltpu.HBM),
        tile_counts,
        pltpu.with_memory_space_constraint(usable_mask, pltpu.HBM),
    )
    solved, fitted = pl.pallas_call(
        write_out,
        out_shape=(out, out),
        in_specs=[vmem, vmem],
        out_specs=(hbm, hbm),
        scratch_shapes=[dma((2,))],
        compiler_params=pltpu.CompilerParams(vmem_limit_bytes=4 * 1024 * 1024),
    )(solved, fitted)
    shape = (2, 2, channels, owned)
    return solved.reshape(shape), fitted.reshape(shape)


def split_parts(data):
    planes = data.astype(jnp.float32)
    shape_rest = planes.shape[1:]
    return (planes[:4].reshape((2, 2) + shape_rest), planes[4:].reshape((2, 2) + shape_rest))


def poly_basis(channel_total):
    node_values = (2.0 * jnp.arange(channel_total, dtype=jnp.float32) - (channel_total - 1)) / (
        channel_total - 1
    )
    basis_rows = []
    for degree in range(4):
        vector = node_values**degree
        for earlier in basis_rows:
            vector = vector - jnp.sum(vector * earlier) * earlier
        vector = vector / jnp.sqrt(jnp.sum(vector * vector))
        basis_rows.append(vector)
    return jnp.stack(basis_rows)


def contributions(
    model_real_part, model_imaginary, vis_real, vis_imag, first_gain, second_gain, weights
):
    second_real = second_gain[0][None]
    second_imag = second_gain[1][None]
    left_real = model_real_part * second_real + model_imaginary * second_imag
    left_imag = model_imaginary * second_real - model_real_part * second_imag
    first_num_real = jnp.sum(left_real * vis_real + left_imag * vis_imag, axis=1) * weights
    first_num_imag = jnp.sum(left_real * vis_imag - left_imag * vis_real, axis=1) * weights
    first_den = jnp.sum(left_real * left_real + left_imag * left_imag, axis=1) * weights
    first_real = first_gain[0][:, None]
    first_imag = first_gain[1][:, None]
    right_real = model_real_part * first_real - model_imaginary * first_imag
    right_imag = model_real_part * first_imag + model_imaginary * first_real
    second_num_real = jnp.sum(right_real * vis_real + right_imag * vis_imag, axis=0) * weights
    second_num_imag = jnp.sum(right_imag * vis_real - right_real * vis_imag, axis=0) * weights
    second_den = jnp.sum(right_real * right_real + right_imag * right_imag, axis=0) * weights
    return (
        jnp.stack([first_num_real, first_num_imag, first_den]),
        jnp.stack([second_num_real, second_num_imag, second_den]),
    )


def refresh(station_sums, previous):
    divisor = station_sums[2] + damping
    return jnp.stack(
        [
            (station_sums[0] + damping * previous[0]) / divisor,
            (station_sums[1] + damping * previous[1]) / divisor,
        ]
    )


def station_totals(end_first, end_second, first_endpoints, second_ends):
    total_slots = end_first.shape[3]
    flat_first = end_first.reshape(-1, total_slots)
    flat_second = end_second.reshape(-1, total_slots)
    block_rows = math.gcd(total_slots, 1024)
    block_count = total_slots // block_rows
    station_index = jnp.arange(STATION_COUNT, dtype=jnp.int32)

    def add_block(block, total):
        table_first = (first_endpoints[:, None] == station_index[None, :]).astype(jnp.float32)
        table_second = (second_ends[:, None] == station_index[None, :]).astype(jnp.float32)
        return (
            total
            + jnp.dot(
                flat_first, table_first, precision=highest, preferred_element_type=jnp.float32
            )
            + jnp.dot(
                flat_second, table_second, precision=highest, preferred_element_type=jnp.float32
            )
        )

    empty = jnp.zeros((flat_first.shape[0], STATION_COUNT), jnp.float32)
    summed = lax.fori_loop(0, block_count, add_block, empty)
    return summed.reshape(end_first.shape[:3] + (STATION_COUNT,))


def spread(owned_gains):
    return lax.all_gather(owned_gains, "bl", axis=3, tiled=True)


def local(visibilities, sky_model, antenna_pairs, tile_counts, usable_mask):
    vis_real, vis_imag = split_parts(visibilities)
    model_real_part, model_imaginary = split_parts(sky_model)
    channel_local = visibilities.shape[1]
    tile_rows = visibilities.shape[2]
    owner_count = lax.axis_size("bl")
    owned_count = STATION_COUNT // owner_count
    owner_start = lax.axis_index("bl") * owned_count
    live_slots = jnp.arange(tile_rows, dtype=jnp.int32) < tile_counts[0]
    weights = usable_mask.astype(jnp.float32) * live_slots.astype(jnp.float32)[None, :]
    channel_total = channel_local * lax.axis_size("ch")
    poly_rows = lax.dynamic_slice_in_dim(
        poly_basis(channel_total), lax.axis_index("ch") * channel_local, channel_local, 1
    )
    gain_state = jnp.stack(
        [
            jnp.ones((2, channel_local, STATION_COUNT), jnp.float32),
            jnp.zeros((2, channel_local, STATION_COUNT), jnp.float32),
        ]
    )
    solved = gain_state
    for iteration in range(SWEEPS):
        first_gain = jnp.take(gain_state, antenna_pairs[0], axis=3)
        second_gain = jnp.take(gain_state, antenna_pairs[1], axis=3)
        end_first, end_second = contributions(
            model_real_part, model_imaginary, vis_real, vis_imag, first_gain, second_gain, weights
        )
        partial_sums = station_totals(end_first, end_second, antenna_pairs[0], antenna_pairs[1])
        station_sums = lax.psum_scatter(partial_sums, "bl", scatter_dimension=3, tiled=True)
        previous = lax.dynamic_slice_in_dim(gain_state, owner_start, owned_count, 3)
        renewed = refresh(station_sums, previous)
        if iteration == 1:
            renewed = 0.5 * (renewed + previous)
        solved = renewed
        if iteration < SWEEPS - 1:
            gain_state = spread(renewed)
    local_moments = jnp.einsum("kc,rfca->krfa", poly_rows, solved, precision=highest)
    moments = lax.psum(local_moments, "ch")
    fitted = jnp.einsum("kc,krfa->rfca", poly_rows, moments, precision=highest)
    return (solved, fitted)


def solution(mesh):
    n_bl, n_ch = mesh.shape["bl"], mesh.shape["ch"]

    def run(visibilities, sky_model, antenna_pairs, tile_counts, usable_mask):
        channels, slots = usable_mask.shape
        whole_tiles = (
            channels % (n_bl * SUBLANES) == 0
            and slots % LANES == 0
            and STATION_COUNT % (n_bl * LANES) == 0
            and n_bl & (n_bl - 1) == 0
        )
        plan = functools.partial(fused, n_bl, n_ch) if whole_tiles else local
        return plan(visibilities, sky_model, antenna_pairs, tile_counts, usable_mask)

    return jax.shard_map(
        run,
        mesh=mesh,
        in_specs=(
            P(None, "ch", ("grp", "bl")),
            P(None, "ch", ("grp", "bl")),
            P(None, ("grp", "bl")),
            P(("grp", "bl")),
            P("ch", ("grp", "bl")),
        ),
        out_specs=(P(None, None, "ch", ("grp", "bl")), P(None, None, "ch", ("grp", "bl"))),
        check_vma=False,
    )
```

```python
import functools
import math

import jax
import jax.numpy as jnp
import numpy as np
from jax import lax
from jax.experimental import pallas as pl
from jax.experimental.pallas import tpu as pltpu
from jax.sharding import PartitionSpec as P

STATION_COUNT = 512
SWEEPS = 2


damping = 4.0
highest = lax.Precision.HIGHEST
MESH = pl.DeviceIdType.MESH
LANES = 128
SUBLANES = 8


def basis_coefficients(channel_total):
    x = (2.0 * np.arange(channel_total, dtype=np.float64) - (channel_total - 1)) / (channel_total - 1)
    m = np.mean(x**2)
    r = np.sum(x**4) / np.sum(x**2)
    a = [1.0 / np.sqrt(np.sum(v * v)) for v in (np.ones_like(x), x, x**2 - m, x**3 - r * x)]
    return [float(v) for v in a], float(m), float(r)


def split_hi_lo(values):
    hi = values.astype(jnp.bfloat16).astype(jnp.float32)
    return jnp.concatenate([hi, values - hi], axis=0).astype(jnp.bfloat16)


def exchange_partner(me, k, n):
    partner, bit = 0, 1
    while bit < n:
        mine, other = (me // bit) % 2, (k // bit) % 2
        partner = partner + (mine + other - 2 * mine * other) * bit
        bit *= 2
    return partner


def calibrate(
    n_bl, n_ch, vis_hbm, model_hbm, pairs_hbm, counts_ref, mask_hbm, sol, fit,
    vis_ref, model_ref, mask_ref, outgoing, incoming, pairs_all, onehot, onehot_t, products, state, moments, moments_in,
    load_sem, data_send, data_recv, pair_send, pair_recv, sol_send, sol_recv, mom_send, mom_recv,
):
    me_bl = lax.axis_index("bl")
    me_ch = lax.axis_index("ch")
    channels, slots = mask_ref.shape
    own = channels // n_bl
    stations = state.shape[2]
    owned = stations // n_bl
    half = stations // 2
    f32 = jnp.float32

    loads = [
        pltpu.make_async_copy(pairs_hbm, pairs_all.at[0], load_sem.at[0]),
        pltpu.make_async_copy(vis_hbm, vis_ref, load_sem.at[1]),
        pltpu.make_async_copy(mask_hbm, mask_ref, load_sem.at[2]),
        pltpu.make_async_copy(model_hbm, model_ref, load_sem.at[3]),
    ]
    for load in loads:
        load.start()
    barrier = pltpu.get_barrier_semaphore()
    for k in range(1, n_bl):
        pl.semaphore_signal(barrier, inc=1, device_id={"bl": exchange_partner(me_bl, k, n_bl)}, device_id_type=MESH)
    for k in range(1, n_ch):
        pl.semaphore_signal(barrier, inc=1, device_id={"ch": lax.rem(me_ch + k, n_ch)}, device_id_type=MESH)

    group = own // 2

    def prepare(h, weights):
        for part, ref in enumerate((vis_ref, model_ref)):
            for plane in range(0, 8, 4):
                four = [ref[j].astype(f32) for j in range(plane, plane + 4)]
                if part == 1:
                    four = [v * weights for v in four]
                base = (4 * part + plane // 2) * own
                for z in range(n_bl):
                    rows = slice(z * own + h * group, z * own + (h + 1) * group)
                    block = jnp.concatenate([v[rows] for v in four], axis=0)
                    outgoing[h, z, base : base + 2 * own, :] = block.astype(jnp.bfloat16)

    def data_copy(part, k):
        partner = exchange_partner(me_bl, k, n_bl)
        return pltpu.make_async_remote_copy(
            src_ref=outgoing.at[part, partner], dst_ref=incoming.at[part, k], send_sem=data_send.at[part, k],
            recv_sem=data_recv.at[part, k], device_id={"bl": partner}, device_id_type=MESH,
        )

    odd = lax.rem(me_ch, 2)

    def send(h):
        for i in range(1, n_bl):
            k = i + odd * (n_bl - 2 * i)
            if h:
                data_copy(h - 1, k).wait_send()
            data_copy(h, k).start()

    for load in loads:
        load.wait()
    live = lax.broadcasted_iota(jnp.int32, (channels, slots), 1) < counts_ref[0]
    weights = jnp.where(live, mask_ref[...], 0).astype(f32)
    prepare(0, weights)
    pl.semaphore_wait(barrier, n_bl + n_ch - 2)
    pair_copies = {}
    for k in range(1, n_bl):
        pair_copies[k] = pltpu.make_async_remote_copy(
            src_ref=pairs_all.at[0], dst_ref=pairs_all.at[k], send_sem=pair_send.at[k], recv_sem=pair_recv.at[k],
            device_id={"bl": exchange_partner(me_bl, k, n_bl)}, device_id_type=MESH,
        )
        pair_copies[k].start()
    send(0)
    prepare(1, weights)

    def end_row(k):
        return jnp.concatenate([pairs_all[k, 0:1, :], pairs_all[k, 1:2, :]], axis=1)

    def is_upper(k, e):
        return pairs_all[k, e : e + 1, :] >= half

    def build_onehot(k):
        ends = end_row(k)
        within = jnp.where(ends >= half, ends - half, ends)
        step = 32

        def rows(i, carry):
            base = pl.multiple_of(i * step, step)
            station = lax.broadcasted_iota(jnp.int32, (step, 2 * slots), 0) + base
            onehot[k, pl.ds(base, step), :] = jnp.where(station == within, 1.0, 0.0).astype(jnp.bfloat16)
            return carry

        lax.fori_loop(0, half // step, rows, 0)
        onehot_t[k] = onehot[k].T

    def scatter(k, e, blocks):
        split = split_hi_lo(jnp.concatenate(blocks, axis=0))
        upper = split * jnp.where(is_upper(k, e), 1.0, 0.0).astype(jnp.bfloat16)
        both = jnp.concatenate([split - upper, upper], axis=0)
        summed = jnp.dot(both, onehot_t[k, e * slots : (e + 1) * slots, :], preferred_element_type=f32)
        n = len(blocks) * own
        return jnp.concatenate([summed[:n] + summed[n : 2 * n], summed[2 * n : 3 * n] + summed[3 * n :]], axis=1)

    def gather(k, e, split_gains):
        both = jnp.dot(split_gains, onehot[k, :, e * slots : (e + 1) * slots], preferred_element_type=f32)
        n = split_gains.shape[0] // 4
        both = jnp.where(is_upper(k, e), both[2 * n : 3 * n] + both[3 * n :], both[:n] + both[n : 2 * n])
        return both.reshape(n // own, own, slots)

    def split_halves(blocks):
        split = split_hi_lo(jnp.concatenate(blocks, axis=0))
        return jnp.concatenate([split[:, :half], split[:, half:]], axis=0)

    def make_products(h, k, block):
        block = block.astype(f32).reshape(8, own, slots)
        a_re, a_im, b = [], [], []
        for p in range(2):
            vr, vi, mr, mi = block[p], block[2 + p], block[4 + p], block[6 + p]
            a_re.append(mr * vr + mi * vi)
            a_im.append(mr * vi - mi * vr)
            b.append(mr * mr + mi * mi)
            products[h, k, p] = a_re[p]
            products[h, k, 2 + p] = a_im[p]
            products[h, k, 4 + p] = b[p]
        first = scatter(k, 0, a_re + a_im + b)
        second = scatter(k, 1, [a_re[0] + a_re[1], -(a_im[0] + a_im[1]), b[0] + b[1]])
        return first, second

    def add(left, right):
        return right if left is None else (left[0] + right[0], left[1] + right[1])

    def station_sums(total):
        first = total[0].reshape(6, own, stations)
        second = total[1].reshape(3, own, stations)
        sums = []
        for i in range(3):
            feeds = [first[2 * i + p][:group] + first[2 * i + p][group:] for p in range(2)]
            sums.append(jnp.concatenate(feeds, axis=0) + second[i])
        return sums

    def solve(h, total):
        num_re, num_im, den = station_sums(total)
        gain_re = (num_re + damping) / (den + damping)
        gain_im = num_im / (den + damping)
        for_second = split_halves([gain_re, gain_im])
        twice = [jnp.concatenate([g[f * group : (f + 1) * group]] * 2, axis=0) for g in (gain_re, gain_im) for f in range(2)]
        for_first = split_halves(twice)
        total = None
        gathered = [(gather(k, 0, for_first), gather(k, 1, for_second)) for k in range(n_bl)]
        for k in range(n_bl):
            ga, (ge_re, ge_im) = gathered[k]
            ge_sq = ge_re * ge_re + ge_im * ge_im
            first, second = [[], [], []], [[], [], []]
            for p in range(2):
                a_re, a_im, b = products[h, k, p], products[h, k, 2 + p], products[h, k, 4 + p]
                ga_re, ga_im = ga[p], ga[2 + p]
                first[0].append(a_re * ge_re - a_im * ge_im)
                first[1].append(a_re * ge_im + a_im * ge_re)
                first[2].append(b * ge_sq)
                second[0].append(a_re * ga_re + a_im * ga_im)
                second[1].append(a_re * ga_im - a_im * ga_re)
                second[2].append(b * (ga_re * ga_re + ga_im * ga_im))
            part = scatter(k, 0, sum(first, [])), scatter(k, 1, [v[0] + v[1] for v in second])
            total = add(total, part)
        num_re, num_im, den = station_sums(total)
        for i, (num, previous) in enumerate(((num_re, gain_re), (num_im, gain_im))):
            solved = 0.5 * ((num + damping * previous) / (den + damping) + previous)
            for f in range(2):
                state[2 * i + f, h * group : (h + 1) * group, :] = solved[f * group : (f + 1) * group]

    build_onehot(0)
    totals = [make_products(h, 0, outgoing[h, me_bl]) for h in range(2)]
    for k in range(1, n_bl):
        pair_copies[k].wait()
        build_onehot(k)
    send(1)
    for h in range(2):
        total = totals[h]
        for k in range(1, n_bl):
            data_copy(h, k).wait_recv()
            total = add(total, make_products(h, k, incoming[h, k]))
        solve(h, total)

    my_rows = pl.ds(pl.multiple_of(me_bl * own, SUBLANES), own)
    sol_copies = []
    for k in range(n_bl - 1, 0, -1):
        partner = exchange_partner(me_bl, k, n_bl)
        sol_copies.append(
            pltpu.make_async_remote_copy(
                src_ref=state.at[:, :, pl.ds(pl.multiple_of(partner * owned, LANES), owned)],
                dst_ref=sol.at[:, my_rows, :], send_sem=sol_send.at[k], recv_sem=sol_recv.at[k],
                device_id={"bl": partner}, device_id_type=MESH,
            )
        )
        sol_copies[-1].start()
    sol[:, my_rows, :] = state[:, :, pl.ds(pl.multiple_of(me_bl * owned, LANES), owned)]

    channel_total = channels * n_ch
    scale, mean_square, ratio = basis_coefficients(channel_total)
    index = lax.broadcasted_iota(jnp.int32, (channels, owned), 0) + me_ch * channels
    x = (2.0 * index.astype(f32) - (channel_total - 1.0)) * (1.0 / (channel_total - 1.0))
    basis = [
        jnp.full((channels, owned), scale[0], f32),
        scale[1] * x,
        scale[2] * (x * x - mean_square),
        scale[3] * (x * (x * x - ratio)),
    ]
    for copy in sol_copies:
        copy.wait_recv()
    for i in range(4):
        solved = sol[i]
        for d in range(4):
            moments[4 * i + d : 4 * i + d + 1, :] = jnp.sum(basis[d] * solved, axis=0, keepdims=True)
    mom_copies = []
    for k in range(1, n_ch):
        mom_copies.append(
            pltpu.make_async_remote_copy(
                src_ref=moments, dst_ref=moments_in.at[k], send_sem=mom_send.at[k], recv_sem=mom_recv.at[k],
                device_id={"ch": lax.rem(me_ch + k, n_ch)}, device_id_type=MESH,
            )
        )
        mom_copies[-1].start()
    whole = moments[...]
    for k, copy in enumerate(mom_copies, 1):
        copy.wait_recv()
        whole = whole + moments_in[k]
    for i in range(4):
        row = basis[0] * whole[4 * i : 4 * i + 1, :]
        for d in range(1, 4):
            row = row + basis[d] * whole[4 * i + d : 4 * i + d + 1, :]
        fit[i] = row
    sent = [data_copy(1, k) for k in range(1, n_bl)]
    for copy in sent + sol_copies + mom_copies:
        copy.wait_send()


def write_out(solved_ref, fitted_ref, solved_out, fitted_out, sems):
    copies = [
        pltpu.make_async_copy(solved_ref, solved_out, sems.at[0]),
        pltpu.make_async_copy(fitted_ref, fitted_out, sems.at[1]),
    ]
    for copy in copies:
        copy.start()
    for copy in copies:
        copy.wait()


def fused(n_bl, n_ch, visibilities, sky_model, antenna_pairs, tile_counts, usable_mask):
    channels, slots = usable_mask.shape
    own = channels // n_bl
    owned = STATION_COUNT // n_bl
    out = jax.ShapeDtypeStruct((4, channels, owned), jnp.float32)
    vmem = pl.BlockSpec(memory_space=pltpu.VMEM)
    hbm = pl.BlockSpec(memory_space=pltpu.HBM)
    dma = pltpu.SemaphoreType.DMA
    solved, fitted = pl.pallas_call(
        functools.partial(calibrate, n_bl, n_ch),
        out_shape=(out, out),
        in_specs=[hbm, hbm, hbm, pl.BlockSpec(memory_space=pltpu.SMEM), hbm],
        out_specs=(vmem, vmem),
        scratch_shapes=[
            pltpu.VMEM(visibilities.shape, visibilities.dtype),
            pltpu.VMEM(sky_model.shape, sky_model.dtype),
            pltpu.VMEM(usable_mask.shape, usable_mask.dtype),
            pltpu.VMEM((2, n_bl, 8 * own, slots), jnp.bfloat16),
            pltpu.VMEM((2, n_bl, 8 * own, slots), jnp.bfloat16),
            pltpu.VMEM((n_bl, 2, slots), jnp.int32),
            pltpu.VMEM((n_bl, STATION_COUNT // 2, 2 * slots), jnp.bfloat16),
            pltpu.VMEM((n_bl, 2 * slots, STATION_COUNT // 2), jnp.bfloat16),
            pltpu.VMEM((2, n_bl, 6, own, slots), jnp.float32),
            pltpu.VMEM((4, own, STATION_COUNT), jnp.float32),
            pltpu.VMEM((16, owned), jnp.float32),
            pltpu.VMEM((n_ch, 16, owned), jnp.float32),
            dma((4,)), dma((2, n_bl)), dma((2, n_bl)), dma((n_bl,)), dma((n_bl,)),
            dma((n_bl,)), dma((n_bl,)), dma((n_ch,)), dma((n_ch,)),
        ],
        compiler_params=pltpu.CompilerParams(
            collective_id=0, has_side_effects=True, vmem_limit_bytes=40 * 1024 * 1024
        ),
    )(
        pltpu.with_memory_space_constraint(visibilities, pltpu.HBM),
        pltpu.with_memory_space_constraint(sky_model, pltpu.HBM),
        pltpu.with_memory_space_constraint(antenna_pairs, pltpu.HBM),
        tile_counts,
        pltpu.with_memory_space_constraint(usable_mask, pltpu.HBM),
    )
    solved, fitted = pl.pallas_call(
        write_out,
        out_shape=(out, out),
        in_specs=[vmem, vmem],
        out_specs=(hbm, hbm),
        scratch_shapes=[dma((2,))],
        compiler_params=pltpu.CompilerParams(vmem_limit_bytes=4 * 1024 * 1024),
    )(solved, fitted)
    shape = (2, 2, channels, owned)
    return solved.reshape(shape), fitted.reshape(shape)


def split_parts(data):
    planes = data.astype(jnp.float32)
    shape_rest = planes.shape[1:]
    return (planes[:4].reshape((2, 2) + shape_rest), planes[4:].reshape((2, 2) + shape_rest))


def poly_basis(channel_total):
    node_values = (2.0 * jnp.arange(channel_total, dtype=jnp.float32) - (channel_total - 1)) / (
        channel_total - 1
    )
    basis_rows = []
    for degree in range(4):
        vector = node_values**degree
        for earlier in basis_rows:
            vector = vector - jnp.sum(vector * earlier) * earlier
        vector = vector / jnp.sqrt(jnp.sum(vector * vector))
        basis_rows.append(vector)
    return jnp.stack(basis_rows)


def contributions(
    model_real_part, model_imaginary, vis_real, vis_imag, first_gain, second_gain, weights
):
    second_real = second_gain[0][None]
    second_imag = second_gain[1][None]
    left_real = model_real_part * second_real + model_imaginary * second_imag
    left_imag = model_imaginary * second_real - model_real_part * second_imag
    first_num_real = jnp.sum(left_real * vis_real + left_imag * vis_imag, axis=1) * weights
    first_num_imag = jnp.sum(left_real * vis_imag - left_imag * vis_real, axis=1) * weights
    first_den = jnp.sum(left_real * left_real + left_imag * left_imag, axis=1) * weights
    first_real = first_gain[0][:, None]
    first_imag = first_gain[1][:, None]
    right_real = model_real_part * first_real - model_imaginary * first_imag
    right_imag = model_real_part * first_imag + model_imaginary * first_real
    second_num_real = jnp.sum(right_real * vis_real + right_imag * vis_imag, axis=0) * weights
    second_num_imag = jnp.sum(right_imag * vis_real - right_real * vis_imag, axis=0) * weights
    second_den = jnp.sum(right_real * right_real + right_imag * right_imag, axis=0) * weights
    return (
        jnp.stack([first_num_real, first_num_imag, first_den]),
        jnp.stack([second_num_real, second_num_imag, second_den]),
    )


def refresh(station_sums, previous):
    divisor = station_sums[2] + damping
    return jnp.stack(
        [
            (station_sums[0] + damping * previous[0]) / divisor,
            (station_sums[1] + damping * previous[1]) / divisor,
        ]
    )


def station_totals(end_first, end_second, first_endpoints, second_ends):
    total_slots = end_first.shape[3]
    flat_first = end_first.reshape(-1, total_slots)
    flat_second = end_second.reshape(-1, total_slots)
    block_rows = math.gcd(total_slots, 1024)
    block_count = total_slots // block_rows
    station_index = jnp.arange(STATION_COUNT, dtype=jnp.int32)

    def add_block(block, total):
        table_first = (first_endpoints[:, None] == station_index[None, :]).astype(jnp.float32)
        table_second = (second_ends[:, None] == station_index[None, :]).astype(jnp.float32)
        return (
            total
            + jnp.dot(
                flat_first, table_first, precision=highest, preferred_element_type=jnp.float32
            )
            + jnp.dot(
                flat_second, table_second, precision=highest, preferred_element_type=jnp.float32
            )
        )

    empty = jnp.zeros((flat_first.shape[0], STATION_COUNT), jnp.float32)
    summed = lax.fori_loop(0, block_count, add_block, empty)
    return summed.reshape(end_first.shape[:3] + (STATION_COUNT,))


def spread(owned_gains):
    return lax.all_gather(owned_gains, "bl", axis=3, tiled=True)


def local(visibilities, sky_model, antenna_pairs, tile_counts, usable_mask):
    vis_real, vis_imag = split_parts(visibilities)
    model_real_part, model_imaginary = split_parts(sky_model)
    channel_local = visibilities.shape[1]
    tile_rows = visibilities.shape[2]
    owner_count = lax.axis_size("bl")
    owned_count = STATION_COUNT // owner_count
    owner_start = lax.axis_index("bl") * owned_count
    live_slots = jnp.arange(tile_rows, dtype=jnp.int32) < tile_counts[0]
    weights = usable_mask.astype(jnp.float32) * live_slots.astype(jnp.float32)[None, :]
    channel_total = channel_local * lax.axis_size("ch")
    poly_rows = lax.dynamic_slice_in_dim(
        poly_basis(channel_total), lax.axis_index("ch") * channel_local, channel_local, 1
    )
    gain_state = jnp.stack(
        [
            jnp.ones((2, channel_local, STATION_COUNT), jnp.float32),
            jnp.zeros((2, channel_local, STATION_COUNT), jnp.float32),
        ]
    )
    solved = gain_state
    for iteration in range(SWEEPS):
        first_gain = jnp.take(gain_state, antenna_pairs[0], axis=3)
        second_gain = jnp.take(gain_state, antenna_pairs[1], axis=3)
        end_first, end_second = contributions(
            model_real_part, model_imaginary, vis_real, vis_imag, first_gain, second_gain, weights
        )
        partial_sums = station_totals(end_first, end_second, antenna_pairs[0], antenna_pairs[1])
        station_sums = lax.psum_scatter(partial_sums, "bl", scatter_dimension=3, tiled=True)
        previous = lax.dynamic_slice_in_dim(gain_state, owner_start, owned_count, 3)
        renewed = refresh(station_sums, previous)
        if iteration == 1:
            renewed = 0.5 * (renewed + previous)
        solved = renewed
        if iteration < SWEEPS - 1:
            gain_state = spread(renewed)
    local_moments = jnp.einsum("kc,rfca->krfa", poly_rows, solved, precision=highest)
    moments = lax.psum(local_moments, "ch")
    fitted = jnp.einsum("kc,krfa->rfca", poly_rows, moments, precision=highest)
    return (solved, fitted)


def solution(mesh):
    n_bl, n_ch = mesh.shape["bl"], mesh.shape["ch"]

    def run(visibilities, sky_model, antenna_pairs, tile_counts, usable_mask):
        channels, slots = usable_mask.shape
        whole_tiles = (
            channels % (n_bl * SUBLANES) == 0
            and slots % LANES == 0
            and STATION_COUNT % (n_bl * LANES) == 0
            and n_bl & (n_bl - 1) == 0
        )
        plan = functools.partial(fused, n_bl, n_ch) if whole_tiles else local
        return plan(visibilities, sky_model, antenna_pairs, tile_counts, usable_mask)

    return jax.shard_map(
        run,
        mesh=mesh,
        in_specs=(
            P(None, "ch", ("grp", "bl")),
            P(None, "ch", ("grp", "bl")),
            P(None, ("grp", "bl")),
            P(("grp", "bl")),
            P("ch", ("grp", "bl")),
        ),
        out_specs=(P(None, None, "ch", ("grp", "bl")), P(None, None, "ch", ("grp", "bl"))),
        check_vma=False,
    )
```

```python
import functools
import math

import jax
import jax.numpy as jnp
import numpy as np
from jax import lax
from jax.experimental import pallas as pl
from jax.experimental.pallas import tpu as pltpu
from jax.sharding import PartitionSpec as P

STATION_COUNT = 512
SWEEPS = 2


damping = 4.0
highest = lax.Precision.HIGHEST
MESH = pl.DeviceIdType.MESH
LANES = 128
SUBLANES = 8


def basis_coefficients(channel_total):
    x = (2.0 * np.arange(channel_total, dtype=np.float64) - (channel_total - 1)) / (channel_total - 1)
    m = np.mean(x**2)
    r = np.sum(x**4) / np.sum(x**2)
    a = [1.0 / np.sqrt(np.sum(v * v)) for v in (np.ones_like(x), x, x**2 - m, x**3 - r * x)]
    return [float(v) for v in a], float(m), float(r)


def split_hi_lo(values):
    hi = values.astype(jnp.bfloat16).astype(jnp.float32)
    return jnp.concatenate([hi, values - hi], axis=0).astype(jnp.bfloat16)


def exchange_partner(me, k, n):
    partner, bit = 0, 1
    while bit < n:
        mine, other = (me // bit) % 2, (k // bit) % 2
        partner = partner + (mine + other - 2 * mine * other) * bit
        bit *= 2
    return partner


def calibrate(
    n_bl, n_ch, vis_hbm, model_hbm, pairs_hbm, counts_ref, mask_hbm, sol, fit,
    vis_ref, model_ref, mask_ref, outgoing, incoming, pairs_all, onehot, onehot_t, products, state, moments, moments_in,
    load_sem, data_send, data_recv, pair_send, pair_recv, sol_send, sol_recv, mom_send, mom_recv,
):
    me_bl = lax.axis_index("bl")
    me_ch = lax.axis_index("ch")
    channels, slots = mask_ref.shape
    own = channels // n_bl
    stations = state.shape[2]
    owned = stations // n_bl
    half = stations // 2
    f32 = jnp.float32

    loads = [
        pltpu.make_async_copy(pairs_hbm, pairs_all.at[0], load_sem.at[0]),
        pltpu.make_async_copy(vis_hbm.at[0:4], vis_ref.at[0:4], load_sem.at[1]),
        pltpu.make_async_copy(vis_hbm.at[4:8], vis_ref.at[4:8], load_sem.at[2]),
        pltpu.make_async_copy(mask_hbm, mask_ref, load_sem.at[3]),
        pltpu.make_async_copy(model_hbm.at[0:4], model_ref.at[0:4], load_sem.at[4]),
        pltpu.make_async_copy(model_hbm.at[4:8], model_ref.at[4:8], load_sem.at[5]),
    ]
    for load in loads:
        load.start()
    barrier = pltpu.get_barrier_semaphore()
    for k in range(1, n_bl):
        pl.semaphore_signal(barrier, inc=1, device_id={"bl": exchange_partner(me_bl, k, n_bl)}, device_id_type=MESH)
    for k in range(1, n_ch):
        pl.semaphore_signal(barrier, inc=1, device_id={"ch": lax.rem(me_ch + k, n_ch)}, device_id_type=MESH)

    group = own // 2

    def prepare(h, part, plane, weights):
        ref = (vis_ref, model_ref)[part]
        four = [ref[j].astype(f32) for j in range(plane, plane + 4)]
        if part == 1:
            four = [v * weights for v in four]
        base = (4 * part + plane // 2) * own
        for z in range(n_bl):
            rows = slice(z * own + h * group, z * own + (h + 1) * group)
            block = jnp.concatenate([v[rows] for v in four], axis=0)
            outgoing[h, z, base : base + 2 * own, :] = block.astype(jnp.bfloat16)

    def data_copy(part, k):
        partner = exchange_partner(me_bl, k, n_bl)
        return pltpu.make_async_remote_copy(
            src_ref=outgoing.at[part, partner], dst_ref=incoming.at[part, k], send_sem=data_send.at[part, k],
            recv_sem=data_recv.at[part, k], device_id={"bl": partner}, device_id_type=MESH,
        )

    odd = lax.rem(me_ch, 2)

    def send(h):
        for i in range(1, n_bl):
            data_copy(h, i + odd * (n_bl - 2 * i)).start()

    loads[0].wait()
    loads[1].wait()
    prepare(0, 0, 0, None)
    loads[2].wait()
    prepare(0, 0, 4, None)
    loads[3].wait()
    live = lax.broadcasted_iota(jnp.int32, (channels, slots), 1) < counts_ref[0]
    weights = jnp.where(live, mask_ref[...], 0).astype(f32)
    loads[4].wait()
    prepare(0, 1, 0, weights)
    loads[5].wait()
    prepare(0, 1, 4, weights)
    pl.semaphore_wait(barrier, n_bl + n_ch - 2)
    pair_copies = {}
    for k in range(1, n_bl):
        pair_copies[k] = pltpu.make_async_remote_copy(
            src_ref=pairs_all.at[0], dst_ref=pairs_all.at[k], send_sem=pair_send.at[k], recv_sem=pair_recv.at[k],
            device_id={"bl": exchange_partner(me_bl, k, n_bl)}, device_id_type=MESH,
        )
        pair_copies[k].start()
    send(0)
    for part in range(2):
        for plane in range(0, 8, 4):
            prepare(1, part, plane, weights)
    send(1)

    def end_row(k):
        return jnp.concatenate([pairs_all[k, 0:1, :], pairs_all[k, 1:2, :]], axis=1)

    def is_upper(k, e):
        return pairs_all[k, e : e + 1, :] >= half

    def build_onehot(k):
        ends = end_row(k)
        within = jnp.where(ends >= half, ends - half, ends)
        step = 32

        def rows(i, carry):
            base = pl.multiple_of(i * step, step)
            station = lax.broadcasted_iota(jnp.int32, (step, 2 * slots), 0) + base
            onehot[k, pl.ds(base, step), :] = jnp.where(station == within, 1.0, 0.0).astype(jnp.bfloat16)
            return carry

        lax.fori_loop(0, half // step, rows, 0)
        onehot_t[k] = onehot[k].T

    def scatter(k, e, blocks):
        split = split_hi_lo(jnp.concatenate(blocks, axis=0))
        upper = split * jnp.where(is_upper(k, e), 1.0, 0.0).astype(jnp.bfloat16)
        both = jnp.concatenate([split - upper, upper], axis=0)
        summed = jnp.dot(both, onehot_t[k, e * slots : (e + 1) * slots, :], preferred_element_type=f32)
        n = len(blocks) * own
        return jnp.concatenate([summed[:n] + summed[n : 2 * n], summed[2 * n : 3 * n] + summed[3 * n :]], axis=1)

    def gather(k, e, split_gains):
        both = jnp.dot(split_gains, onehot[k, :, e * slots : (e + 1) * slots], preferred_element_type=f32)
        n = split_gains.shape[0] // 4
        both = jnp.where(is_upper(k, e), both[2 * n : 3 * n] + both[3 * n :], both[:n] + both[n : 2 * n])
        return both.reshape(n // own, own, slots)

    def split_halves(blocks):
        split = split_hi_lo(jnp.concatenate(blocks, axis=0))
        return jnp.concatenate([split[:, :half], split[:, half:]], axis=0)

    def make_products(h, k, block):
        block = block.astype(f32).reshape(8, own, slots)
        a_re, a_im, b = [], [], []
        for p in range(2):
            vr, vi, mr, mi = block[p], block[2 + p], block[4 + p], block[6 + p]
            a_re.append(mr * vr + mi * vi)
            a_im.append(mr * vi - mi * vr)
            b.append(mr * mr + mi * mi)
            products[h, k, p] = a_re[p]
            products[h, k, 2 + p] = a_im[p]
            products[h, k, 4 + p] = b[p]
        first = scatter(k, 0, a_re + a_im + b)
        second = scatter(k, 1, [a_re[0] + a_re[1], -(a_im[0] + a_im[1]), b[0] + b[1]])
        return first, second

    def add(left, right):
        return right if left is None else (left[0] + right[0], left[1] + right[1])

    def station_sums(total):
        first = total[0].reshape(6, own, stations)
        second = total[1].reshape(3, own, stations)
        sums = []
        for i in range(3):
            feeds = [first[2 * i + p][:group] + first[2 * i + p][group:] for p in range(2)]
            sums.append(jnp.concatenate(feeds, axis=0) + second[i])
        return sums

    def solve(h, total):
        num_re, num_im, den = station_sums(total)
        gain_re = (num_re + damping) / (den + damping)
        gain_im = num_im / (den + damping)
        for_second = split_halves([gain_re, gain_im])
        twice = [jnp.concatenate([g[f * group : (f + 1) * group]] * 2, axis=0) for g in (gain_re, gain_im) for f in range(2)]
        for_first = split_halves(twice)
        total = None
        gathered = [(gather(k, 0, for_first), gather(k, 1, for_second)) for k in range(n_bl)]
        for k in range(n_bl):
            ga, (ge_re, ge_im) = gathered[k]
            ge_sq = ge_re * ge_re + ge_im * ge_im
            first, second = [[], [], []], [[], [], []]
            for p in range(2):
                a_re, a_im, b = products[h, k, p], products[h, k, 2 + p], products[h, k, 4 + p]
                ga_re, ga_im = ga[p], ga[2 + p]
                first[0].append(a_re * ge_re - a_im * ge_im)
                first[1].append(a_re * ge_im + a_im * ge_re)
                first[2].append(b * ge_sq)
                second[0].append(a_re * ga_re + a_im * ga_im)
                second[1].append(a_re * ga_im - a_im * ga_re)
                second[2].append(b * (ga_re * ga_re + ga_im * ga_im))
            part = scatter(k, 0, sum(first, [])), scatter(k, 1, [v[0] + v[1] for v in second])
            total = add(total, part)
        num_re, num_im, den = station_sums(total)
        for i, (num, previous) in enumerate(((num_re, gain_re), (num_im, gain_im))):
            solved = 0.5 * ((num + damping * previous) / (den + damping) + previous)
            for f in range(2):
                state[2 * i + f, h * group : (h + 1) * group, :] = solved[f * group : (f + 1) * group]

    build_onehot(0)
    totals = [make_products(h, 0, outgoing[h, me_bl]) for h in range(2)]
    for k in range(1, n_bl):
        pair_copies[k].wait()
        build_onehot(k)
    for h in range(2):
        total = totals[h]
        for k in range(1, n_bl):
            data_copy(h, k).wait_recv()
            total = add(total, make_products(h, k, incoming[h, k]))
        solve(h, total)

    my_rows = pl.ds(pl.multiple_of(me_bl * own, SUBLANES), own)
    sol_copies = []
    for k in range(n_bl - 1, 0, -1):
        partner = exchange_partner(me_bl, k, n_bl)
        sol_copies.append(
            pltpu.make_async_remote_copy(
                src_ref=state.at[:, :, pl.ds(pl.multiple_of(partner * owned, LANES), owned)],
                dst_ref=sol.at[:, my_rows, :], send_sem=sol_send.at[k], recv_sem=sol_recv.at[k],
                device_id={"bl": partner}, device_id_type=MESH,
            )
        )
        sol_copies[-1].start()
    sol[:, my_rows, :] = state[:, :, pl.ds(pl.multiple_of(me_bl * owned, LANES), owned)]

    channel_total = channels * n_ch
    scale, mean_square, ratio = basis_coefficients(channel_total)
    index = lax.broadcasted_iota(jnp.int32, (channels, owned), 0) + me_ch * channels
    x = (2.0 * index.astype(f32) - (channel_total - 1.0)) * (1.0 / (channel_total - 1.0))
    basis = [
        jnp.full((channels, owned), scale[0], f32),
        scale[1] * x,
        scale[2] * (x * x - mean_square),
        scale[3] * (x * (x * x - ratio)),
    ]
    for copy in sol_copies:
        copy.wait_recv()
    for i in range(4):
        solved = sol[i]
        for d in range(4):
            moments[4 * i + d : 4 * i + d + 1, :] = jnp.sum(basis[d] * solved, axis=0, keepdims=True)
    mom_copies = []
    for k in range(1, n_ch):
        mom_copies.append(
            pltpu.make_async_remote_copy(
                src_ref=moments, dst_ref=moments_in.at[k], send_sem=mom_send.at[k], recv_sem=mom_recv.at[k],
                device_id={"ch": lax.rem(me_ch + k, n_ch)}, device_id_type=MESH,
            )
        )
        mom_copies[-1].start()
    whole = moments[...]
    for k, copy in enumerate(mom_copies, 1):
        copy.wait_recv()
        whole = whole + moments_in[k]
    for i in range(4):
        row = basis[0] * whole[4 * i : 4 * i + 1, :]
        for d in range(1, 4):
            row = row + basis[d] * whole[4 * i + d : 4 * i + d + 1, :]
        fit[i] = row
    sent = [data_copy(h, k) for h in range(2) for k in range(1, n_bl)]
    for copy in sent + sol_copies + mom_copies:
        copy.wait_send()


def write_out(solved_ref, fitted_ref, solved_out, fitted_out, sems):
    copies = [
        pltpu.make_async_copy(solved_ref, solved_out, sems.at[0]),
        pltpu.make_async_copy(fitted_ref, fitted_out, sems.at[1]),
    ]
    for copy in copies:
        copy.start()
    for copy in copies:
        copy.wait()


def fused(n_bl, n_ch, visibilities, sky_model, antenna_pairs, tile_counts, usable_mask):
    channels, slots = usable_mask.shape
    own = channels // n_bl
    owned = STATION_COUNT // n_bl
    out = jax.ShapeDtypeStruct((4, channels, owned), jnp.float32)
    vmem = pl.BlockSpec(memory_space=pltpu.VMEM)
    hbm = pl.BlockSpec(memory_space=pltpu.HBM)
    dma = pltpu.SemaphoreType.DMA
    solved, fitted = pl.pallas_call(
        functools.partial(calibrate, n_bl, n_ch),
        out_shape=(out, out),
        in_specs=[hbm, hbm, hbm, pl.BlockSpec(memory_space=pltpu.SMEM), hbm],
        out_specs=(vmem, vmem),
        scratch_shapes=[
            pltpu.VMEM(visibilities.shape, visibilities.dtype),
            pltpu.VMEM(sky_model.shape, sky_model.dtype),
            pltpu.VMEM(usable_mask.shape, usable_mask.dtype),
            pltpu.VMEM((2, n_bl, 8 * own, slots), jnp.bfloat16),
            pltpu.VMEM((2, n_bl, 8 * own, slots), jnp.bfloat16),
            pltpu.VMEM((n_bl, 2, slots), jnp.int32),
            pltpu.VMEM((n_bl, STATION_COUNT // 2, 2 * slots), jnp.bfloat16),
            pltpu.VMEM((n_bl, 2 * slots, STATION_COUNT // 2), jnp.bfloat16),
            pltpu.VMEM((2, n_bl, 6, own, slots), jnp.float32),
            pltpu.VMEM((4, own, STATION_COUNT), jnp.float32),
            pltpu.VMEM((16, owned), jnp.float32),
            pltpu.VMEM((n_ch, 16, owned), jnp.float32),
            dma((6,)), dma((2, n_bl)), dma((2, n_bl)), dma((n_bl,)), dma((n_bl,)),
            dma((n_bl,)), dma((n_bl,)), dma((n_ch,)), dma((n_ch,)),
        ],
        compiler_params=pltpu.CompilerParams(
            collective_id=0, has_side_effects=True, vmem_limit_bytes=40 * 1024 * 1024
        ),
    )(
        pltpu.with_memory_space_constraint(visibilities, pltpu.HBM),
        pltpu.with_memory_space_constraint(sky_model, pltpu.HBM),
        pltpu.with_memory_space_constraint(antenna_pairs, pltpu.HBM),
        tile_counts,
        pltpu.with_memory_space_constraint(usable_mask, pltpu.HBM),
    )
    solved, fitted = pl.pallas_call(
        write_out,
        out_shape=(out, out),
        in_specs=[vmem, vmem],
        out_specs=(hbm, hbm),
        scratch_shapes=[dma((2,))],
        compiler_params=pltpu.CompilerParams(vmem_limit_bytes=4 * 1024 * 1024),
    )(solved, fitted)
    shape = (2, 2, channels, owned)
    return solved.reshape(shape), fitted.reshape(shape)


def split_parts(data):
    planes = data.astype(jnp.float32)
    shape_rest = planes.shape[1:]
    return (planes[:4].reshape((2, 2) + shape_rest), planes[4:].reshape((2, 2) + shape_rest))


def poly_basis(channel_total):
    node_values = (2.0 * jnp.arange(channel_total, dtype=jnp.float32) - (channel_total - 1)) / (
        channel_total - 1
    )
    basis_rows = []
    for degree in range(4):
        vector = node_values**degree
        for earlier in basis_rows:
            vector = vector - jnp.sum(vector * earlier) * earlier
        vector = vector / jnp.sqrt(jnp.sum(vector * vector))
        basis_rows.append(vector)
    return jnp.stack(basis_rows)


def contributions(
    model_real_part, model_imaginary, vis_real, vis_imag, first_gain, second_gain, weights
):
    second_real = second_gain[0][None]
    second_imag = second_gain[1][None]
    left_real = model_real_part * second_real + model_imaginary * second_imag
    left_imag = model_imaginary * second_real - model_real_part * second_imag
    first_num_real = jnp.sum(left_real * vis_real + left_imag * vis_imag, axis=1) * weights
    first_num_imag = jnp.sum(left_real * vis_imag - left_imag * vis_real, axis=1) * weights
    first_den = jnp.sum(left_real * left_real + left_imag * left_imag, axis=1) * weights
    first_real = first_gain[0][:, None]
    first_imag = first_gain[1][:, None]
    right_real = model_real_part * first_real - model_imaginary * first_imag
    right_imag = model_real_part * first_imag + model_imaginary * first_real
    second_num_real = jnp.sum(right_real * vis_real + right_imag * vis_imag, axis=0) * weights
    second_num_imag = jnp.sum(right_imag * vis_real - right_real * vis_imag, axis=0) * weights
    second_den = jnp.sum(right_real * right_real + right_imag * right_imag, axis=0) * weights
    return (
        jnp.stack([first_num_real, first_num_imag, first_den]),
        jnp.stack([second_num_real, second_num_imag, second_den]),
    )


def refresh(station_sums, previous):
    divisor = station_sums[2] + damping
    return jnp.stack(
        [
            (station_sums[0] + damping * previous[0]) / divisor,
            (station_sums[1] + damping * previous[1]) / divisor,
        ]
    )


def station_totals(end_first, end_second, first_endpoints, second_ends):
    total_slots = end_first.shape[3]
    flat_first = end_first.reshape(-1, total_slots)
    flat_second = end_second.reshape(-1, total_slots)
    block_rows = math.gcd(total_slots, 1024)
    block_count = total_slots // block_rows
    station_index = jnp.arange(STATION_COUNT, dtype=jnp.int32)

    def add_block(block, total):
        table_first = (first_endpoints[:, None] == station_index[None, :]).astype(jnp.float32)
        table_second = (second_ends[:, None] == station_index[None, :]).astype(jnp.float32)
        return (
            total
            + jnp.dot(
                flat_first, table_first, precision=highest, preferred_element_type=jnp.float32
            )
            + jnp.dot(
                flat_second, table_second, precision=highest, preferred_element_type=jnp.float32
            )
        )

    empty = jnp.zeros((flat_first.shape[0], STATION_COUNT), jnp.float32)
    summed = lax.fori_loop(0, block_count, add_block, empty)
    return summed.reshape(end_first.shape[:3] + (STATION_COUNT,))


def spread(owned_gains):
    return lax.all_gather(owned_gains, "bl", axis=3, tiled=True)


def local(visibilities, sky_model, antenna_pairs, tile_counts, usable_mask):
    vis_real, vis_imag = split_parts(visibilities)
    model_real_part, model_imaginary = split_parts(sky_model)
    channel_local = visibilities.shape[1]
    tile_rows = visibilities.shape[2]
    owner_count = lax.axis_size("bl")
    owned_count = STATION_COUNT // owner_count
    owner_start = lax.axis_index("bl") * owned_count
    live_slots = jnp.arange(tile_rows, dtype=jnp.int32) < tile_counts[0]
    weights = usable_mask.astype(jnp.float32) * live_slots.astype(jnp.float32)[None, :]
    channel_total = channel_local * lax.axis_size("ch")
    poly_rows = lax.dynamic_slice_in_dim(
        poly_basis(channel_total), lax.axis_index("ch") * channel_local, channel_local, 1
    )
    gain_state = jnp.stack(
        [
            jnp.ones((2, channel_local, STATION_COUNT), jnp.float32),
            jnp.zeros((2, channel_local, STATION_COUNT), jnp.float32),
        ]
    )
    solved = gain_state
    for iteration in range(SWEEPS):
        first_gain = jnp.take(gain_state, antenna_pairs[0], axis=3)
        second_gain = jnp.take(gain_state, antenna_pairs[1], axis=3)
        end_first, end_second = contributions(
            model_real_part, model_imaginary, vis_real, vis_imag, first_gain, second_gain, weights
        )
        partial_sums = station_totals(end_first, end_second, antenna_pairs[0], antenna_pairs[1])
        station_sums = lax.psum_scatter(partial_sums, "bl", scatter_dimension=3, tiled=True)
        previous = lax.dynamic_slice_in_dim(gain_state, owner_start, owned_count, 3)
        renewed = refresh(station_sums, previous)
        if iteration == 1:
            renewed = 0.5 * (renewed + previous)
        solved = renewed
        if iteration < SWEEPS - 1:
            gain_state = spread(renewed)
    local_moments = jnp.einsum("kc,rfca->krfa", poly_rows, solved, precision=highest)
    moments = lax.psum(local_moments, "ch")
    fitted = jnp.einsum("kc,krfa->rfca", poly_rows, moments, precision=highest)
    return (solved, fitted)


def solution(mesh):
    n_bl, n_ch = mesh.shape["bl"], mesh.shape["ch"]

    def run(visibilities, sky_model, antenna_pairs, tile_counts, usable_mask):
        channels, slots = usable_mask.shape
        whole_tiles = (
            channels % (n_bl * SUBLANES) == 0
            and slots % LANES == 0
            and STATION_COUNT % (n_bl * LANES) == 0
            and n_bl & (n_bl - 1) == 0
        )
        plan = functools.partial(fused, n_bl, n_ch) if whole_tiles else local
        return plan(visibilities, sky_model, antenna_pairs, tile_counts, usable_mask)

    return jax.shard_map(
        run,
        mesh=mesh,
        in_specs=(
            P(None, "ch", ("grp", "bl")),
            P(None, "ch", ("grp", "bl")),
            P(None, ("grp", "bl")),
            P(("grp", "bl")),
            P("ch", ("grp", "bl")),
        ),
        out_specs=(P(None, None, "ch", ("grp", "bl")), P(None, None, "ch", ("grp", "bl"))),
        check_vma=False,
    )
```

```python
import functools
import math

import jax
import jax.numpy as jnp
import numpy as np
from jax import lax
from jax.experimental import pallas as pl
from jax.experimental.pallas import tpu as pltpu
from jax.sharding import PartitionSpec as P

STATION_COUNT = 512
SWEEPS = 2


damping = 4.0
highest = lax.Precision.HIGHEST
MESH = pl.DeviceIdType.MESH
LANES = 128
SUBLANES = 8


def basis_coefficients(channel_total):
    x = (2.0 * np.arange(channel_total, dtype=np.float64) - (channel_total - 1)) / (channel_total - 1)
    m = np.mean(x**2)
    r = np.sum(x**4) / np.sum(x**2)
    a = [1.0 / np.sqrt(np.sum(v * v)) for v in (np.ones_like(x), x, x**2 - m, x**3 - r * x)]
    return [float(v) for v in a], float(m), float(r)


def split_hi_lo(values):
    hi = values.astype(jnp.bfloat16).astype(jnp.float32)
    return jnp.concatenate([hi, values - hi], axis=0).astype(jnp.bfloat16)


def exchange_partner(me, k, n):
    partner, bit = 0, 1
    while bit < n:
        mine, other = (me // bit) % 2, (k // bit) % 2
        partner = partner + (mine + other - 2 * mine * other) * bit
        bit *= 2
    return partner


def calibrate(
    n_bl, n_ch, vis_hbm, model_hbm, pairs_hbm, counts_ref, mask_hbm, sol, fit,
    vis_ref, model_ref, mask_ref, outgoing, incoming, pairs_all, onehot, products, state, moments, moments_in,
    load_sem, data_send, data_recv, pair_send, pair_recv, sol_send, sol_recv, mom_send, mom_recv,
):
    me_bl = lax.axis_index("bl")
    me_ch = lax.axis_index("ch")
    channels, slots = mask_ref.shape
    own = channels // n_bl
    stations = state.shape[2]
    owned = stations // n_bl
    half = stations // 2
    f32 = jnp.float32

    loads = [
        pltpu.make_async_copy(pairs_hbm, pairs_all.at[0], load_sem.at[0]),
        pltpu.make_async_copy(vis_hbm.at[0:4], vis_ref.at[0:4], load_sem.at[1]),
        pltpu.make_async_copy(vis_hbm.at[4:8], vis_ref.at[4:8], load_sem.at[2]),
        pltpu.make_async_copy(mask_hbm, mask_ref, load_sem.at[3]),
        pltpu.make_async_copy(model_hbm.at[0:4], model_ref.at[0:4], load_sem.at[4]),
        pltpu.make_async_copy(model_hbm.at[4:8], model_ref.at[4:8], load_sem.at[5]),
    ]
    for load in loads:
        load.start()
    barrier = pltpu.get_barrier_semaphore()
    for k in range(1, n_bl):
        pl.semaphore_signal(barrier, inc=1, device_id={"bl": exchange_partner(me_bl, k, n_bl)}, device_id_type=MESH)
    for k in range(1, n_ch):
        pl.semaphore_signal(barrier, inc=1, device_id={"ch": lax.rem(me_ch + k, n_ch)}, device_id_type=MESH)

    group = own // 2

    def prepare(h, part, plane, weights):
        ref = (vis_ref, model_ref)[part]
        four = [ref[j].astype(f32) for j in range(plane, plane + 4)]
        if part == 1:
            four = [v * weights for v in four]
        base = (4 * part + plane // 2) * own
        for z in range(n_bl):
            rows = slice(z * own + h * group, z * own + (h + 1) * group)
            block = jnp.concatenate([v[rows] for v in four], axis=0)
            outgoing[h, z, base : base + 2 * own, :] = block.astype(jnp.bfloat16)

    def data_copy(part, k):
        partner = exchange_partner(me_bl, k, n_bl)
        return pltpu.make_async_remote_copy(
            src_ref=outgoing.at[part, partner], dst_ref=incoming.at[part, k], send_sem=data_send.at[part, k],
            recv_sem=data_recv.at[part, k], device_id={"bl": partner}, device_id_type=MESH,
        )

    odd = lax.rem(me_ch, 2)

    def send(h):
        for i in range(1, n_bl):
            data_copy(h, i + odd * (n_bl - 2 * i)).start()

    loads[0].wait()
    loads[1].wait()
    prepare(0, 0, 0, None)
    loads[2].wait()
    prepare(0, 0, 4, None)
    loads[3].wait()
    live = lax.broadcasted_iota(jnp.int32, (channels, slots), 1) < counts_ref[0]
    weights = jnp.where(live, mask_ref[...], 0).astype(f32)
    loads[4].wait()
    prepare(0, 1, 0, weights)
    loads[5].wait()
    prepare(0, 1, 4, weights)
    pl.semaphore_wait(barrier, n_bl + n_ch - 2)
    pair_copies = {}
    for k in range(1, n_bl):
        pair_copies[k] = pltpu.make_async_remote_copy(
            src_ref=pairs_all.at[0], dst_ref=pairs_all.at[k], send_sem=pair_send.at[k], recv_sem=pair_recv.at[k],
            device_id={"bl": exchange_partner(me_bl, k, n_bl)}, device_id_type=MESH,
        )
        pair_copies[k].start()
    send(0)
    for part in range(2):
        for plane in range(0, 8, 4):
            prepare(1, part, plane, weights)
    send(1)

    def end_row(k):
        return jnp.concatenate([pairs_all[k, 0:1, :], pairs_all[k, 1:2, :]], axis=1)

    def is_upper(k, e):
        return pairs_all[k, e : e + 1, :] >= half

    def build_onehot(k):
        ends = end_row(k)
        within = jnp.where(ends >= half, ends - half, ends)
        step = 32

        def rows(i, carry):
            base = pl.multiple_of(i * step, step)
            station = lax.broadcasted_iota(jnp.int32, (step, 2 * slots), 0) + base
            onehot[k, pl.ds(base, step), :] = jnp.where(station == within, 1.0, 0.0).astype(jnp.bfloat16)
            return carry

        lax.fori_loop(0, half // step, rows, 0)

    def scatter(k, e, blocks):
        split = split_hi_lo(jnp.concatenate(blocks, axis=0))
        upper = split * jnp.where(is_upper(k, e), 1.0, 0.0).astype(jnp.bfloat16)
        both = jnp.concatenate([split - upper, upper], axis=0)
        summed = lax.dot_general(
            both, onehot[k, :, e * slots : (e + 1) * slots], (((1,), (1,)), ((), ())), preferred_element_type=f32
        )
        n = len(blocks) * own
        return jnp.concatenate([summed[:n] + summed[n : 2 * n], summed[2 * n : 3 * n] + summed[3 * n :]], axis=1)

    def gather(k, e, split_gains):
        both = jnp.dot(split_gains, onehot[k, :, e * slots : (e + 1) * slots], preferred_element_type=f32)
        n = split_gains.shape[0] // 4
        both = jnp.where(is_upper(k, e), both[2 * n : 3 * n] + both[3 * n :], both[:n] + both[n : 2 * n])
        return both.reshape(n // own, own, slots)

    def split_halves(blocks):
        split = split_hi_lo(jnp.concatenate(blocks, axis=0))
        return jnp.concatenate([split[:, :half], split[:, half:]], axis=0)

    def make_products(h, k, block):
        block = block.astype(f32).reshape(8, own, slots)
        a_re, a_im, b = [], [], []
        for p in range(2):
            vr, vi, mr, mi = block[p], block[2 + p], block[4 + p], block[6 + p]
            a_re.append(mr * vr + mi * vi)
            a_im.append(mr * vi - mi * vr)
            b.append(mr * mr + mi * mi)
            products[h, k, p] = a_re[p]
            products[h, k, 2 + p] = a_im[p]
            products[h, k, 4 + p] = b[p]
        first = scatter(k, 0, a_re + a_im + b)
        second = scatter(k, 1, [a_re[0] + a_re[1], -(a_im[0] + a_im[1]), b[0] + b[1]])
        return first, second

    def add(left, right):
        return right if left is None else (left[0] + right[0], left[1] + right[1])

    def station_sums(total):
        first = total[0].reshape(6, own, stations)
        second = total[1].reshape(3, own, stations)
        sums = []
        for i in range(3):
            feeds = [first[2 * i + p][:group] + first[2 * i + p][group:] for p in range(2)]
            sums.append(jnp.concatenate(feeds, axis=0) + second[i])
        return sums

    def solve(h, total):
        num_re, num_im, den = station_sums(total)
        gain_re = (num_re + damping) / (den + damping)
        gain_im = num_im / (den + damping)
        for_second = split_halves([gain_re, gain_im])
        twice = [jnp.concatenate([g[f * group : (f + 1) * group]] * 2, axis=0) for g in (gain_re, gain_im) for f in range(2)]
        for_first = split_halves(twice)
        total = None
        gathered = [(gather(k, 0, for_first), gather(k, 1, for_second)) for k in range(n_bl)]
        for k in range(n_bl):
            ga, (ge_re, ge_im) = gathered[k]
            ge_sq = ge_re * ge_re + ge_im * ge_im
            first, second = [[], [], []], [[], [], []]
            for p in range(2):
                a_re, a_im, b = products[h, k, p], products[h, k, 2 + p], products[h, k, 4 + p]
                ga_re, ga_im = ga[p], ga[2 + p]
                first[0].append(a_re * ge_re - a_im * ge_im)
                first[1].append(a_re * ge_im + a_im * ge_re)
                first[2].append(b * ge_sq)
                second[0].append(a_re * ga_re + a_im * ga_im)
                second[1].append(a_re * ga_im - a_im * ga_re)
                second[2].append(b * (ga_re * ga_re + ga_im * ga_im))
            part = scatter(k, 0, sum(first, [])), scatter(k, 1, [v[0] + v[1] for v in second])
            total = add(total, part)
        num_re, num_im, den = station_sums(total)
        for i, (num, previous) in enumerate(((num_re, gain_re), (num_im, gain_im))):
            solved = 0.5 * ((num + damping * previous) / (den + damping) + previous)
            for f in range(2):
                state[2 * i + f, h * group : (h + 1) * group, :] = solved[f * group : (f + 1) * group]

    build_onehot(0)
    totals = [make_products(h, 0, outgoing[h, me_bl]) for h in range(2)]
    for k in range(1, n_bl):
        pair_copies[k].wait()
        build_onehot(k)
    for h in range(2):
        total = totals[h]
        for k in range(1, n_bl):
            data_copy(h, k).wait_recv()
            total = add(total, make_products(h, k, incoming[h, k]))
        solve(h, total)

    my_rows = pl.ds(pl.multiple_of(me_bl * own, SUBLANES), own)
    sol_copies = []
    for k in range(n_bl - 1, 0, -1):
        partner = exchange_partner(me_bl, k, n_bl)
        sol_copies.append(
            pltpu.make_async_remote_copy(
                src_ref=state.at[:, :, pl.ds(pl.multiple_of(partner * owned, LANES), owned)],
                dst_ref=sol.at[:, my_rows, :], send_sem=sol_send.at[k], recv_sem=sol_recv.at[k],
                device_id={"bl": partner}, device_id_type=MESH,
            )
        )
        sol_copies[-1].start()
    sol[:, my_rows, :] = state[:, :, pl.ds(pl.multiple_of(me_bl * owned, LANES), owned)]

    channel_total = channels * n_ch
    scale, mean_square, ratio = basis_coefficients(channel_total)
    index = lax.broadcasted_iota(jnp.int32, (channels, owned), 0) + me_ch * channels
    x = (2.0 * index.astype(f32) - (channel_total - 1.0)) * (1.0 / (channel_total - 1.0))
    basis = [
        jnp.full((channels, owned), scale[0], f32),
        scale[1] * x,
        scale[2] * (x * x - mean_square),
        scale[3] * (x * (x * x - ratio)),
    ]
    for copy in sol_copies:
        copy.wait_recv()
    for i in range(4):
        solved = sol[i]
        for d in range(4):
            moments[4 * i + d : 4 * i + d + 1, :] = jnp.sum(basis[d] * solved, axis=0, keepdims=True)
    mom_copies = []
    for k in range(1, n_ch):
        mom_copies.append(
            pltpu.make_async_remote_copy(
                src_ref=moments, dst_ref=moments_in.at[k], send_sem=mom_send.at[k], recv_sem=mom_recv.at[k],
                device_id={"ch": lax.rem(me_ch + k, n_ch)}, device_id_type=MESH,
            )
        )
        mom_copies[-1].start()
    whole = moments[...]
    for k, copy in enumerate(mom_copies, 1):
        copy.wait_recv()
        whole = whole + moments_in[k]
    for i in range(4):
        row = basis[0] * whole[4 * i : 4 * i + 1, :]
        for d in range(1, 4):
            row = row + basis[d] * whole[4 * i + d : 4 * i + d + 1, :]
        fit[i] = row
    sent = [data_copy(h, k) for h in range(2) for k in range(1, n_bl)]
    for copy in sent + sol_copies + mom_copies:
        copy.wait_send()


def write_out(solved_ref, fitted_ref, solved_out, fitted_out, sems):
    copies = [
        pltpu.make_async_copy(solved_ref, solved_out, sems.at[0]),
        pltpu.make_async_copy(fitted_ref, fitted_out, sems.at[1]),
    ]
    for copy in copies:
        copy.start()
    for copy in copies:
        copy.wait()


def fused(n_bl, n_ch, visibilities, sky_model, antenna_pairs, tile_counts, usable_mask):
    channels, slots = usable_mask.shape
    own = channels // n_bl
    owned = STATION_COUNT // n_bl
    out = jax.ShapeDtypeStruct((4, channels, owned), jnp.float32)
    vmem = pl.BlockSpec(memory_space=pltpu.VMEM)
    hbm = pl.BlockSpec(memory_space=pltpu.HBM)
    dma = pltpu.SemaphoreType.DMA
    solved, fitted = pl.pallas_call(
        functools.partial(calibrate, n_bl, n_ch),
        out_shape=(out, out),
        in_specs=[hbm, hbm, hbm, pl.BlockSpec(memory_space=pltpu.SMEM), hbm],
        out_specs=(vmem, vmem),
        scratch_shapes=[
            pltpu.VMEM(visibilities.shape, visibilities.dtype),
            pltpu.VMEM(sky_model.shape, sky_model.dtype),
            pltpu.VMEM(usable_mask.shape, usable_mask.dtype),
            pltpu.VMEM((2, n_bl, 8 * own, slots), jnp.bfloat16),
            pltpu.VMEM((2, n_bl, 8 * own, slots), jnp.bfloat16),
            pltpu.VMEM((n_bl, 2, slots), jnp.int32),
            pltpu.VMEM((n_bl, STATION_COUNT // 2, 2 * slots), jnp.bfloat16),
            pltpu.VMEM((2, n_bl, 6, own, slots), jnp.float32),
            pltpu.VMEM((4, own, STATION_COUNT), jnp.float32),
            pltpu.VMEM((16, owned), jnp.float32),
            pltpu.VMEM((n_ch, 16, owned), jnp.float32),
            dma((6,)), dma((2, n_bl)), dma((2, n_bl)), dma((n_bl,)), dma((n_bl,)),
            dma((n_bl,)), dma((n_bl,)), dma((n_ch,)), dma((n_ch,)),
        ],
        compiler_params=pltpu.CompilerParams(
            collective_id=0, has_side_effects=True, vmem_limit_bytes=40 * 1024 * 1024
        ),
    )(
        pltpu.with_memory_space_constraint(visibilities, pltpu.HBM),
        pltpu.with_memory_space_constraint(sky_model, pltpu.HBM),
        pltpu.with_memory_space_constraint(antenna_pairs, pltpu.HBM),
        tile_counts,
        pltpu.with_memory_space_constraint(usable_mask, pltpu.HBM),
    )
    solved, fitted = pl.pallas_call(
        write_out,
        out_shape=(out, out),
        in_specs=[vmem, vmem],
        out_specs=(hbm, hbm),
        scratch_shapes=[dma((2,))],
        compiler_params=pltpu.CompilerParams(vmem_limit_bytes=4 * 1024 * 1024),
    )(solved, fitted)
    shape = (2, 2, channels, owned)
    return solved.reshape(shape), fitted.reshape(shape)


def split_parts(data):
    planes = data.astype(jnp.float32)
    shape_rest = planes.shape[1:]
    return (planes[:4].reshape((2, 2) + shape_rest), planes[4:].reshape((2, 2) + shape_rest))


def poly_basis(channel_total):
    node_values = (2.0 * jnp.arange(channel_total, dtype=jnp.float32) - (channel_total - 1)) / (
        channel_total - 1
    )
    basis_rows = []
    for degree in range(4):
        vector = node_values**degree
        for earlier in basis_rows:
            vector = vector - jnp.sum(vector * earlier) * earlier
        vector = vector / jnp.sqrt(jnp.sum(vector * vector))
        basis_rows.append(vector)
    return jnp.stack(basis_rows)


def contributions(
    model_real_part, model_imaginary, vis_real, vis_imag, first_gain, second_gain, weights
):
    second_real = second_gain[0][None]
    second_imag = second_gain[1][None]
    left_real = model_real_part * second_real + model_imaginary * second_imag
    left_imag = model_imaginary * second_real - model_real_part * second_imag
    first_num_real = jnp.sum(left_real * vis_real + left_imag * vis_imag, axis=1) * weights
    first_num_imag = jnp.sum(left_real * vis_imag - left_imag * vis_real, axis=1) * weights
    first_den = jnp.sum(left_real * left_real + left_imag * left_imag, axis=1) * weights
    first_real = first_gain[0][:, None]
    first_imag = first_gain[1][:, None]
    right_real = model_real_part * first_real - model_imaginary * first_imag
    right_imag = model_real_part * first_imag + model_imaginary * first_real
    second_num_real = jnp.sum(right_real * vis_real + right_imag * vis_imag, axis=0) * weights
    second_num_imag = jnp.sum(right_imag * vis_real - right_real * vis_imag, axis=0) * weights
    second_den = jnp.sum(right_real * right_real + right_imag * right_imag, axis=0) * weights
    return (
        jnp.stack([first_num_real, first_num_imag, first_den]),
        jnp.stack([second_num_real, second_num_imag, second_den]),
    )


def refresh(station_sums, previous):
    divisor = station_sums[2] + damping
    return jnp.stack(
        [
            (station_sums[0] + damping * previous[0]) / divisor,
            (station_sums[1] + damping * previous[1]) / divisor,
        ]
    )


def station_totals(end_first, end_second, first_endpoints, second_ends):
    total_slots = end_first.shape[3]
    flat_first = end_first.reshape(-1, total_slots)
    flat_second = end_second.reshape(-1, total_slots)
    block_rows = math.gcd(total_slots, 1024)
    block_count = total_slots // block_rows
    station_index = jnp.arange(STATION_COUNT, dtype=jnp.int32)

    def add_block(block, total):
        table_first = (first_endpoints[:, None] == station_index[None, :]).astype(jnp.float32)
        table_second = (second_ends[:, None] == station_index[None, :]).astype(jnp.float32)
        return (
            total
            + jnp.dot(
                flat_first, table_first, precision=highest, preferred_element_type=jnp.float32
            )
            + jnp.dot(
                flat_second, table_second, precision=highest, preferred_element_type=jnp.float32
            )
        )

    empty = jnp.zeros((flat_first.shape[0], STATION_COUNT), jnp.float32)
    summed = lax.fori_loop(0, block_count, add_block, empty)
    return summed.reshape(end_first.shape[:3] + (STATION_COUNT,))


def spread(owned_gains):
    return lax.all_gather(owned_gains, "bl", axis=3, tiled=True)


def local(visibilities, sky_model, antenna_pairs, tile_counts, usable_mask):
    vis_real, vis_imag = split_parts(visibilities)
    model_real_part, model_imaginary = split_parts(sky_model)
    channel_local = visibilities.shape[1]
    tile_rows = visibilities.shape[2]
    owner_count = lax.axis_size("bl")
    owned_count = STATION_COUNT // owner_count
    owner_start = lax.axis_index("bl") * owned_count
    live_slots = jnp.arange(tile_rows, dtype=jnp.int32) < tile_counts[0]
    weights = usable_mask.astype(jnp.float32) * live_slots.astype(jnp.float32)[None, :]
    channel_total = channel_local * lax.axis_size("ch")
    poly_rows = lax.dynamic_slice_in_dim(
        poly_basis(channel_total), lax.axis_index("ch") * channel_local, channel_local, 1
    )
    gain_state = jnp.stack(
        [
            jnp.ones((2, channel_local, STATION_COUNT), jnp.float32),
            jnp.zeros((2, channel_local, STATION_COUNT), jnp.float32),
        ]
    )
    solved = gain_state
    for iteration in range(SWEEPS):
        first_gain = jnp.take(gain_state, antenna_pairs[0], axis=3)
        second_gain = jnp.take(gain_state, antenna_pairs[1], axis=3)
        end_first, end_second = contributions(
            model_real_part, model_imaginary, vis_real, vis_imag, first_gain, second_gain, weights
        )
        partial_sums = station_totals(end_first, end_second, antenna_pairs[0], antenna_pairs[1])
        station_sums = lax.psum_scatter(partial_sums, "bl", scatter_dimension=3, tiled=True)
        previous = lax.dynamic_slice_in_dim(gain_state, owner_start, owned_count, 3)
        renewed = refresh(station_sums, previous)
        if iteration == 1:
            renewed = 0.5 * (renewed + previous)
        solved = renewed
        if iteration < SWEEPS - 1:
            gain_state = spread(renewed)
    local_moments = jnp.einsum("kc,rfca->krfa", poly_rows, solved, precision=highest)
    moments = lax.psum(local_moments, "ch")
    fitted = jnp.einsum("kc,krfa->rfca", poly_rows, moments, precision=highest)
    return (solved, fitted)


def solution(mesh):
    n_bl, n_ch = mesh.shape["bl"], mesh.shape["ch"]

    def run(visibilities, sky_model, antenna_pairs, tile_counts, usable_mask):
        channels, slots = usable_mask.shape
        whole_tiles = (
            channels % (n_bl * SUBLANES) == 0
            and slots % LANES == 0
            and STATION_COUNT % (n_bl * LANES) == 0
            and n_bl & (n_bl - 1) == 0
        )
        plan = functools.partial(fused, n_bl, n_ch) if whole_tiles else local
        return plan(visibilities, sky_model, antenna_pairs, tile_counts, usable_mask)

    return jax.shard_map(
        run,
        mesh=mesh,
        in_specs=(
            P(None, "ch", ("grp", "bl")),
            P(None, "ch", ("grp", "bl")),
            P(None, ("grp", "bl")),
            P(("grp", "bl")),
            P("ch", ("grp", "bl")),
        ),
        out_specs=(P(None, None, "ch", ("grp", "bl")), P(None, None, "ch", ("grp", "bl"))),
        check_vma=False,
    )
```
